128 devices in a mesh: span: 16 (over y, z_lo, core), chord: 8 (over z_hi, x).
Axes of the slice: x: 4, y: 4, z: 4 (z_hi: 2, z_lo: 2; z = z_hi * 2 + z_lo), core: 2. Of those that a mesh axis runs over, the one named last changes fastest.
Arguments:
- velocity: float32 [3, 64, 128, 512], P(None, 'span', 'chord'), may hold values from -6 to 6
- stress: float32 [6, 64, 128, 512], P(None, 'span', 'chord'), may hold values from -6 to 6
- grain_ids: int32 [64, 128, 512], P(None, 'chord', 'span'), may hold values from 0 to 4095
- lattice_tilt: float32 [3, 64, 128, 512], P(None, None, 'chord', 'span'), may hold values from -1 to 1
- grain_orient: int32 [4096], replicated, may hold values from 0 to 511
- orientations: float32 [3, 512], replicated, may hold values from -3.140625 to 3.140625
- source_cells: int32 [16, 3], replicated, may hold values from 0 to 511, as said below
- source_signal: float32 [16, 4], replicated, may hold values from -6 to 6
Outputs:
- velocity_out: float32 [3, 64, 128, 512], P(None, 'span', 'chord')
- stress_out: float32 [6, 64, 128, 512], P(None, 'span', 'chord')
The draws below stay inside these ranges and needn't reach their ends.
Inputs may be any that keep to these rules, and one draw needn't show every extreme that they name: `source_cells`: each row holds the span, chord and thickness index of a source voxel, below 64, 128 and 512 respectively; two rows may name the same voxel.
All inputs are finite; a program needn't handle non-finite values.
Results may differ from the reference program's by a relative error of at most 0.00002.
Values sent between devices are 32-bit elements; how exact they have to be, the bound alone decides.
No kernel may reach another device: no remote copies, remote signals or barrier semaphores. Data moves between devices by JAX's collectives and lax.ppermute only.
A program may use at most 128 MiB of HBM per device.

```python
import jax
import jax.numpy as jnp
from jax import lax

NZ = 512
STEPS = 4
GRAINS = 4096
ORIENTS = 512
SOURCES = 16
NX = 64
NY = 128


def draw_source_cells(key, part):
    key = jax.random.fold_in(key, 7)
    subkeys = jax.random.split(key, 3)
    span_cells = jax.random.randint(subkeys[0], (SOURCES,), 0, NX)
    chord_cells = jax.random.randint(subkeys[1], (SOURCES,), 0, NY)
    depth_cells = jax.random.randint(subkeys[2], (SOURCES,), 0, NZ)
    cells = jnp.stack((span_cells, chord_cells, depth_cells), axis=1).astype(jnp.int32)
    cells = cells.at[0].set(jnp.zeros((3,), jnp.int32))
    cells = cells.at[1].set(jnp.array([NX - 1, NY - 1, NZ - 1], jnp.int32))
    return cells


def place_ends(values, own_key, low, largest):
    longest = values.shape.index(max(values.shape))
    spots = []
    for shift in (0, 1):
        where = [jax.random.randint(jax.random.fold_in(own_key, axis), (), 0, length) for axis, length in enumerate(values.shape)]
        where[longest] = (where[longest] + shift) % values.shape[longest]
        spots.append(tuple(where))
    return values.at[spots[0]].set(low).at[spots[1]].set(largest)


def block_scale(rng, shape, pieces, low, high):
    level = 1.0
    for dim, parts in pieces:
        draws = jax.random.uniform(jax.random.fold_in(jax.random.fold_in(rng, 6), dim), (parts,), jnp.float32, low / len(pieces), high / len(pieces))
        level = level * jnp.repeat(jnp.exp(draws), shape[dim] // parts).reshape((-1,) + (1,) * (len(shape) - 1 - dim))
    return level


def normal_values(key, extent, deviation, limit, pieces=(), kind=jnp.bfloat16):
    values = jax.random.normal(key, extent, jnp.float32) * deviation
    if len(pieces) > 0:
        values = block_scale(key, extent, pieces, -0.22, 0.18) * values
    return jnp.clip(values, min=-limit, max=limit).astype(kind)


def setup_inputs(seed: int = 0) -> dict:
    keys = jax.random.split(jax.random.key(seed), 9)
    velocity = normal_values(keys[0], (3, NX, NY, NZ), 1.0, 6.0, ((1, 16), (2, 8)), jnp.float32)
    stress = normal_values(keys[1], (6, NX, NY, NZ), 1.0, 6.0, ((1, 16), (2, 8)), jnp.float32)
    grain_ids = place_ends(jax.random.randint(keys[2], (NX, NY, NZ), 0, GRAINS), jax.random.fold_in(keys[2], 1), 0, GRAINS - 1).astype(jnp.int32)
    lattice_tilt = normal_values(keys[3], (3, NX, NY, NZ), 0.25, 1.0, ((2, 8), (3, 16)), jnp.float32)
    grain_orient = place_ends(jax.random.randint(keys[4], (GRAINS,), 0, ORIENTS), jax.random.fold_in(keys[4], 1), 0, ORIENTS - 1).astype(jnp.int32)
    orientations = jnp.clip(jax.random.uniform(keys[5], (3, ORIENTS), jnp.float32, -3.140625, 3.140625), -3.140625, 3.140625)
    source_cells = draw_source_cells(jax.random.fold_in(keys[8], 71), 0)
    source_signal = normal_values(keys[7], (SOURCES, STEPS), 1.0, 6.0, (), jnp.float32)
    return dict(velocity=velocity, stress=stress, grain_ids=grain_ids, lattice_tilt=lattice_tilt, grain_orient=grain_orient, orientations=orientations, source_cells=source_cells, source_signal=source_signal)


normal_modulus = 0.9
cross_modulus = 1.6
shear_modulus = 1.3
time_step = 0.25


def euler_rows(first_angle, middle_angle, last_angle):
    cos_first = jnp.cos(first_angle)
    sin_first = jnp.sin(first_angle)
    cos_middle = jnp.cos(middle_angle)
    sin_middle = jnp.sin(middle_angle)
    cos_last = jnp.cos(last_angle)
    sin_last = jnp.sin(last_angle)
    return [cos_first * cos_last - sin_first * sin_last * cos_middle,
            sin_first * cos_last + cos_first * sin_last * cos_middle,
            sin_last * sin_middle,
            -cos_first * sin_last - sin_first * cos_last * cos_middle,
            -sin_first * sin_last + cos_first * cos_last * cos_middle,
            cos_last * sin_middle,
            sin_first * sin_middle,
            -cos_first * sin_middle,
            cos_middle]


def compose(left_rows, right_rows):
    return [left_rows[3 * row_at] * right_rows[col_at]
            + left_rows[3 * row_at + 1] * right_rows[3 + col_at]
            + left_rows[3 * row_at + 2] * right_rows[6 + col_at]
            for row_at in range(3) for col_at in range(3)]


def bond_stiffness(rotation):
    def element(row_at, col_at):
        return rotation[3 * row_at + col_at]

    bond_rows = []
    for row_at in range(3):
        bond_rows.append([element(row_at, 0) * element(row_at, 0),
                          element(row_at, 1) * element(row_at, 1),
                          element(row_at, 2) * element(row_at, 2),
                          2.0 * element(row_at, 1) * element(row_at, 2),
                          2.0 * element(row_at, 2) * element(row_at, 0),
                          2.0 * element(row_at, 0) * element(row_at, 1)])
    for first_at, second_at in ((1, 2), (2, 0), (0, 1)):
        bond_rows.append([element(first_at, 0) * element(second_at, 0),
                          element(first_at, 1) * element(second_at, 1),
                          element(first_at, 2) * element(second_at, 2),
                          element(first_at, 1) * element(second_at, 2) + element(first_at, 2) * element(second_at, 1),
                          element(first_at, 2) * element(second_at, 0) + element(first_at, 0) * element(second_at, 2),
                          element(first_at, 0) * element(second_at, 1) + element(first_at, 1) * element(second_at, 0)])
    weights = [normal_modulus] * 3 + [shear_modulus] * 3
    row_sums = [bond_rows[row_at][0] + bond_rows[row_at][1] + bond_rows[row_at][2] for row_at in range(6)]
    result = []
    for row_at in range(6):
        for col_at in range(row_at, 6):
            accumulated = cross_modulus * row_sums[row_at] * row_sums[col_at]
            for inner_at in range(6):
                accumulated = accumulated + weights[inner_at] * bond_rows[row_at][inner_at] * bond_rows[col_at][inner_at]
            result.append(accumulated)
    return result


def cell_rotation(grain_rot, grain_index, tilt):
    grain_part = jnp.take(grain_rot, grain_index, axis=1)
    return compose([grain_part[element_at] for element_at in range(9)], euler_rows(tilt[0], tilt[1], tilt[2]))


def upper_index(row_at, col_at):
    lower_at = min(row_at, col_at)
    upper_at = max(row_at, col_at)
    return lower_at * 6 - lower_at * (lower_at - 1) // 2 + upper_at - lower_at


def pair_sum(field, axis_at):
    length = field.shape[axis_at]
    return lax.slice_in_dim(field, 0, length - 1, axis=axis_at) + lax.slice_in_dim(field, 1, length, axis=axis_at)


def pair_diff(field, axis_at):
    length = field.shape[axis_at]
    return lax.slice_in_dim(field, 1, length, axis=axis_at) - lax.slice_in_dim(field, 0, length - 1, axis=axis_at)


def slopes(padded):
    depth_sum = pair_sum(padded, 3)
    slope_x = 0.25 * pair_diff(pair_sum(depth_sum, 2), 1)
    slope_y = 0.25 * pair_sum(pair_diff(depth_sum, 2), 1)
    slope_z = 0.25 * pair_sum(pair_sum(pair_diff(padded, 3), 2), 1)
    return slope_x, slope_y, slope_z


def move_velocity(velocity, padded_stress):
    slope_x, slope_y, slope_z = slopes(padded_stress)
    forces = jnp.stack((slope_x[0] + slope_y[5] + slope_z[4],
                        slope_x[5] + slope_y[1] + slope_z[3],
                        slope_x[4] + slope_y[3] + slope_z[2]))
    return velocity + time_step * forces


def move_stress(stress, padded_velocity, stiffness):
    slope_x, slope_y, slope_z = slopes(padded_velocity)
    strain = [slope_x[0], slope_y[1], slope_z[2],
              slope_y[2] + slope_z[1], slope_x[2] + slope_z[0], slope_x[1] + slope_y[0]]
    rates = []
    for row_at in range(6):
        accumulated = stiffness[upper_index(row_at, 0)] * strain[0]
        for col_at in range(1, 6):
            accumulated = accumulated + stiffness[upper_index(row_at, col_at)] * strain[col_at]
        rates.append(accumulated)
    return stress + time_step * jnp.stack(rates)


def reference(velocity, stress, grain_ids, lattice_tilt, grain_orient, orientations, source_cells, source_signal):
    rot_table = jnp.stack(euler_rows(orientations[0], orientations[1], orientations[2]))
    grain_rot = jnp.take(rot_table, grain_orient, axis=1)

    def slab_stiffness(slab):
        ids_slab, tilt_slab = slab
        return jnp.stack(bond_stiffness(cell_rotation(grain_rot, ids_slab, tilt_slab)))

    stiffness = lax.map(slab_stiffness, (grain_ids, jnp.moveaxis(lattice_tilt, 1, 0)))
    stiffness = jnp.moveaxis(stiffness, 1, 0)

    def advance(step_at, state):
        moving, stressed = state
        padded = jnp.pad(stressed, ((0, 0), (0, 1), (0, 1), (0, 1)))
        moving = move_velocity(moving, padded)
        moving = moving.at[2, source_cells[:, 0], source_cells[:, 1], source_cells[:, 2]].add(source_signal[:, step_at])
        padded = jnp.pad(moving, ((0, 0), (1, 0), (1, 0), (1, 0)))
        stressed = move_stress(stressed, padded, stiffness)
        return moving, stressed

    velocity_out, stress_out = lax.fori_loop(0, STEPS, advance, (velocity, stress))
    return velocity_out, stress_out
```

```python
import jax
import jax.numpy as jnp
from jax import lax
from jax.experimental import pallas as pl
from jax.experimental.pallas import tpu as pltpu
from jax.sharding import PartitionSpec as P

normal_modulus = 0.9
cross_modulus = 1.6
shear_modulus = 1.3
time_step = 0.25
anisotropy = normal_modulus - 2.0 * shear_modulus

DEEP = 4
ROWS = 24
TABLE_ROWS = 11
VMEM = pltpu.CompilerParams(vmem_limit_bytes=48 * 2**20)
WHOLE = pl.BlockSpec(memory_space=pltpu.VMEM)
SCALARS = pl.BlockSpec(memory_space=pltpu.SMEM)


def call(kernel, outs, operands, scalars=0, scratch=(), flops=0):
    return pl.pallas_call(
        kernel,
        out_shape=[jax.ShapeDtypeStruct(shape, jnp.float32) for shape in outs],
        in_specs=[SCALARS] * scalars + [WHOLE] * (len(operands) - scalars),
        out_specs=[WHOLE] * len(outs),
        scratch_shapes=[pltpu.VMEM(shape, jnp.float32) for shape in scratch],
        compiler_params=VMEM,
        cost_estimate=pl.CostEstimate(
            flops=flops,
            bytes_accessed=4 * sum(operand.size for operand in operands),
            transcendentals=0,
        ),
    )(*operands)


def small_sin(x):
    y = x * x
    return x * (
        1.0 + y * (-1.0 / 6 + y * (1.0 / 120 + y * (-1.0 / 5040 + y * (1.0 / 362880))))
    )


def small_cos(x):
    y = x * x
    return 1.0 + y * (
        -0.5
        + y * (1.0 / 24 + y * (-1.0 / 720 + y * (1.0 / 40320 + y * (-1.0 / 3628800))))
    )


def wide_sin_cos(x):
    quarter = 0.25 * x
    s, c = small_sin(quarter), small_cos(quarter)
    s, c = 2.0 * s * c, 1.0 - 2.0 * s * s
    return 2.0 * s * c, 1.0 - 2.0 * s * s


def quaternion(first, middle, last, sin_cos):
    s_mid, c_mid = sin_cos(0.5 * middle)
    s_sum, c_sum = sin_cos(0.5 * (first + last))
    s_dif, c_dif = sin_cos(0.5 * (first - last))
    return c_mid * c_sum, -s_mid * c_dif, -s_mid * s_dif, -c_mid * s_sum


def product(a, b):
    return (
        a[0] * b[0] - a[1] * b[1] - a[2] * b[2] - a[3] * b[3],
        a[0] * b[1] + a[1] * b[0] + a[2] * b[3] - a[3] * b[2],
        a[0] * b[2] - a[1] * b[3] + a[2] * b[0] + a[3] * b[1],
        a[0] * b[3] + a[1] * b[2] - a[2] * b[1] + a[3] * b[0],
    )


def reduced(q):
    w, x, y, z = q
    aw, ax, ay, az = jnp.abs(w), jnp.abs(x), jnp.abs(y), jnp.abs(z)
    low, high = jnp.maximum(aw, ax), jnp.maximum(ay, az)
    upper = high > low
    second = jnp.where(upper, az - ay, ax - aw) > 0.0

    def pick(a, b, c, d):
        return jnp.where(upper, jnp.where(second, d, c), jnp.where(second, b, a))

    lead = pick(w, x, y, z)
    flip = jnp.where(lead < 0.0, -1.0, 1.0)
    return (
        pick(x, -w, z, -y) * flip,
        pick(y, -z, -w, x) * flip,
        pick(z, y, -x, -w) * flip,
    )


def look_up(row, lane):
    return jnp.take_along_axis(
        jnp.broadcast_to(row, lane.shape), lane, axis=1, mode="promise_in_bounds"
    )


def rotation_kernel(ids_ref, tilt_ref, grain_ref, angle_ref, out_ref, turned_ref):
    packed = []
    for at in range(TABLE_ROWS):
        row = grain_ref[at : at + 1, :] + grain_ref[at + 11 : at + 12, :] * 512
        if at + 22 < 32:
            row = row + grain_ref[at + 22 : at + 23, :] * (512 * 512)
        packed.append(row)
    table = quaternion(angle_ref[0], angle_ref[1], angle_ref[2], wide_sin_cos)
    entries = [[part[at : at + 1, :] for at in range(4)] for part in table]
    for pair in range(2):
        parts = [[], [], []]
        for group in range(4):
            chord = 4 * group + 2 * pair
            both = lambda ref, *lead: jnp.concatenate(
                [ref[(*lead, chord)], ref[(*lead, chord + 1)]], axis=1
            )
            grain = both(ids_ref)
            third = jnp.where(grain >= 2816, 2, jnp.where(grain >= 1408, 1, 0))
            grain = grain - 1408 * third
            lane, place = grain & 127, grain >> 7
            entry = look_up(packed[0], lane)
            for at in range(1, TABLE_ROWS):
                entry = jnp.where(place == at, look_up(packed[at], lane), entry)
            entry = (entry >> (9 * third)) & 511
            lane, place = entry & 127, entry >> 7
            grain_turn = []
            for part in entries:
                low = jnp.where(place == 1, look_up(part[1], lane), look_up(part[0], lane))
                high = jnp.where(place == 3, look_up(part[3], lane), look_up(part[2], lane))
                grain_turn.append(jnp.where(place >= 2, high, low))
            tilt_turn = quaternion(
                both(tilt_ref, 0),
                both(tilt_ref, 1),
                both(tilt_ref, 2),
                lambda x: (small_sin(x), small_cos(x)),
            )
            for at, value in enumerate(reduced(product(grain_turn, tilt_turn))):
                parts[at].append(value)
        for at in range(3):
            turned = jnp.concatenate(parts[at], axis=0).T
            for half in range(2):
                turned_ref[at, 2 * pair + half, 0:64, :] = turned[64 * half : 64 * half + 64, :]
    for at in range(3):
        for rest in range(4):
            turned_ref[at, rest, 64:72, :] = jnp.zeros((8, 128), jnp.float32)
    for device in range(16):
        for at in range(3):
            for layer in range(5):
                row = 20 * at + 4 * layer
                out_ref[device, row : row + 4, :] = turned_ref[at, :, 4 * device + layer, :]
        out_ref[device, 60:64, :] = jnp.zeros((4, 128), jnp.float32)


def arrange_kernel(got_ref, out_ref, low_ref, high_ref):
    for four in range(4):
        pieces = [got_ref[4 * four + at] for at in range(4)]
        for group in range(4):
            lanes = jnp.concatenate(
                [piece[:, 32 * group : 32 * group + 32] for piece in pieces], axis=1
            )
            for at in range(15):
                out_ref[at, 4 * group : 4 * group + 4, 128 * four : 128 * four + 128] = lanes[
                    4 * at : 4 * at + 4, :
                ]
    low_ref[...] = out_ref[:, 0:DEEP, :]
    high_ref[...] = out_ref[:, 16 - DEEP : 16, :]


def after(x):
    lane = lax.broadcasted_iota(jnp.int32, x.shape, 1)
    return jnp.where(lane == x.shape[1] - 1, 0.0, pltpu.roll(x, x.shape[1] - 1, 1))


def before(x):
    lane = lax.broadcasted_iota(jnp.int32, x.shape, 1)
    return jnp.where(lane == 0, 0.0, pltpu.roll(x, 1, 1))


def next_row(x):
    return pltpu.roll(x, x.shape[0] - 1, 0)


def row_before(x):
    return pltpu.roll(x, 1, 0)


def move_velocity(s_ref, v_ref, plus_ref, minus_ref, layers, s_off, v_off, scale):
    def combine(x, _):
        field = [s_ref[at, x + s_off] for at in range(6)]
        later = [after(value) for value in field]
        total = [a + b for a, b in zip(field, later)]
        change = [b - a for a, b in zip(field, later)]
        for at, (lead, side, deep) in enumerate(((0, 5, 4), (5, 1, 3), (4, 3, 2))):
            ahead = total[lead] + next_row(total[lead])
            rest = next_row(total[side] + change[deep]) + (change[deep] - total[side])
            plus_ref[at, x] = rest + ahead
            minus_ref[at, x] = rest - ahead
        return 0

    lax.fori_loop(0, layers + 1, combine, 0)

    def update(x, _):
        factor = scale(x)
        for at in range(3):
            v_ref[at, x + v_off] = v_ref[at, x + v_off] + factor * (
                plus_ref[at, x + 1] + minus_ref[at, x]
            )
        return 0

    lax.fori_loop(0, layers, update, 0)


def add_sources(v_ref, cells_ref, signal_ref, place_ref, step_at, first, layers, v_off):
    def one(at, _):
        layer = cells_ref[at, 0] - 4 * place_ref[0] - first
        chord = cells_ref[at, 1] - 16 * place_ref[1]
        row = jnp.where(chord < 0, chord + ROWS, chord)
        deep = cells_ref[at, 2]

        @pl.when((layer >= 0) & (layer < layers) & (chord >= -DEEP) & (chord < 16 + DEEP))
        def _():
            rows = pl.ds(pl.multiple_of((row // 8) * 8, 8), 8)
            lanes = pl.ds(pl.multiple_of((deep // 128) * 128, 128), 128)
            hit = (lax.broadcasted_iota(jnp.int32, (8, 128), 0) == row % 8) & (
                lax.broadcasted_iota(jnp.int32, (8, 128), 1) == deep % 128
            )
            old = v_ref[2, layer + v_off, rows, lanes]
            v_ref[2, layer + v_off, rows, lanes] = old + jnp.where(
                hit, signal_ref[at, step_at], 0.0
            )

        return 0

    lax.fori_loop(0, 16, one, 0)


def strain_parts(v_ref, at_layer):
    sums, rows, deeps = [], [], []
    for at in range(3):
        value = v_ref[at, at_layer]
        earlier = before(value)
        total, change = value + earlier, value - earlier
        behind = row_before(total)
        sums.append(total + behind)
        rows.append(total - behind)
        deeps.append(change + row_before(change))
    return (
        sums[0],
        rows[1],
        deeps[2],
        rows[2] + deeps[1],
        deeps[0] + sums[2],
        deeps[0] - sums[2],
        rows[0] + sums[1],
        rows[0] - sums[1],
    )


def move_stress(v_ref, s_ref, q_ref, part_ref, layers, v_off, s_off, scale):
    def fill(x, _):
        for at, value in enumerate(strain_parts(v_ref, x + v_off - 1)):
            part_ref[at, x] = value
        return 0

    lax.fori_loop(0, layers + 1, fill, 0)

    def update(x, _):
        now = lambda at: part_ref[at, x + 1]
        old = lambda at: part_ref[at, x]
        e = (
            now(0) - old(0),
            now(1) + old(1),
            now(2) + old(2),
            now(3) + old(3),
            now(4) + old(5),
            now(6) + old(7),
        )
        a, b, c = q_ref[0, x], q_ref[1, x], q_ref[2, x]
        w = jnp.sqrt(jnp.maximum(1.0 - a * a - b * b - c * c, 0.0))
        ab, ac, bc = a * b, a * c, b * c
        wa, wb, wc = w * a, w * b, w * c
        aa, bb, cc = a * a, b * b, c * c
        columns = (
            (1.0 - 2.0 * (bb + cc), 2.0 * (ab + wc), 2.0 * (ac - wb)),
            (2.0 * (ab - wc), 1.0 - 2.0 * (aa + cc), 2.0 * (bc + wa)),
        )
        trace = e[0] + e[1] + e[2]
        bonds, along = [], []
        for p, q, r in columns:
            bond = (p * p, q * q, r * r, q * r, r * p, p * q)
            bonds.append(bond)
            part = bond[0] * e[0]
            for at in range(1, 6):
                part = part + bond[at] * e[at]
            along.append(part)
        third = trace - along[0] - along[1]
        first_weight = anisotropy * (along[0] - third)
        second_weight = anisotropy * (along[1] - third)
        level = cross_modulus * trace + anisotropy * third
        factor = scale(x)
        for at in range(6):
            rate = bonds[0][at] * first_weight + bonds[1][at] * second_weight
            if at < 3:
                rate = rate + (2.0 * shear_modulus * e[at] + level)
            else:
                rate = rate + shear_modulus * e[at]
            s_ref[at, x + s_off] = s_ref[at, x + s_off] + factor * rate
        return 0

    lax.fori_loop(0, layers, update, 0)


def row_scale(place_ref):
    row = lax.broadcasted_iota(jnp.int32, (ROWS, 512), 0)
    outside = ((row >= 16 + DEEP) & (place_ref[1] == 0)) | (
        (row >= 16) & (row < 16 + DEEP) & (place_ref[1] == 7)
    )
    return jnp.where(outside, 0.0, 0.25 * time_step)


def velocity_scale(base, place_ref, lowest):
    return lambda x: jnp.where((x == lowest) & (place_ref[0] == 0), 0.0, base)


def stress_scale(base, place_ref, highest):
    return lambda x: jnp.where((x == highest) & (place_ref[0] == 15), 0.0, base)


def send_out(v_ref, v_off, place_ref, chip_ref, far_ref):
    core = place_ref[0] % 2
    for at in range(3):
        chip_ref[at] = v_ref[at, v_off + 3 - 3 * core]
        far_ref[at] = v_ref[at, v_off + 3 * core]


def pack_kernel(v_ref, s_ref, right_ref, left_ref, low_ref, high_ref):
    for ref, rows in ((low_ref, slice(0, DEEP)), (high_ref, slice(16 - DEEP, 16))):
        for at in range(6):
            ref[7 * at] = left_ref[at, rows]
            ref[7 * at + 1 : 7 * at + 5] = s_ref[at, :, rows]
            ref[7 * at + 5 : 7 * at + 7] = right_ref[2 * at : 2 * at + 2, rows]
        for at in range(3):
            ref[42 + 6 * at] = left_ref[6 + at, rows]
            ref[42 + 6 * at + 1 : 42 + 6 * at + 5] = v_ref[at, :, rows]
            ref[42 + 6 * at + 5] = right_ref[12 + at, rows]


def first_kernel(
    place_ref, cells_ref, signal_ref,
    v_ref, s_ref, right_ref, left_ref, next_ref, prior_ref, turn_ref, next_turn_ref, prior_turn_ref,
    v_out, s_out, q_out, chip_ref, far_ref,
    v_all, s_all, plus_ref, minus_ref, part_ref,
):
    for at in range(6):
        s_all[at, 0, 0:16] = left_ref[at]
        s_all[at, 1:5, 0:16] = s_ref[at]
        s_all[at, 5:7, 0:16] = right_ref[2 * at : 2 * at + 2]
        s_all[at, :, 16 : 16 + DEEP] = next_ref[7 * at : 7 * at + 7]
        s_all[at, :, 16 + DEEP : 24] = prior_ref[7 * at : 7 * at + 7]
    for at in range(3):
        v_all[at, 0, 0:16] = left_ref[6 + at]
        v_all[at, 1:5, 0:16] = v_ref[at]
        v_all[at, 5, 0:16] = right_ref[12 + at]
        v_all[at, :, 16 : 16 + DEEP] = next_ref[42 + 6 * at : 48 + 6 * at]
        v_all[at, :, 16 + DEEP : 24] = prior_ref[42 + 6 * at : 48 + 6 * at]
        q_out[at, :, 0:16] = turn_ref[5 * at : 5 * at + 5]
        q_out[at, :, 16 : 16 + DEEP] = next_turn_ref[5 * at : 5 * at + 5]
        q_out[at, :, 16 + DEEP : 24] = prior_turn_ref[5 * at : 5 * at + 5]
    base = row_scale(place_ref)
    move_velocity(s_all, v_all, plus_ref, minus_ref, 6, 0, 0, velocity_scale(base, place_ref, 0))
    add_sources(v_all, cells_ref, signal_ref, place_ref, 0, -1, 6, 0)
    for at in range(6):
        s_out[at] = s_all[at, 1:6]
    move_stress(v_all, s_out, q_out, part_ref, 5, 1, 0, stress_scale(base, place_ref, 4))
    for at in range(3):
        v_out[at] = v_all[at, 1:5]
    move_velocity(s_out, v_out, plus_ref, minus_ref, 4, 0, 0, lambda x: base)
    add_sources(v_out, cells_ref, signal_ref, place_ref, 1, 0, 4, 0)
    send_out(v_out, 0, place_ref, chip_ref, far_ref)


def step_kernel(
    step_at, place_ref, cells_ref, signal_ref, v_ref, s_ref, q_ref, chip_ref, far_ref,
    v_out, s_out, next_chip_ref, next_far_ref, v_all, plus_ref, minus_ref, part_ref,
):
    odd = place_ref[0] % 2 == 1
    for at in range(3):
        v_all[at, 0] = jnp.where(odd, chip_ref[at], far_ref[at])
        v_all[at, 1:5] = v_ref[at]
        v_all[at, 5] = jnp.where(odd, far_ref[at], chip_ref[at])
        v_out[at] = v_ref[at]
    s_out[...] = s_ref[...]
    base = row_scale(place_ref)
    move_stress(v_all, s_out, q_ref, part_ref, 5, 1, 0, stress_scale(base, place_ref, 4))
    move_velocity(s_out, v_out, plus_ref, minus_ref, 4, 0, 0, lambda x: base)
    add_sources(v_out, cells_ref, signal_ref, place_ref, step_at, 0, 4, 0)
    send_out(v_out, 0, place_ref, next_chip_ref, next_far_ref)


def last_kernel(
    place_ref, cells_ref, signal_ref, v_ref, s_ref, q_ref, chip_ref, far_ref,
    v_out, s_out, v_all, s_all, part_ref,
):
    odd = place_ref[0] % 2 == 1
    for at in range(3):
        v_all[at, 0] = jnp.where(odd, chip_ref[at], far_ref[at])
        v_all[at, 1:5] = v_ref[at, :, :]
        v_out[at] = v_ref[at, :, 0:16]
    s_all[...] = s_ref[:, 0:4]
    base = row_scale(place_ref)
    move_stress(v_all, s_all, q_ref, part_ref, 4, 1, 0, lambda x: base)
    s_out[...] = s_all[:, :, 0:16, :]


def shift(x, axis, by):
    peers = lax.axis_size(axis)
    pairs = [(i, i + by) for i in range(peers) if 0 <= i + by < peers]
    return lax.ppermute(x, axis, pairs)


def swap(x, first):
    peers = lax.axis_size("span")
    pairs = []
    for i in range(first, peers - 1, 2):
        pairs += [(i, i + 1), (i + 1, i)]
    return lax.ppermute(x, "span", pairs)


def shards(
    velocity, stress, grain_ids, lattice_tilt, grain_orient, orientations, source_cells, source_signal
):
    place = jnp.stack([lax.axis_index("span"), lax.axis_index("chord")]).astype(jnp.int32)
    known = (place, source_cells, source_signal)

    to_left = jnp.concatenate(
        (stress[:, 0:2].reshape(12, 16, 512), velocity[:, 0].reshape(3, 16, 512)), axis=0
    )
    to_right = jnp.concatenate((stress[:, 3], velocity[:, 3]), axis=0)
    right = shift(to_left, "span", -1)
    left = shift(to_right, "span", 1)

    (sent,) = call(
        rotation_kernel,
        [(16, 64, 128)],
        (
            jnp.transpose(grain_ids, (1, 2, 0)),
            jnp.transpose(lattice_tilt, (0, 2, 3, 1)),
            grain_orient.reshape(32, 128),
            orientations.reshape(3, 4, 128),
        ),
        scratch=[(3, 4, 72, 128)],
        flops=32768 * 200,
    )
    got = lax.all_to_all(sent, "span", 0, 0, tiled=True)

    low, high = call(pack_kernel, [(60, DEEP, 512)] * 2, (velocity, stress, right, left))
    next_rows = shift(low, "chord", -1)
    prior_rows = shift(high, "chord", 1)

    turn, low, high = call(arrange_kernel, [(15, 16, 512), (15, DEEP, 512), (15, DEEP, 512)], (got,))
    next_turn = shift(low, "chord", -1)
    prior_turn = shift(high, "chord", 1)

    v_shape, s_shape, q_shape, edge = (3, 4, ROWS, 512), (6, 5, ROWS, 512), (3, 5, ROWS, 512), (3, ROWS, 512)
    work = [(3, 7, ROWS, 512), (3, 7, ROWS, 512), (8, 6, ROWS, 512)]
    v, s, q, chip, far = call(
        first_kernel,
        [v_shape, s_shape, q_shape, edge, edge],
        (*known, velocity, stress, right, left, next_rows, prior_rows, turn, next_turn, prior_turn),
        scalars=3,
        scratch=[(3, 6, ROWS, 512), (6, 7, ROWS, 512), *work],
    )
    for step_at in (2, 3):
        chip, far = swap(chip, 0), swap(far, 1)
        v, s, chip, far = call(
            lambda *refs, step_at=step_at: step_kernel(step_at, *refs),
            [v_shape, s_shape, edge, edge],
            (*known, v, s, q, chip, far),
            scalars=3,
            scratch=[(3, 6, ROWS, 512), *work],
        )
    chip, far = swap(chip, 0), swap(far, 1)
    v, s = call(
        last_kernel,
        [velocity.shape, stress.shape],
        (*known, v, s, q, chip, far),
        scalars=3,
        scratch=[(3, 5, ROWS, 512), (6, 4, ROWS, 512), work[2]],
    )
    return v, s


def solution(mesh):
    return jax.shard_map(
        shards,
        mesh=mesh,
        in_specs=(
            P(None, "span", "chord", None),
            P(None, "span", "chord", None),
            P(None, "chord", "span"),
            P(None, None, "chord", "span"),
            P(),
            P(),
            P(),
            P(),
        ),
        out_specs=(P(None, "span", "chord", None), P(None, "span", "chord", None)),
        check_vma=False,
    )
```

```python
import jax
import jax.numpy as jnp
from jax import lax
from jax.experimental import pallas as pl
from jax.experimental.pallas import tpu as pltpu
from jax.sharding import PartitionSpec as P

normal_modulus = 0.9
cross_modulus = 1.6
shear_modulus = 1.3
time_step = 0.25
anisotropy = normal_modulus - 2.0 * shear_modulus

DEEP = 4
ROWS = 24
TABLE_ROWS = 11
VMEM = pltpu.CompilerParams(vmem_limit_bytes=20 * 2**20)
WHOLE = pl.BlockSpec(memory_space=pltpu.VMEM)
SCALARS = pl.BlockSpec(memory_space=pltpu.SMEM)


def call(kernel, outs, operands, scalars=0, scratch=(), flops=0):
    return pl.pallas_call(
        kernel,
        out_shape=[jax.ShapeDtypeStruct(shape, jnp.float32) for shape in outs],
        in_specs=[SCALARS] * scalars + [WHOLE] * (len(operands) - scalars),
        out_specs=[WHOLE] * len(outs),
        scratch_shapes=[pltpu.VMEM(shape, jnp.float32) for shape in scratch],
        compiler_params=VMEM,
        cost_estimate=pl.CostEstimate(
            flops=flops,
            bytes_accessed=4 * sum(operand.size for operand in operands),
            transcendentals=0,
        ),
    )(*operands)


def small_sin(x):
    y = x * x
    return x * (
        1.0 + y * (-1.0 / 6 + y * (1.0 / 120 + y * (-1.0 / 5040 + y * (1.0 / 362880))))
    )


def small_cos(x):
    y = x * x
    return 1.0 + y * (
        -0.5
        + y * (1.0 / 24 + y * (-1.0 / 720 + y * (1.0 / 40320 + y * (-1.0 / 3628800))))
    )


def wide_sin_cos(x):
    quarter = 0.25 * x
    s, c = small_sin(quarter), small_cos(quarter)
    s, c = 2.0 * s * c, 1.0 - 2.0 * s * s
    return 2.0 * s * c, 1.0 - 2.0 * s * s


def quaternion(first, middle, last, sin_cos):
    s_mid, c_mid = sin_cos(0.5 * middle)
    s_sum, c_sum = sin_cos(0.5 * (first + last))
    s_dif, c_dif = sin_cos(0.5 * (first - last))
    return c_mid * c_sum, -s_mid * c_dif, -s_mid * s_dif, -c_mid * s_sum


def product(a, b):
    return (
        a[0] * b[0] - a[1] * b[1] - a[2] * b[2] - a[3] * b[3],
        a[0] * b[1] + a[1] * b[0] + a[2] * b[3] - a[3] * b[2],
        a[0] * b[2] - a[1] * b[3] + a[2] * b[0] + a[3] * b[1],
        a[0] * b[3] + a[1] * b[2] - a[2] * b[1] + a[3] * b[0],
    )


def reduced(q):
    w, x, y, z = q
    aw, ax, ay, az = jnp.abs(w), jnp.abs(x), jnp.abs(y), jnp.abs(z)
    low, high = jnp.maximum(aw, ax), jnp.maximum(ay, az)
    upper = high > low
    second = jnp.where(upper, az - ay, ax - aw) > 0.0

    def pick(a, b, c, d):
        return jnp.where(upper, jnp.where(second, d, c), jnp.where(second, b, a))

    lead = pick(w, x, y, z)
    flip = jnp.where(lead < 0.0, -1.0, 1.0)
    return (
        pick(x, -w, z, -y) * flip,
        pick(y, -z, -w, x) * flip,
        pick(z, y, -x, -w) * flip,
    )


def look_up(row, lane):
    return jnp.take_along_axis(
        jnp.broadcast_to(row, lane.shape), lane, axis=1, mode="promise_in_bounds"
    )


def rotation_kernel(ids_ref, tilt_ref, grain_ref, angle_ref, out_ref, turned_ref):
    packed = []
    for at in range(TABLE_ROWS):
        row = grain_ref[at : at + 1, :] + grain_ref[at + 11 : at + 12, :] * 512
        if at + 22 < 32:
            row = row + grain_ref[at + 22 : at + 23, :] * (512 * 512)
        packed.append(row)
    table = quaternion(angle_ref[0], angle_ref[1], angle_ref[2], wide_sin_cos)
    entries = [[part[at : at + 1, :] for at in range(4)] for part in table]
    for pair in range(2):
        parts = [[], [], []]
        for group in range(4):
            chord = 4 * group + 2 * pair
            both = lambda ref, *lead: jnp.concatenate(
                [ref[(*lead, chord)], ref[(*lead, chord + 1)]], axis=1
            )
            grain = both(ids_ref)
            third = jnp.where(grain >= 2816, 2, jnp.where(grain >= 1408, 1, 0))
            grain = grain - 1408 * third
            lane, place = grain & 127, grain >> 7
            entry = look_up(packed[0], lane)
            for at in range(1, TABLE_ROWS):
                entry = jnp.where(place == at, look_up(packed[at], lane), entry)
            entry = (entry >> (9 * third)) & 511
            lane, place = entry & 127, entry >> 7
            grain_turn = []
            for part in entries:
                low = jnp.where(place == 1, look_up(part[1], lane), look_up(part[0], lane))
                high = jnp.where(place == 3, look_up(part[3], lane), look_up(part[2], lane))
                grain_turn.append(jnp.where(place >= 2, high, low))
            tilt_turn = quaternion(
                both(tilt_ref, 0),
                both(tilt_ref, 1),
                both(tilt_ref, 2),
                lambda x: (small_sin(x), small_cos(x)),
            )
            for at, value in enumerate(reduced(product(grain_turn, tilt_turn))):
                parts[at].append(value)
        for at in range(3):
            turned = jnp.concatenate(parts[at], axis=0).T
            for half in range(2):
                turned_ref[at, 2 * pair + half, 0:64, :] = turned[64 * half : 64 * half + 64, :]
    for at in range(3):
        for rest in range(4):
            turned_ref[at, rest, 64:72, :] = jnp.zeros((8, 128), jnp.float32)
    for device in range(16):
        for at in range(3):
            for layer in range(5):
                row = 20 * at + 4 * layer
                out_ref[device, row : row + 4, :] = turned_ref[at, :, 4 * device + layer, :]
        out_ref[device, 60:64, :] = jnp.zeros((4, 128), jnp.float32)


def arrange_kernel(got_ref, out_ref, low_ref, high_ref):
    for four in range(4):
        pieces = [got_ref[4 * four + at] for at in range(4)]
        for group in range(4):
            lanes = jnp.concatenate(
                [piece[:, 32 * group : 32 * group + 32] for piece in pieces], axis=1
            )
            for at in range(15):
                out_ref[at, 4 * group : 4 * group + 4, 128 * four : 128 * four + 128] = lanes[
                    4 * at : 4 * at + 4, :
                ]
    for at in range(15):
        low_ref[3 * at : 3 * at + 3, :] = out_ref[at, 0:3, :]
        high_ref[3 * at : 3 * at + 3, :] = out_ref[at, 13:16, :]
    low_ref[45:48, :] = jnp.zeros((3, 512), jnp.float32)
    high_ref[45:48, :] = jnp.zeros((3, 512), jnp.float32)


SCALE = 0.25 * time_step
LANES = [slice(128 * at, 128 * at + 128) for at in range(4)]


def lane_is(at):
    return lax.broadcasted_iota(jnp.int32, (ROWS, 128), 1) == at


def next_row(x):
    return pltpu.roll(x, ROWS - 1, 0)


def row_before(x):
    return pltpu.roll(x, 1, 0)


def strain_parts(load):
    first = lane_is(0)
    held = [0.0] * 3
    for lanes in LANES:
        sums, rows, deeps = [], [], []
        for at in range(3):
            value = load(at, lanes)
            rolled = pltpu.roll(value, 1, 1)
            earlier = jnp.where(first, held[at], rolled)
            held[at] = rolled
            total, change = value + earlier, value - earlier
            behind = row_before(total)
            sums.append(total + behind)
            rows.append(total - behind)
            deeps.append(change + row_before(change))
        yield lanes, (
            sums[0],
            rows[1],
            deeps[2],
            rows[2] + deeps[1],
            deeps[0] + sums[2],
            deeps[0] - sums[2],
            rows[0] + sums[1],
            rows[0] - sums[1],
        )


def strains(now, old):
    return (
        now[0] - old[0],
        now[1] + old[1],
        now[2] + old[2],
        now[3] + old[3],
        now[4] + old[5],
        now[6] + old[7],
    )


def force_parts(load, need=(True, True)):
    last = lane_is(127)
    held = [0.0] * 6
    for lanes in reversed(LANES):
        total, change = [], []
        for at in range(6):
            value = load(at, lanes)
            rolled = pltpu.roll(value, 127, 1)
            later = jnp.where(last, held[at], rolled)
            held[at] = rolled
            total.append(value + later)
            change.append(later - value)
        plus, minus = [], []
        for lead, side, deep in ((0, 5, 4), (5, 1, 3), (4, 3, 2)):
            ahead = total[lead] + next_row(total[lead])
            rest = next_row(total[side] + change[deep]) + (change[deep] - total[side])
            plus.append(rest + ahead if need[0] else None)
            minus.append(rest - ahead if need[1] else None)
        yield lanes, plus, minus


def stress_rates(e, first_bond, second_bond):
    trace = e[0] + e[1] + e[2]
    along = []
    for bond in (first_bond, second_bond):
        part = bond[0] * e[0]
        for at in range(1, 6):
            part = part + bond[at] * e[at]
        along.append(part)
    third = trace - along[0] - along[1]
    first_weight = (SCALE * anisotropy) * (along[0] - third)
    second_weight = (SCALE * anisotropy) * (along[1] - third)
    level = (SCALE * cross_modulus) * trace + (SCALE * anisotropy) * third
    rates = []
    for at in range(6):
        rate = first_bond[at] * first_weight + second_bond[at] * second_weight
        if at < 3:
            rate = rate + ((2.0 * SCALE * shear_modulus) * e[at] + level)
        else:
            rate = rate + (SCALE * shear_modulus) * e[at]
        rates.append(rate)
    return rates


def bonds_of(a, b, c):
    w = jnp.sqrt(jnp.maximum(1.0 - a * a - b * b - c * c, 0.0))
    ab, ac, bc = a * b, a * c, b * c
    wa, wb, wc = w * a, w * b, w * c
    aa, bb, cc = a * a, b * b, c * c
    bonds = []
    for p, q, r in (
        (1.0 - 2.0 * (bb + cc), 2.0 * (ab + wc), 2.0 * (ac - wb)),
        (2.0 * (ab - wc), 1.0 - 2.0 * (aa + cc), 2.0 * (bc + wa)),
    ):
        bonds += [p * p, q * q, r * r, q * r, r * p, p * q]
    return bonds


def outer_scale(outside_low, outside_high):
    row = lax.broadcasted_iota(jnp.int32, (8, 128), 0)
    outside = ((row < DEEP) & outside_high) | ((row >= DEEP) & outside_low)
    return jnp.where(outside, 0.0, 1.0)


def put(ref, lead, lanes, value, outer):
    ref[(*lead, slice(0, 16), lanes)] = value[0:16]
    ref[(*lead, slice(16, ROWS), lanes)] = value[16:ROWS] * outer


def add_sources(v_ref, cells_ref, signal_ref, place_ref, step_at, places):
    first, layers, v_off = places

    def one(at, _):
        layer = cells_ref[at, 0] - 4 * place_ref[0] - first
        chord = cells_ref[at, 1] - 16 * place_ref[1]
        row = jnp.where(chord < 0, chord + ROWS, chord)
        deep = cells_ref[at, 2]

        @pl.when((layer >= 0) & (layer < layers) & (chord >= -DEEP) & (chord < 16 + DEEP))
        def _():
            rows = pl.ds(pl.multiple_of((row // 8) * 8, 8), 8)
            lanes = pl.ds(pl.multiple_of((deep // 128) * 128, 128), 128)
            hit = (lax.broadcasted_iota(jnp.int32, (8, 128), 0) == row % 8) & (
                lax.broadcasted_iota(jnp.int32, (8, 128), 1) == deep % 128
            )
            old = v_ref[2, layer + v_off, rows, lanes]
            v_ref[2, layer + v_off, rows, lanes] = old + jnp.where(
                hit, signal_ref[at, step_at], 0.0
            )

        return 0

    lax.fori_loop(0, 16, one, 0)


def send_out(v_ref, place_ref, chip_ref, far_ref):
    core = place_ref[0] % 2
    for at in range(3):
        chip_ref[at] = v_ref[at, 3 - 3 * core]
        far_ref[at] = v_ref[at, 3 * core]


def edge_kernel(v_ref, s_ref, low_ref, high_ref):
    for ref, rows in ((low_ref, slice(0, DEEP)), (high_ref, slice(16 - DEEP, 16))):
        for at in range(6):
            ref[4 * at : 4 * at + 4] = s_ref[at, :, rows]
        for at in range(3):
            ref[24 + 4 * at : 28 + 4 * at] = v_ref[at, :, rows]


def before_span_kernel(
    place_ref, cells_ref, signal_ref, v_ref, s_ref, next_ref, prior_ref,
    v_out, s_out, low_ref, high_ref, minus_ref,
):
    for out, ref, first, count in ((s_out, s_ref, 0, 6), (v_out, v_ref, 24, 3)):
        for at in range(count):
            out[at, :, 0:16] = ref[at]
            out[at, :, 16 : 16 + DEEP] = next_ref[first + 4 * at : first + 4 * at + 4]
            out[at, :, 16 + DEEP : ROWS] = prior_ref[first + 4 * at : first + 4 * at + 4]
    outer = outer_scale(place_ref[1] == 0, False)
    for x in range(4):
        load = lambda at, lanes: s_out[at, x, :, lanes]
        for lanes, plus, minus in force_parts(load, (x > 0, x < 3)):
            for at in range(3):
                if x > 0:
                    value = v_out[at, x - 1, :, lanes] + SCALE * (plus[at] + minus_ref[at, :, lanes])
                    put(v_out, (at, x - 1), lanes, value, outer)
                if x < 3:
                    minus_ref[at, :, lanes] = minus[at]
    add_sources(v_out, cells_ref, signal_ref, place_ref, 0, (0, 3, 0))
    for at in range(6):
        low_ref[at] = s_out[at, 0]
        high_ref[at] = s_out[at, 3]
    for at in range(3):
        low_ref[6 + at] = v_out[at, 0]
        high_ref[6 + at] = v_out[at, 3]


def after_span_kernel(
    place_ref, cells_ref, signal_ref, v_ref, s_ref, right_ref, left_ref,
    v_out, e_out, v_all, minus_ref, part_ref,
):
    outer = outer_scale(place_ref[1] == 0, False)
    inside = jnp.where(place_ref[0] == 0, 0.0, outer)
    inside_rows = jnp.where(place_ref[0] == 0, 0.0, 1.0)
    for at in range(3):
        v_all[at, 1:4] = v_ref[at, 0:3]
        v_all[at, 5] = right_ref[6 + at]
    for low, high, slot, held, factor in (
        (lambda at, lanes: left_ref[at, :, lanes], lambda at, lanes: s_ref[at, 0, :, lanes],
         0, lambda at, lanes: left_ref[6 + at, :, lanes], inside_rows),
        (lambda at, lanes: s_ref[at, 3, :, lanes], lambda at, lanes: right_ref[at, :, lanes],
         4, lambda at, lanes: v_ref[at, 3, :, lanes], 1.0),
    ):
        for lanes, _, minus in force_parts(low, (False, True)):
            for at in range(3):
                minus_ref[at, :, lanes] = minus[at]
        for lanes, plus, _ in force_parts(high, (True, False)):
            for at in range(3):
                value = held(at, lanes) + SCALE * (plus[at] + minus_ref[at, :, lanes])
                put(v_all, (at, slot), lanes, value * factor, outer)
    add_sources(v_all, cells_ref, signal_ref, place_ref, 0, (-1, 1, 0))
    add_sources(v_all, cells_ref, signal_ref, place_ref, 0, (3, 1, 4))
    for at in range(3):
        v_out[at] = v_all[at, 1:5]
    for x in range(-1, 5):
        for lanes, now in strain_parts(lambda at, lanes: v_all[at, x + 1, :, lanes]):
            if x >= 0:
                old = [part_ref[at, :, lanes] for at in range(8)]
                for at, value in enumerate(strains(now, old)):
                    e_out[at, x, :, lanes] = value
            if x < 4:
                for at in range(8):
                    part_ref[at, :, lanes] = now[at]


def move_on(x, layers, strain_of, bond_of, s_of, s_out, v_of, v_out, minus_ref, place_ref, outer_s, outer_v):
    edge = jnp.where(place_ref[0] == 15, 0.0, 1.0)
    for lanes, e in strain_of(x):
        bonds = bond_of(x, lanes)
        for at, rate in enumerate(stress_rates(e, bonds[:6], bonds[6:])):
            if x == 4:
                rate = rate * edge
            put(s_out, (at, x), lanes, s_of(at, x, lanes) + rate, outer_s)
    load = lambda at, lanes: s_out[at, x, :, lanes]
    for lanes, plus, minus in force_parts(load, (x > 0, x < 4)):
        for at in range(3):
            if x > 0:
                value = v_of(at, x - 1, lanes) + SCALE * (plus[at] + minus_ref[at, :, lanes])
                put(v_out, (at, x - 1), lanes, value, outer_v)
            if x < 4:
                minus_ref[at, :, lanes] = minus[at]


def first_kernel(
    place_ref, cells_ref, signal_ref,
    v_ref, e_ref, s_ref, right_ref, turn_ref, next_ref, prior_ref,
    v_out, s_out, b_out, chip_ref, far_ref,
    q_ref, minus_ref,
):
    q_ref[...] = jnp.zeros(q_ref.shape, jnp.float32)
    for at in range(15):
        q_ref[at, 0:16] = turn_ref[at]
        q_ref[at, 16:19] = next_ref[3 * at : 3 * at + 3]
        q_ref[at, 21:24] = prior_ref[3 * at : 3 * at + 3]
    outer_s = outer_scale(False, place_ref[1] == 7)
    outer_v = outer_scale(place_ref[1] == 0, False)

    def bond_of(x, lanes):
        bonds = bonds_of(*[q_ref[5 * at + x, :, lanes] for at in range(3)])
        for at, value in enumerate(bonds):
            b_out[at, x, :, lanes] = value
        return bonds

    def strain_of(x):
        for lanes in LANES:
            yield lanes, [e_ref[at, x, :, lanes] for at in range(6)]

    def s_of(at, x, lanes):
        return s_ref[at, x, :, lanes] if x < 4 else right_ref[at, :, lanes]

    v_of = lambda at, x, lanes: v_ref[at, x, :, lanes]
    for x in range(5):
        move_on(x, 5, strain_of, bond_of, s_of, s_out, v_of, v_out, minus_ref, place_ref, outer_s, outer_v)
    add_sources(v_out, cells_ref, signal_ref, place_ref, 1, (0, 4, 0))
    send_out(v_out, place_ref, chip_ref, far_ref)


def step_kernel(
    step_at, place_ref, cells_ref, signal_ref, v_ref, s_ref, b_ref, chip_ref, far_ref,
    v_out, s_out, next_chip_ref, next_far_ref, side_ref, minus_ref, part_ref,
):
    odd = place_ref[0] % 2 == 1
    for at in range(3):
        side_ref[at, 0] = jnp.where(odd, chip_ref[at], far_ref[at])
        side_ref[at, 1] = jnp.where(odd, far_ref[at], chip_ref[at])
    outer_s = outer_scale(False, place_ref[1] == 7)
    outer_v = outer_scale(place_ref[1] == 0, False)

    def layer(x):
        if 0 <= x < 4:
            return lambda at, lanes: v_ref[at, x, :, lanes]
        return lambda at, lanes: side_ref[at, 0 if x < 0 else 1, :, lanes]

    for lanes, now in strain_parts(layer(-1)):
        for at in range(8):
            part_ref[at, :, lanes] = now[at]

    def strain_of(x):
        for lanes, now in strain_parts(layer(x)):
            old = [part_ref[at, :, lanes] for at in range(8)]
            if x < 4:
                for at in range(8):
                    part_ref[at, :, lanes] = now[at]
            yield lanes, strains(now, old)

    bond_of = lambda x, lanes: [b_ref[at, x, :, lanes] for at in range(12)]
    s_of = lambda at, x, lanes: s_ref[at, x, :, lanes]
    v_of = lambda at, x, lanes: v_ref[at, x, :, lanes]
    for x in range(5):
        move_on(x, 5, strain_of, bond_of, s_of, s_out, v_of, v_out, minus_ref, place_ref, outer_s, outer_v)
    add_sources(v_out, cells_ref, signal_ref, place_ref, step_at, (0, 4, 0))
    send_out(v_out, place_ref, next_chip_ref, next_far_ref)


def last_kernel(
    place_ref, v_ref, s_ref, b_ref, chip_ref, far_ref, v_out, s_out, side_ref, part_ref
):
    odd = place_ref[0] % 2 == 1
    for at in range(3):
        side_ref[at] = jnp.where(odd, chip_ref[at], far_ref[at])
        v_out[at] = v_ref[at, :, 0:16]
    for x in range(-1, 4):
        layer = lambda at, lanes: side_ref[at, :, lanes] if x < 0 else v_ref[at, x, :, lanes]
        for lanes, now in strain_parts(layer):
            if x >= 0:
                e = strains(now, [part_ref[at, :, lanes] for at in range(8)])
                e = [value[0:16] for value in e]
                bonds = [b_ref[at, x, 0:16, lanes] for at in range(12)]
                for at, rate in enumerate(stress_rates(e, bonds[:6], bonds[6:])):
                    s_out[at, x, :, lanes] = s_ref[at, x, 0:16, lanes] + rate
            if x < 3:
                for at in range(8):
                    part_ref[at, :, lanes] = now[at]


def shift(x, axis, by):
    peers = lax.axis_size(axis)
    pairs = [(i, i + by) for i in range(peers) if 0 <= i + by < peers]
    return lax.ppermute(x, axis, pairs)


def swap(x, first):
    peers = lax.axis_size("span")
    pairs = []
    for i in range(first, peers - 1, 2):
        pairs += [(i, i + 1), (i + 1, i)]
    return lax.ppermute(x, "span", pairs)


def shards(
    velocity, stress, grain_ids, lattice_tilt, grain_orient, orientations, source_cells, source_signal
):
    place = jnp.stack([lax.axis_index("span"), lax.axis_index("chord")]).astype(jnp.int32)
    known = (place, source_cells, source_signal)

    low, high = call(edge_kernel, [(36, DEEP, 512)] * 2, (velocity, stress))
    next_rows = shift(low, "chord", -1)
    prior_rows = shift(high, "chord", 1)

    (sent,) = call(
        rotation_kernel,
        [(16, 64, 128)],
        (
            jnp.transpose(grain_ids, (1, 2, 0)),
            jnp.transpose(lattice_tilt, (0, 2, 3, 1)),
            grain_orient.reshape(32, 128),
            orientations.reshape(3, 4, 128),
        ),
        scratch=[(3, 4, 72, 128)],
        flops=32768 * 200,
    )
    got = lax.all_to_all(sent, "span", 0, 0, tiled=True)

    v_shape, s_shape, edge = (3, 4, ROWS, 512), (6, 5, ROWS, 512), (3, ROWS, 512)
    sides, minus, part = (3, 2, ROWS, 512), (3, ROWS, 512), (8, ROWS, 512)
    v, s, low, high = call(
        before_span_kernel,
        [v_shape, (6, 4, ROWS, 512), (9, ROWS, 512), (9, ROWS, 512)],
        (*known, velocity, stress, next_rows, prior_rows),
        scalars=3,
        scratch=[minus],
    )
    right = shift(low, "span", -1)
    left = shift(high, "span", 1)
    v, e = call(
        after_span_kernel,
        [v_shape, s_shape],
        (*known, v, s, right, left),
        scalars=3,
        scratch=[(3, 6, ROWS, 512), minus, part],
    )

    turn, low, high = call(arrange_kernel, [(15, 16, 512), (48, 512), (48, 512)], (got,))
    next_turn = shift(low, "chord", -1)
    prior_turn = shift(high, "chord", 1)

    v, s, bonds, chip, far = call(
        first_kernel,
        [v_shape, s_shape, (12, 5, ROWS, 512), edge, edge],
        (*known, v, e, s, right, turn, next_turn, prior_turn),
        scalars=3,
        scratch=[(15, ROWS, 512), minus],
    )
    for step_at in (2, 3):
        chip, far = swap(chip, 0), swap(far, 1)
        v, s, chip, far = call(
            lambda *refs, step_at=step_at: step_kernel(step_at, *refs),
            [v_shape, s_shape, edge, edge],
            (*known, v, s, bonds, chip, far),
            scalars=3,
            scratch=[sides, minus, part],
        )
    chip, far = swap(chip, 0), swap(far, 1)
    v, s = call(
        last_kernel,
        [velocity.shape, stress.shape],
        (place, v, s, bonds, chip, far),
        scalars=1,
        scratch=[edge, part],
    )
    return v, s


def solution(mesh):
    return jax.shard_map(
        shards,
        mesh=mesh,
        in_specs=(
            P(None, "span", "chord", None),
            P(None, "span", "chord", None),
            P(None, "chord", "span"),
            P(None, None, "chord", "span"),
            P(),
            P(),
            P(),
            P(),
        ),
        out_specs=(P(None, "span", "chord", None), P(None, "span", "chord", None)),
        check_vma=False,
    )
```

```python
import jax
import jax.numpy as jnp
from jax import lax
from jax.experimental import pallas as pl
from jax.experimental.pallas import tpu as pltpu
from jax.sharding import PartitionSpec as P

normal_modulus = 0.9
cross_modulus = 1.6
shear_modulus = 1.3
time_step = 0.25
anisotropy = normal_modulus - 2.0 * shear_modulus

DEEP = 4
ROWS = 24
TABLE_ROWS = 11
VMEM = pltpu.CompilerParams(vmem_limit_bytes=16 * 2**20)
WHOLE = pl.BlockSpec(memory_space=pltpu.VMEM)
LANES = [slice(128 * at, 128 * at + 128) for at in range(4)]


def call(kernel, outs, operands, scratch=(), spaces=(), aliases=None, flops=0):
    spaces = dict(spaces)
    return pl.pallas_call(
        kernel,
        out_shape=[jax.ShapeDtypeStruct(shape, jnp.float32) for shape in outs],
        in_specs=[pl.BlockSpec(memory_space=spaces.get(at, pltpu.VMEM)) for at in range(len(operands))],
        out_specs=[WHOLE] * len(outs),
        scratch_shapes=[
            pltpu.VMEM(shape, jnp.float32) if isinstance(shape, tuple) else shape for shape in scratch
        ],
        input_output_aliases=aliases or {},
        compiler_params=VMEM,
        cost_estimate=pl.CostEstimate(
            flops=flops,
            bytes_accessed=4 * sum(operand.size for operand in operands),
            transcendentals=0,
        ),
    )(*operands)


def small_sin(x):
    y = x * x
    return x * (
        1.0 + y * (-1.0 / 6 + y * (1.0 / 120 + y * (-1.0 / 5040 + y * (1.0 / 362880))))
    )


def small_cos(x):
    y = x * x
    return 1.0 + y * (
        -0.5
        + y * (1.0 / 24 + y * (-1.0 / 720 + y * (1.0 / 40320 + y * (-1.0 / 3628800))))
    )


def wide_sin_cos(x):
    quarter = 0.25 * x
    s, c = small_sin(quarter), small_cos(quarter)
    s, c = 2.0 * s * c, 1.0 - 2.0 * s * s
    return 2.0 * s * c, 1.0 - 2.0 * s * s


def quaternion(first, middle, last, sin_cos):
    s_mid, c_mid = sin_cos(0.5 * middle)
    s_sum, c_sum = sin_cos(0.5 * (first + last))
    s_dif, c_dif = sin_cos(0.5 * (first - last))
    return c_mid * c_sum, -s_mid * c_dif, -s_mid * s_dif, -c_mid * s_sum


def product(a, b):
    return (
        a[0] * b[0] - a[1] * b[1] - a[2] * b[2] - a[3] * b[3],
        a[0] * b[1] + a[1] * b[0] + a[2] * b[3] - a[3] * b[2],
        a[0] * b[2] - a[1] * b[3] + a[2] * b[0] + a[3] * b[1],
        a[0] * b[3] + a[1] * b[2] - a[2] * b[1] + a[3] * b[0],
    )


def reduced(q):
    w, x, y, z = q
    aw, ax, ay, az = jnp.abs(w), jnp.abs(x), jnp.abs(y), jnp.abs(z)
    low, high = jnp.maximum(aw, ax), jnp.maximum(ay, az)
    upper = high > low
    second = jnp.where(upper, az - ay, ax - aw) > 0.0

    def pick(a, b, c, d):
        return jnp.where(upper, jnp.where(second, d, c), jnp.where(second, b, a))

    lead = pick(w, x, y, z)
    flip = jnp.where(lead < 0.0, -1.0, 1.0)
    return (
        pick(x, -w, z, -y) * flip,
        pick(y, -z, -w, x) * flip,
        pick(z, y, -x, -w) * flip,
    )


def look_up(row, lane):
    return jnp.take_along_axis(
        jnp.broadcast_to(row, lane.shape), lane, axis=1, mode="promise_in_bounds"
    )


def turned_parts(grain, angles, grain_ref, angle_ref):
    packed = []
    for at in range(TABLE_ROWS):
        row = grain_ref[at : at + 1, :] + grain_ref[at + 11 : at + 12, :] * 512
        if at + 22 < 32:
            row = row + grain_ref[at + 22 : at + 23, :] * (512 * 512)
        packed.append(row)
    table = quaternion(angle_ref[0], angle_ref[1], angle_ref[2], wide_sin_cos)
    entries = [[part[at : at + 1, :] for at in range(4)] for part in table]
    third = jnp.where(grain >= 2816, 2, jnp.where(grain >= 1408, 1, 0))
    grain = grain - 1408 * third
    lane, place = grain & 127, grain >> 7
    entry = look_up(packed[0], lane)
    for at in range(1, TABLE_ROWS):
        entry = jnp.where(place == at, look_up(packed[at], lane), entry)
    entry = (entry >> (9 * third)) & 511
    lane, place = entry & 127, entry >> 7
    grain_turn = []
    for part in entries:
        low = jnp.where(place == 1, look_up(part[1], lane), look_up(part[0], lane))
        high = jnp.where(place == 3, look_up(part[3], lane), look_up(part[2], lane))
        grain_turn.append(jnp.where(place >= 2, high, low))
    tilt_turn = quaternion(*angles, lambda x: (small_sin(x), small_cos(x)))
    return reduced(product(grain_turn, tilt_turn))


def side_by_side(ref, *lead):
    *lead, chord = lead
    return jnp.concatenate([ref[(*lead, chord)], ref[(*lead, chord + 1)]], axis=1)


def rotation_kernel(ids_ref, tilt_ref, grain_ref, angle_ref, out_ref, sorted_ref):
    for pair in range(2):
        parts = [[], [], []]
        for group in range(4):
            chord = 4 * group + 2 * pair
            values = turned_parts(
                side_by_side(ids_ref, chord),
                [side_by_side(tilt_ref, at, chord) for at in range(3)],
                grain_ref,
                angle_ref,
            )
            for at in range(3):
                parts[at].append(values[at])
        for at in range(3):
            turned = jnp.concatenate(parts[at], axis=0).T
            for half in range(2):
                sorted_ref[at, pl.ds(2 * pair + half, 64, stride=4), :] = turned[
                    64 * half : 64 * half + 64, :
                ]
    for at in range(3):
        sorted_ref[at, 256:272, :] = jnp.zeros((16, 128), jnp.float32)
    for device in range(16):
        for at in range(3):
            row = 16 * device
            out_ref[device, 16 * at : 16 * at + 16, :] = sorted_ref[at, row : row + 16, :]
            out_ref[device, 48 + 4 * at : 52 + 4 * at, :] = sorted_ref[at, row + 16 : row + 20, :]


def arrange_kernel(got_ref, q_ref, pair_ref, other_ref):
    for four, deep in enumerate(LANES):
        pieces = [got_ref[4 * four + at] for at in range(4)]
        for group in range(4):
            lanes = jnp.concatenate(
                [piece[:, 32 * group : 32 * group + 32] for piece in pieces], axis=1
            )
            for at in range(3):
                for layer in range(5):
                    row = 16 * at + 4 * layer if layer < 4 else 48 + 4 * at
                    q_ref[5 * at + layer, 4 * group : 4 * group + 4, deep] = lanes[row : row + 4, :]

    def fill(ref, first):
        for at in range(15):
            ref[3 * at : 3 * at + 3, :] = q_ref[at, first : first + 3, :]
        ref[45:48, :] = jnp.zeros((3, 512), jnp.float32)

    by_chord(fill, pair_ref, other_ref, 0, 13)


def by_chord(fill, pair_ref, other_ref, low, high):
    even = lax.axis_index("chord") % 2 == 0

    @pl.when(even)
    def _():
        fill(pair_ref, high)
        fill(other_ref, low)

    @pl.when(jnp.logical_not(even))
    def _():
        fill(pair_ref, low)
        fill(other_ref, high)


def halo_by_chord(take, pair_ref, other_ref):
    even = lax.axis_index("chord") % 2 == 0

    @pl.when(even)
    def _():
        take(pair_ref, other_ref)

    @pl.when(jnp.logical_not(even))
    def _():
        take(other_ref, pair_ref)


SCALE = 0.25 * time_step


def lane_is(at):
    return lax.broadcasted_iota(jnp.int32, (ROWS, 128), 1) == at


def next_row(x):
    return pltpu.roll(x, ROWS - 1, 0)


def row_before(x):
    return pltpu.roll(x, 1, 0)


def strain_parts(load):
    first = lane_is(0)
    held = [0.0] * 3
    for lanes in LANES:
        sums, rows, deeps = [], [], []
        for at in range(3):
            value = load(at, lanes)
            rolled = pltpu.roll(value, 1, 1)
            earlier = jnp.where(first, held[at], rolled)
            held[at] = rolled
            total, change = value + earlier, value - earlier
            behind = row_before(total)
            sums.append(total + behind)
            rows.append(total - behind)
            deeps.append(change + row_before(change))
        yield lanes, (
            sums[0],
            rows[1],
            deeps[2],
            rows[2] + deeps[1],
            deeps[0] + sums[2],
            deeps[0] - sums[2],
            rows[0] + sums[1],
            rows[0] - sums[1],
        )


def strains(now, old):
    return (
        now[0] - old[0],
        now[1] + old[1],
        now[2] + old[2],
        now[3] + old[3],
        now[4] + old[5],
        now[6] + old[7],
    )


def force_parts(load, need=(True, True)):
    last = lane_is(127)
    held = [0.0] * 6
    for lanes in reversed(LANES):
        total, change = [], []
        for at in range(6):
            value = load(at, lanes)
            rolled = pltpu.roll(value, 127, 1)
            later = jnp.where(last, held[at], rolled)
            held[at] = rolled
            total.append(value + later)
            change.append(later - value)
        plus, minus = [], []
        for lead, side, deep in ((0, 5, 4), (5, 1, 3), (4, 3, 2)):
            ahead = total[lead] + next_row(total[lead])
            rest = next_row(total[side] + change[deep]) + (change[deep] - total[side])
            plus.append(rest + ahead if need[0] else None)
            minus.append(rest - ahead if need[1] else None)
        yield lanes, plus, minus


def stress_rates(e, first_bond, second_bond):
    trace = e[0] + e[1] + e[2]
    along = []
    for bond in (first_bond, second_bond):
        part = bond[0] * e[0]
        for at in range(1, 6):
            part = part + bond[at] * e[at]
        along.append(part)
    third = trace - along[0] - along[1]
    first_weight = (SCALE * anisotropy) * (along[0] - third)
    second_weight = (SCALE * anisotropy) * (along[1] - third)
    level = (SCALE * cross_modulus) * trace + (SCALE * anisotropy) * third
    rates = []
    for at in range(6):
        rate = first_bond[at] * first_weight + second_bond[at] * second_weight
        if at < 3:
            rate = rate + ((2.0 * SCALE * shear_modulus) * e[at] + level)
        else:
            rate = rate + (SCALE * shear_modulus) * e[at]
        rates.append(rate)
    return rates


def bonds_of(a, b, c):
    w = jnp.sqrt(jnp.maximum(1.0 - a * a - b * b - c * c, 0.0))
    ab, ac, bc = a * b, a * c, b * c
    wa, wb, wc = w * a, w * b, w * c
    aa, bb, cc = a * a, b * b, c * c
    bonds = []
    for p, q, r in (
        (1.0 - 2.0 * (bb + cc), 2.0 * (ab + wc), 2.0 * (ac - wb)),
        (2.0 * (ab - wc), 1.0 - 2.0 * (aa + cc), 2.0 * (bc + wa)),
    ):
        bonds += [p * p, q * q, r * r, q * r, r * p, p * q]
    return bonds


def outer_scale(outside_low, outside_high):
    row = lax.broadcasted_iota(jnp.int32, (8, 128), 0)
    outside = ((row < DEEP) & outside_high) | ((row >= DEEP) & outside_low)
    return jnp.where(outside, 0.0, 1.0)


def put(ref, lead, lanes, value, outer):
    ref[(*lead, slice(0, 16), lanes)] = value[0:16]
    ref[(*lead, slice(16, ROWS), lanes)] = value[16:ROWS] * outer


def push(low, high, old, new, lead, outer, factor=None):
    for (lanes, _, minus), (_, plus, _) in zip(
        force_parts(low, (False, True)), force_parts(high, (True, False))
    ):
        for at in range(3):
            value = old(at, lanes) + SCALE * (plus[at] + minus[at])
            if factor is not None:
                value = value * factor
            put(new, (at, lead), lanes, value, outer)


def push_two(loads, old, new, outer):
    for (lanes, _, first), (_, second, third), (_, fourth, _) in zip(
        force_parts(loads[0], (False, True)),
        force_parts(loads[1]),
        force_parts(loads[2], (True, False)),
    ):
        for at in range(3):
            put(new, (at, 0), lanes, old(at, 0, lanes) + SCALE * (second[at] + first[at]), outer)
            put(new, (at, 1), lanes, old(at, 1, lanes) + SCALE * (fourth[at] + third[at]), outer)


def strain(e, bonds, old, new, lead, lanes, outer, factor=None):
    for at, rate in enumerate(stress_rates(e, bonds[:6], bonds[6:])):
        if factor is not None:
            rate = rate * factor
        put(new, (at, lead), lanes, old(at) + rate, outer)


def layer_of(ref, x):
    return lambda at, lanes: ref[at, x, :, lanes]


def plane_of(ref, first=0):
    return lambda at, lanes: ref[first + at, :, lanes]


def span_odd():
    return lax.axis_index("span") % 2 == 1


def rows_scale():
    chord = lax.axis_index("chord")
    return outer_scale(False, chord == 7), outer_scale(chord == 0, False)


def edge_kernel(v_ref, s_ref, v_out, s_out, pair_ref, other_ref, v_sem, s_sem):
    take_v = pltpu.make_async_copy(v_ref, v_out.at[:, :, 0:16], v_sem)
    take_s = pltpu.make_async_copy(s_ref, s_out.at[:, :, 0:16], s_sem)
    take_v.start()
    take_s.start()
    take_v.wait()
    take_s.wait()

    def fill(ref, first):
        rows = slice(first, first + DEEP)
        for at in range(9):
            for x in range(4):
                row = 16 * at + 4 * x
                ref[row : row + 4, :] = s_out[at, x, rows] if at < 6 else v_out[at - 6, x, rows]

    by_chord(fill, pair_ref, other_ref, 0, 16 - DEEP)


def spot(sources_ref, at):
    layer = sources_ref[at, 0].astype(jnp.int32) - 4 * lax.axis_index("span")
    chord = sources_ref[at, 1].astype(jnp.int32) - 16 * lax.axis_index("chord")
    return layer, chord, sources_ref[at, 2].astype(jnp.int32)


def add_at(ref, lead, chord, deep, amount):
    row = jnp.where(chord < 0, chord + ROWS, chord)
    rows = pl.ds(pl.multiple_of((row // 8) * 8, 8), 8)
    lanes = pl.ds(pl.multiple_of((deep // 128) * 128, 128), 128)
    hit = (lax.broadcasted_iota(jnp.int32, (8, 128), 0) == row % 8) & (
        lax.broadcasted_iota(jnp.int32, (8, 128), 1) == deep % 128
    )
    ref[(*lead, rows, lanes)] = ref[(*lead, rows, lanes)] + jnp.where(hit, amount, 0.0)


def before_span_kernel(
    sources_ref, v_ref, s_ref, pair_ref, other_ref, v_out, s_out, chip_ref, far_ref
):
    def take(next_ref, prior_ref):
        for at in range(9):
            out, slot = (s_out, at) if at < 6 else (v_out, at - 6)
            for x in range(4):
                row = 16 * at + 4 * x
                out[slot, x, 16 : 16 + DEEP] = next_ref[row : row + 4, :]
                out[slot, x, 16 + DEEP : ROWS] = prior_ref[row : row + 4, :]

    halo_by_chord(take, pair_ref, other_ref)
    outer = rows_scale()[1]
    for x in range(3):
        push(layer_of(s_out, x), layer_of(s_out, x + 1), layer_of(v_out, x), v_out, x, outer)
    for at in range(16):
        layer, chord, deep = spot(sources_ref, at)

        @pl.when((layer >= 0) & (layer < 3) & (chord >= -DEEP) & (chord < 16 + DEEP))
        def _():
            add_at(v_out, (2, layer), chord, deep, sources_ref[at, 3])

    def fill(low_ref, high_ref):
        for at in range(6):
            low_ref[at] = s_out[at, 0]
            high_ref[at] = s_out[at, 3]
        for at in range(3):
            low_ref[6 + at] = v_out[at, 0]
            high_ref[6 + at] = v_out[at, 3]

    odd = span_odd()

    @pl.when(odd)
    def _():
        fill(chip_ref, far_ref)

    @pl.when(jnp.logical_not(odd))
    def _():
        fill(far_ref, chip_ref)


def after_span_kernel(
    sources_ref, v_ref, s_ref, chip_ref, far_ref, v_out, e_out, s_end_ref, added_ref,
    side_ref, left_ref, right_ref,
):
    for at in range(14):
        added_ref[at] = jnp.zeros((ROWS, 512), jnp.float32)
    for at in range(16):
        layer, chord, deep = spot(sources_ref, at)
        inside = (chord >= -DEEP) & (chord < 16 + DEEP)

        @pl.when(inside & ((layer == -1) | (layer == 3)))
        def _():
            add_at(added_ref, (jnp.where(layer == 3, 1, 0),), chord, deep, sources_ref[at, 3])

        @pl.when(inside & (layer >= 0) & (layer < 4))
        def _():
            for step_at in range(1, 4):
                slot = 4 * step_at - 2 + layer
                add_at(added_ref, (slot,), chord, deep, sources_ref[at, 3 + step_at])

    def split(low_ref, high_ref):
        left_ref[...] = low_ref[...]
        right_ref[...] = high_ref[...]

    odd = span_odd()

    @pl.when(odd)
    def _():
        split(chip_ref, far_ref)

    @pl.when(jnp.logical_not(odd))
    def _():
        split(far_ref, chip_ref)

    outer = rows_scale()[1]
    inside = jnp.where(lax.axis_index("span") == 0, 0.0, 1.0)
    before = with_source(plane_of(left_ref, 6), added_ref, 0)
    push(plane_of(left_ref), layer_of(s_ref, 0), before, side_ref, 0, outer, inside)
    own = with_source(layer_of(v_ref, 3), added_ref, 1)
    push(layer_of(s_ref, 3), plane_of(right_ref), own, side_ref, 1, outer)
    for at in range(6):
        s_end_ref[at] = right_ref[at]
    for at in range(3):
        v_out[at, 0:3] = v_ref[at, 0:3]
        v_out[at, 3] = side_ref[at, 1]
    streams = [strain_parts(layer_of(side_ref, 0))]
    streams += [strain_parts(layer_of(v_out, x)) for x in range(4)]
    streams += [strain_parts(plane_of(right_ref, 6))]
    for layers in zip(*streams):
        lanes = layers[0][0]
        for x in range(5):
            for at, value in enumerate(strains(layers[x + 1][1], layers[x][1])):
                e_out[at, x, :, lanes] = value


def with_source(load, added_ref, slot):
    def both(at, lanes):
        value = load(at, lanes)
        return value + added_ref[slot, :, lanes] if at == 2 else value

    return both


def slot_of(step_at, layer):
    return 4 * step_at - 2 + layer


def out_by_core(ends_ref, chip_ref, far_ref):
    odd = span_odd()
    for at in range(3):
        chip_ref[at] = jnp.where(odd, ends_ref[at, 0], ends_ref[at, 1])
        far_ref[at] = jnp.where(odd, ends_ref[at, 1], ends_ref[at, 0])


def first_stress(x, slot, rows, lanes, q, e_ref, s_ref, s_end_ref, s_out, b_out):
    bonds = bonds_of(*q)
    for at, value in enumerate(bonds):
        b_out[at, slot, rows, lanes] = value
    e = [e_ref[at, x, rows, lanes] for at in range(6)]
    rates = stress_rates(e, bonds[:6], bonds[6:])
    if x == 4:
        edge = jnp.where(lax.axis_index("span") == 15, 0.0, 1.0)
        rates = [rate * edge for rate in rates]
    return [
        (s_ref[at, x, rows, lanes] if x < 4 else s_end_ref[at, rows, lanes]) + rates[at]
        for at in range(6)
    ]


ENDS = (0, 1, 3, 4)


def first_own_kernel(e_ref, s_ref, s_end_ref, q_ref, s_out, b_out):
    for lanes in LANES:
        for slot, x in enumerate(ENDS):
            for rows in (slice(0, 8), slice(8, 16)):
                q = [q_ref[5 * at + x, rows, lanes] for at in range(3)]
                new = first_stress(x, slot, rows, lanes, q, e_ref, s_ref, s_end_ref, s_out, b_out)
                for at in range(6):
                    s_out[at, slot, rows, lanes] = new[at]


def first_end_kernel(
    s_held, b_held, v_ref, e_ref, s_ref, s_end_ref, pair_ref, other_ref, added_ref,
    s_out, b_out, q_out, chip_ref, far_ref, halo_ref, ends_ref,
):
    halo_ref[...] = jnp.zeros(halo_ref.shape, jnp.float32)

    def take(next_ref, prior_ref):
        for at in range(15):
            halo_ref[at, 0:3] = next_ref[3 * at : 3 * at + 3]
            halo_ref[at, 5:8] = prior_ref[3 * at : 3 * at + 3]

    halo_by_chord(take, pair_ref, other_ref)
    outer_s, outer_v = rows_scale()
    rows = slice(16, ROWS)
    for at in range(3):
        q_out[at] = halo_ref[5 * at + 2]
    for lanes in LANES:
        for slot, x in enumerate(ENDS):
            q = [halo_ref[5 * at + x, :, lanes] for at in range(3)]
            new = first_stress(x, slot, rows, lanes, q, e_ref, s_ref, s_end_ref, s_out, b_out)
            for at in range(6):
                s_out[at, slot, rows, lanes] = new[at] * outer_s
    low = with_source(layer_of(v_ref, 0), added_ref, slot_of(1, 0))
    high = with_source(layer_of(v_ref, 3), added_ref, slot_of(1, 3))
    push(layer_of(s_out, 0), layer_of(s_out, 1), low, ends_ref, 0, outer_v)
    push(layer_of(s_out, 2), layer_of(s_out, 3), high, ends_ref, 1, outer_v)
    out_by_core(ends_ref, chip_ref, far_ref)


def middle(v_layers, s_old, bond_of, s_out, outer):
    for layers in zip(*[strain_parts(load) for load in v_layers]):
        lanes = layers[0][0]
        for x in range(3):
            e = strains(layers[x + 1][1], layers[x][1])
            strain(e, bond_of(x, lanes), lambda at: s_old(at, x, lanes), s_out, x, lanes, outer)


def end_layers(chip_ref, far_ref):
    odd = span_odd()
    low = lambda at, lanes: jnp.where(odd, chip_ref[at, :, lanes], far_ref[at, :, lanes])
    high = lambda at, lanes: jnp.where(odd, far_ref[at, :, lanes], chip_ref[at, :, lanes])
    return low, high


def first_middle_kernel(
    v_ref, e_ref, s_ref, ends_ref, b_ref, q_ref, halo_ref, chip_ref, far_ref, added_ref,
    v_out, s_out, b_out, stress_ref, mid_ref,
):
    outer_s, outer_v = rows_scale()
    for lanes in LANES:
        for rows in (slice(0, 8), slice(8, 16), slice(16, ROWS)):
            own = rows.start < 16
            q = [q_ref[5 * at + 2, rows, lanes] if own else halo_ref[at, :, lanes] for at in range(3)]
            new = first_stress(2, 0, rows, lanes, q, e_ref, s_ref, None, stress_ref, b_out)
            for at in range(6):
                stress_ref[at, 0, rows, lanes] = new[at] if own else new[at] * outer_s

    def push_middle(loads, old, new, step_at):
        def moved(at, x, lanes):
            value = old(at, x, lanes)
            return value + added_ref[slot_of(step_at, 1 + x), :, lanes] if at == 2 else value

        push_two(loads, moved, new, outer_v)

    loads = [layer_of(ends_ref, 1), layer_of(stress_ref, 0), layer_of(ends_ref, 2)]
    push_middle(loads, lambda at, x, lanes: v_ref[at, 1 + x, :, lanes], mid_ref, 1)
    low, high = end_layers(chip_ref, far_ref)

    def s_old(at, x, lanes):
        return stress_ref[at, 0, :, lanes] if x == 1 else ends_ref[at, 1 + x // 2, :, lanes]

    def bond_of(x, lanes):
        return [
            b_out[at, 0, :, lanes] if x == 1 else b_ref[at, 1 + x // 2, :, lanes] for at in range(12)
        ]

    middle([low, layer_of(mid_ref, 0), layer_of(mid_ref, 1), high], s_old, bond_of, s_out, outer_s)
    loads = [layer_of(s_out, x) for x in range(3)]
    push_middle(loads, lambda at, x, lanes: mid_ref[at, x, :, lanes], v_out, 2)


def middle_kernel(v_ref, s_ref, b_ref, b_mid_ref, chip_ref, far_ref, added_ref, v_out, s_out):
    outer_s, outer_v = rows_scale()
    low, high = end_layers(chip_ref, far_ref)

    def bond_of(x, lanes):
        return [
            b_mid_ref[at, 0, :, lanes] if x == 1 else b_ref[at, 1 + x // 2, :, lanes]
            for at in range(12)
        ]

    s_old = lambda at, x, lanes: s_ref[at, x, :, lanes]
    middle([low, layer_of(v_ref, 0), layer_of(v_ref, 1), high], s_old, bond_of, s_out, outer_s)
    loads = [layer_of(s_out, x) for x in range(3)]

    def moved(at, x, lanes):
        value = v_ref[at, x, :, lanes]
        return value + added_ref[slot_of(3, 1 + x), :, lanes] if at == 2 else value

    push_two(loads, moved, v_out, outer_v)


def end_kernel(
    step_at, s_ends_ref, s_mid_ref, b_ref, chip_ref, far_ref, got_chip_ref, got_far_ref, added_ref,
    s_out, first_ref, second_ref, ends_ref,
):
    outer_s, outer_v = rows_scale()
    edge = jnp.where(lax.axis_index("span") == 15, 0.0, 1.0)
    low, high = end_layers(chip_ref, far_ref)
    before, after = end_layers(got_chip_ref, got_far_ref)
    count = s_ends_ref.shape[1]
    for parts in zip(*[strain_parts(load) for load in (before, low, high, after)]):
        lanes = parts[0][0]
        for slot, old, now in ((0, parts[0][1], parts[1][1]), (1, parts[2][1], parts[3][1])):
            bonds = [b_ref[at, 3 * slot, :, lanes] for at in range(12)]
            s_old = lambda at: s_ends_ref[at, slot * (count - 1), :, lanes]
            strain(strains(now, old), bonds, s_old, s_out, slot, lanes, outer_s, edge if slot else None)
    low = with_source(low, added_ref, slot_of(step_at, 0))
    high = with_source(high, added_ref, slot_of(step_at, 3))
    push(layer_of(s_out, 0), layer_of(s_mid_ref, 0), low, ends_ref, 0, outer_v)
    push(layer_of(s_mid_ref, 2), layer_of(s_out, 1), high, ends_ref, 1, outer_v)
    if step_at < 3:
        out_by_core(ends_ref, first_ref, second_ref)
    else:
        for at in range(3):
            first_ref[at] = ends_ref[at, 0]
            second_ref[at] = ends_ref[at, 1]


def last_middle_kernel(v_ref, s_ref, b_ref, b_mid_ref, low_ref, high_ref, v_out, s_out):
    layers = [plane_of(low_ref), layer_of(v_ref, 0), layer_of(v_ref, 1), plane_of(high_ref)]
    for parts in zip(*[strain_parts(load) for load in layers]):
        lanes = parts[0][0]
        for x in range(4):
            for at in range(3):
                v_out[at, x, :, lanes] = layers[x](at, lanes)[0:16]
        for x in range(3):
            e = [value[0:16] for value in strains(parts[x + 1][1], parts[x][1])]
            bonds = [
                b_mid_ref[at, 0, 0:16, lanes] if x == 1 else b_ref[at, 1 + x // 2, 0:16, lanes]
                for at in range(12)
            ]
            for at, rate in enumerate(stress_rates(e, bonds[:6], bonds[6:])):
                s_out[at, 1 + x, :, lanes] = s_ref[at, x, 0:16, lanes] + rate


def last_end_kernel(held_ref, s_ref, b_ref, low_ref, before_ref, out_ref, end_ref, sem):
    for (lanes, old), (_, now) in zip(strain_parts(plane_of(before_ref)), strain_parts(plane_of(low_ref))):
        e = [value[0:16] for value in strains(now, old)]
        bonds = [b_ref[at, 0, 0:16, lanes] for at in range(12)]
        for at, rate in enumerate(stress_rates(e, bonds[:6], bonds[6:])):
            end_ref[at, :, lanes] = s_ref[at, 0, 0:16, lanes] + rate
    copy = pltpu.make_async_copy(end_ref, out_ref.at[:, 0], sem)
    copy.start()
    copy.wait()


def shift(x, axis, by):
    peers = lax.axis_size(axis)
    pairs = [(i, i + by) for i in range(peers) if 0 <= i + by < peers]
    return lax.ppermute(x, axis, pairs)


def swap(x, axis, first):
    peers = lax.axis_size(axis)
    pairs = []
    for i in range(first, peers - 1, 2):
        pairs += [(i, i + 1), (i + 1, i)]
    return lax.ppermute(x, axis, pairs)


def swaps(pair, other, axis):
    return swap(pair, axis, 0), swap(other, axis, 1)


def shards(
    velocity, stress, grain_ids, lattice_tilt, grain_orient, orientations, source_cells, source_signal
):
    plane = (ROWS, 512)
    edge, ends = (3, *plane), (3, 2, *plane)
    sources = jnp.concatenate((source_cells.astype(jnp.float32), source_signal), axis=1)
    (sent,) = call(
        rotation_kernel,
        [(16, 64, 128)],
        (
            jnp.transpose(grain_ids, (1, 2, 0)),
            jnp.transpose(lattice_tilt, (0, 2, 3, 1)),
            grain_orient.reshape(32, 128),
            orientations.reshape(3, 4, 128),
        ),
        scratch=[(3, 272, 128)],
        flops=32768 * 200,
    )
    velocity, stress, sent = lax.optimization_barrier((velocity, stress, sent))
    got = lax.all_to_all(sent, "span", 0, 0, tiled=True)

    v, s, pair, other = call(
        edge_kernel,
        [(3, 4, *plane), (6, 4, *plane), (144, 512), (144, 512)],
        (velocity, stress),
        scratch=[pltpu.SemaphoreType.DMA, pltpu.SemaphoreType.DMA],
        spaces={0: pl.ANY, 1: pl.ANY},
    )
    pair, other = swaps(pair, other, "chord")
    v, s, chip, far = call(
        before_span_kernel,
        [(3, 4, *plane), (6, 4, *plane), (9, *plane), (9, *plane)],
        (sources, v, s, pair, other),
        spaces={0: pltpu.SMEM},
        aliases={1: 0, 2: 1},
    )
    chip, far = swaps(chip, far, "span")

    q, pair, other = call(arrange_kernel, [(15, 16, 512), (48, 512), (48, 512)], (got,))
    pair, other = swaps(pair, other, "chord")

    v, e, s_end, added = call(
        after_span_kernel,
        [(3, 4, *plane), (6, 5, *plane), (6, *plane), (14, *plane)],
        (sources, v, s, chip, far),
        scratch=[ends, (9, *plane), (9, *plane)],
        spaces={0: pltpu.SMEM},
    )
    s_ends, bonds = call(
        first_own_kernel, [(6, 4, *plane), (12, 4, *plane)], (e, s, s_end, q), flops=32768 * 100
    )
    s_ends, bonds, halo, chip, far = call(
        first_end_kernel,
        [(6, 4, *plane), (12, 4, *plane), (3, 8, 512), edge, edge],
        (s_ends, bonds, v, e, s, s_end, pair, other, added),
        scratch=[(15, 8, 512), ends],
        aliases={0: 0, 1: 1},
    )
    got_chip, got_far = swaps(chip, far, "span")
    v, s, mid_bonds = call(
        first_middle_kernel,
        [ends, (6, 3, *plane), (12, 1, *plane)],
        (v, e, s, s_ends, bonds, q, halo, chip, far, added),
        scratch=[(6, 1, *plane), ends],
        flops=32768 * 100,
    )
    s_ends, chip, far = call(
        lambda *refs: end_kernel(2, *refs),
        [(6, 2, *plane), edge, edge],
        (s_ends, s, bonds, chip, far, got_chip, got_far, added),
        scratch=[ends],
    )
    got_chip, got_far = swaps(chip, far, "span")
    v, s = call(
        middle_kernel,
        [ends, (6, 3, *plane)],
        (v, s, bonds, mid_bonds, chip, far, added),
        flops=32768 * 100,
    )
    s_ends, low, high = call(
        lambda *refs: end_kernel(3, *refs),
        [(6, 2, *plane), edge, edge],
        (s_ends, s, bonds, chip, far, got_chip, got_far, added),
        scratch=[ends],
    )
    before = shift(high, "span", 1)
    v, s = call(
        last_middle_kernel,
        [velocity.shape, stress.shape],
        (v, s, bonds, mid_bonds, low, high),
        flops=32768 * 100,
    )
    s = pl.pallas_call(
        last_end_kernel,
        out_shape=jax.ShapeDtypeStruct(stress.shape, jnp.float32),
        in_specs=[pl.BlockSpec(memory_space=pl.ANY)] + [WHOLE] * 4,
        out_specs=pl.BlockSpec(memory_space=pl.ANY),
        scratch_shapes=[pltpu.VMEM((6, 16, 512), jnp.float32), pltpu.SemaphoreType.DMA],
        input_output_aliases={0: 0},
        compiler_params=VMEM,
    )(s, s_ends, bonds, low, before)
    return v, s


def solution(mesh):
    return jax.shard_map(
        shards,
        mesh=mesh,
        in_specs=(
            P(None, "span", "chord", None),
            P(None, "span", "chord", None),
            P(None, "chord", "span"),
            P(None, None, "chord", "span"),
            P(),
            P(),
            P(),
            P(),
        ),
        out_specs=(P(None, "span", "chord", None), P(None, "span", "chord", None)),
        check_vma=False,
    )
```

```python
import jax
import jax.numpy as jnp
from jax import lax
from jax.experimental import pallas as pl
from jax.experimental.pallas import tpu as pltpu
from jax.sharding import PartitionSpec as P

normal_modulus = 0.9
cross_modulus = 1.6
shear_modulus = 1.3
time_step = 0.25
anisotropy = normal_modulus - 2.0 * shear_modulus

DEEP = 4
ROWS = 24
TABLE_ROWS = 11
VMEM = pltpu.CompilerParams(vmem_limit_bytes=16 * 2**20)
WHOLE = pl.BlockSpec(memory_space=pltpu.VMEM)
LANES = [slice(128 * at, 128 * at + 128) for at in range(4)]


def call(kernel, outs, operands, scratch=(), spaces=(), aliases=None, flops=0):
    spaces = dict(spaces)
    return pl.pallas_call(
        kernel,
        out_shape=[jax.ShapeDtypeStruct(shape, jnp.float32) for shape in outs],
        in_specs=[pl.BlockSpec(memory_space=spaces.get(at, pltpu.VMEM)) for at in range(len(operands))],
        out_specs=[WHOLE] * len(outs),
        scratch_shapes=[
            pltpu.VMEM(shape, jnp.float32) if isinstance(shape, tuple) else shape for shape in scratch
        ],
        input_output_aliases=aliases or {},
        compiler_params=VMEM,
        cost_estimate=pl.CostEstimate(
            flops=flops,
            bytes_accessed=4 * sum(operand.size for operand in operands),
            transcendentals=0,
        ),
    )(*operands)


def small_sin(x):
    y = x * x
    return x * (
        1.0 + y * (-1.0 / 6 + y * (1.0 / 120 + y * (-1.0 / 5040 + y * (1.0 / 362880))))
    )


def small_cos(x):
    y = x * x
    return 1.0 + y * (
        -0.5
        + y * (1.0 / 24 + y * (-1.0 / 720 + y * (1.0 / 40320 + y * (-1.0 / 3628800))))
    )


def wide_sin_cos(x):
    quarter = 0.25 * x
    s, c = small_sin(quarter), small_cos(quarter)
    s, c = 2.0 * s * c, 1.0 - 2.0 * s * s
    return 2.0 * s * c, 1.0 - 2.0 * s * s


def quaternion(first, middle, last, sin_cos):
    s_mid, c_mid = sin_cos(0.5 * middle)
    s_sum, c_sum = sin_cos(0.5 * (first + last))
    s_dif, c_dif = sin_cos(0.5 * (first - last))
    return c_mid * c_sum, -s_mid * c_dif, -s_mid * s_dif, -c_mid * s_sum


def product(a, b):
    return (
        a[0] * b[0] - a[1] * b[1] - a[2] * b[2] - a[3] * b[3],
        a[0] * b[1] + a[1] * b[0] + a[2] * b[3] - a[3] * b[2],
        a[0] * b[2] - a[1] * b[3] + a[2] * b[0] + a[3] * b[1],
        a[0] * b[3] + a[1] * b[2] - a[2] * b[1] + a[3] * b[0],
    )


def reduced(q):
    w, x, y, z = q
    aw, ax, ay, az = jnp.abs(w), jnp.abs(x), jnp.abs(y), jnp.abs(z)
    low, high = jnp.maximum(aw, ax), jnp.maximum(ay, az)
    upper = high > low
    second = jnp.where(upper, az - ay, ax - aw) > 0.0

    def pick(a, b, c, d):
        return jnp.where(upper, jnp.where(second, d, c), jnp.where(second, b, a))

    lead = pick(w, x, y, z)
    flip = jnp.where(lead < 0.0, -1.0, 1.0)
    return (
        pick(x, -w, z, -y) * flip,
        pick(y, -z, -w, x) * flip,
        pick(z, y, -x, -w) * flip,
    )


def look_up(row, lane):
    return jnp.take_along_axis(
        jnp.broadcast_to(row, lane.shape), lane, axis=1, mode="promise_in_bounds"
    )


LEVEL = 1 << 19
FINE = 0.75 / LEVEL


def coded(q):
    w, x, y, z = q
    aw, ax, ay, az = jnp.abs(w), jnp.abs(x), jnp.abs(y), jnp.abs(z)
    upper = jnp.maximum(ay, az) > jnp.maximum(aw, ax)
    second = jnp.where(upper, az - ay, ax - aw) > 0.0

    def pick(a, b, c, d):
        return jnp.where(upper, jnp.where(second, d, c), jnp.where(second, b, a))

    flip = jnp.where(pick(w, x, y, z) < 0.0, -1.0 / FINE, 1.0 / FINE)
    rest = (pick(x, w, w, w), pick(y, y, x, x), pick(z, z, z, y))
    a, b, c = [jnp.round(part * flip).astype(jnp.int32) + LEVEL for part in rest]
    return (
        a + ((b & 1023) << 20) + jnp.where(second, 1 << 30, 0),
        c + ((b >> 10) << 20) + jnp.where(upper, 1 << 30, 0),
    )


def decoded(one, two):
    mask = (1 << 20) - 1
    a = one & mask
    b = ((one >> 20) & 1023) | (((two >> 20) & 1023) << 10)
    c = two & mask
    a, b, c = [(part - LEVEL).astype(jnp.float32) * FINE for part in (a, b, c)]
    lead = jnp.sqrt(1.0 - a * a - b * b - c * c)
    second, upper = (one >> 30) > 0, (two >> 30) > 0

    def pick(w, x, y, z):
        return jnp.where(upper, jnp.where(second, z, y), jnp.where(second, x, w))

    return pick(lead, a, a, a), pick(a, lead, b, b), pick(b, b, lead, c), pick(c, c, c, lead)


def turned_parts(grain, angles, grain_ref, angle_ref):
    packed = []
    for at in range(TABLE_ROWS):
        row = grain_ref[at : at + 1, :] + grain_ref[at + 11 : at + 12, :] * 512
        if at + 22 < 32:
            row = row + grain_ref[at + 22 : at + 23, :] * (512 * 512)
        packed.append(row)
    table = coded(quaternion(*[angle_ref[at : at + 1, :] for at in range(3)], wide_sin_cos))
    third = jnp.where(grain >= 2816, 2, jnp.where(grain >= 1408, 1, 0))
    grain = grain - 1408 * third
    lane, place = grain & 127, grain >> 7
    entry = look_up(packed[0], lane)
    for at in range(1, TABLE_ROWS):
        entry = jnp.where(place == at, look_up(packed[at], lane), entry)
    entry = (entry >> (9 * third)) & 511
    lane, place = entry & 127, entry >> 7
    found = []
    for code in table:
        part = [code[:, lanes] for lanes in LANES]
        low = jnp.where(place == 1, look_up(part[1], lane), look_up(part[0], lane))
        high = jnp.where(place == 3, look_up(part[3], lane), look_up(part[2], lane))
        found.append(jnp.where(place >= 2, high, low))
    tilt_turn = quaternion(*angles, lambda x: (small_sin(x), small_cos(x)))
    return reduced(product(decoded(*found), tilt_turn))


def side_by_side(ref, *lead):
    *lead, chord = lead
    return jnp.concatenate([ref[(*lead, chord)], ref[(*lead, chord + 1)]], axis=1)


def rotation_kernel(ids_ref, tilt_ref, grain_ref, angle_ref, out_ref, sorted_ref):
    for pair in range(2):
        chords = [4 * group + 2 * pair for group in range(4)]

        def stacked(ref, *lead):
            return jnp.concatenate([side_by_side(ref, *lead, chord) for chord in chords], axis=0)

        values = turned_parts(
            stacked(ids_ref), [stacked(tilt_ref, at) for at in range(3)], grain_ref, angle_ref
        )
        for at in range(3):
            turned = values[at].T
            for half in range(2):
                sorted_ref[at, pl.ds(2 * pair + half, 64, stride=4), :] = turned[
                    64 * half : 64 * half + 64, :
                ]
    for at in range(3):
        sorted_ref[at, 256:272, :] = jnp.zeros((16, 128), jnp.float32)
    for device in range(16):
        for at in range(3):
            row = 16 * device
            out_ref[device, 16 * at : 16 * at + 16, :] = sorted_ref[at, row : row + 16, :]
            out_ref[device, 48 + 4 * at : 52 + 4 * at, :] = sorted_ref[at, row + 16 : row + 20, :]


def depth_parts(got_ref):
    for four, deep in enumerate(LANES):
        pieces = [got_ref[4 * four + at] for at in range(4)]

        def lanes_of(group):
            return jnp.concatenate(
                [piece[:, 32 * group : 32 * group + 32] for piece in pieces], axis=1
            )

        yield deep, lanes_of


def row_of(at, layer):
    return 16 * at + 4 * layer if layer < 4 else 48 + 4 * at


def arrange_edge_kernel(got_ref, pair_ref, other_ref):
    def fill(ref, group, first):
        for deep, lanes_of in depth_parts(got_ref):
            lanes = lanes_of(group)
            for at in range(3):
                for layer in range(5):
                    slot, row = 15 * at + 3 * layer, row_of(at, layer) + first
                    ref[slot : slot + 3, deep] = lanes[row : row + 3, :]
        ref[45:48, :] = jnp.zeros((3, 512), jnp.float32)

    by_chord(lambda ref, low: fill(ref, *low), pair_ref, other_ref, (0, 0), (3, 1))


def arrange_kernel(got_ref, q_ref):
    for deep, lanes_of in depth_parts(got_ref):
        for group in range(4):
            lanes = lanes_of(group)
            for at in range(3):
                for layer in range(5):
                    row = row_of(at, layer)
                    q_ref[5 * at + layer, 4 * group : 4 * group + 4, deep] = lanes[row : row + 4, :]


def by_chord(fill, pair_ref, other_ref, low, high):
    even = lax.axis_index("chord") % 2 == 0

    @pl.when(even)
    def _():
        fill(pair_ref, high)
        fill(other_ref, low)

    @pl.when(jnp.logical_not(even))
    def _():
        fill(pair_ref, low)
        fill(other_ref, high)


def halo_by_chord(take, pair_ref, other_ref):
    even = lax.axis_index("chord") % 2 == 0

    @pl.when(even)
    def _():
        take(pair_ref, other_ref)

    @pl.when(jnp.logical_not(even))
    def _():
        take(other_ref, pair_ref)


SCALE = 0.25 * time_step


def lane_is(at):
    return lax.broadcasted_iota(jnp.int32, (ROWS, 128), 1) == at


def next_row(x):
    return pltpu.roll(x, ROWS - 1, 0)


def row_before(x):
    return pltpu.roll(x, 1, 0)


def strain_parts(load):
    first = lane_is(0)
    held = [0.0] * 3
    for lanes in LANES:
        sums, rows, deeps = [], [], []
        for at in range(3):
            value = load(at, lanes)
            rolled = pltpu.roll(value, 1, 1)
            earlier = jnp.where(first, held[at], rolled)
            held[at] = rolled
            total, change = value + earlier, value - earlier
            behind = row_before(total)
            sums.append(total + behind)
            rows.append(total - behind)
            deeps.append(change + row_before(change))
        yield lanes, (
            sums[0],
            rows[1],
            deeps[2],
            rows[2] + deeps[1],
            deeps[0] + sums[2],
            deeps[0] - sums[2],
            rows[0] + sums[1],
            rows[0] - sums[1],
        )


def strains(now, old):
    return (
        now[0] - old[0],
        now[1] + old[1],
        now[2] + old[2],
        now[3] + old[3],
        now[4] + old[5],
        now[6] + old[7],
    )


def force_parts(load, need=(True, True)):
    last = lane_is(127)
    held = [0.0] * 6
    for lanes in reversed(LANES):
        total, change = [], []
        for at in range(6):
            value = load(at, lanes)
            rolled = pltpu.roll(value, 127, 1)
            later = jnp.where(last, held[at], rolled)
            held[at] = rolled
            total.append(value + later)
            change.append(later - value)
        plus, minus = [], []
        for lead, side, deep in ((0, 5, 4), (5, 1, 3), (4, 3, 2)):
            ahead = total[lead] + next_row(total[lead])
            rest = next_row(total[side] + change[deep]) + (change[deep] - total[side])
            plus.append(rest + ahead if need[0] else None)
            minus.append(rest - ahead if need[1] else None)
        yield lanes, plus, minus


def stress_rates(e, first_bond, second_bond):
    trace = e[0] + e[1] + e[2]
    along = []
    for bond in (first_bond, second_bond):
        part = bond[0] * e[0]
        for at in range(1, 6):
            part = part + bond[at] * e[at]
        along.append(part)
    third = trace - along[0] - along[1]
    first_weight = (SCALE * anisotropy) * (along[0] - third)
    second_weight = (SCALE * anisotropy) * (along[1] - third)
    level = (SCALE * cross_modulus) * trace + (SCALE * anisotropy) * third
    rates = []
    for at in range(6):
        rate = first_bond[at] * first_weight + second_bond[at] * second_weight
        if at < 3:
            rate = rate + ((2.0 * SCALE * shear_modulus) * e[at] + level)
        else:
            rate = rate + (SCALE * shear_modulus) * e[at]
        rates.append(rate)
    return rates


def bonds_of(a, b, c):
    w = jnp.sqrt(jnp.maximum(1.0 - a * a - b * b - c * c, 0.0))
    ab, ac, bc = a * b, a * c, b * c
    wa, wb, wc = w * a, w * b, w * c
    aa, bb, cc = a * a, b * b, c * c
    bonds = []
    for p, q, r in (
        (1.0 - 2.0 * (bb + cc), 2.0 * (ab + wc), 2.0 * (ac - wb)),
        (2.0 * (ab - wc), 1.0 - 2.0 * (aa + cc), 2.0 * (bc + wa)),
    ):
        bonds += [p * p, q * q, r * r, q * r, r * p, p * q]
    return bonds


def outer_scale(outside_low, outside_high):
    row = lax.broadcasted_iota(jnp.int32, (8, 128), 0)
    outside = ((row < DEEP) & outside_high) | ((row >= DEEP) & outside_low)
    return jnp.where(outside, 0.0, 1.0)


def put(ref, lead, lanes, value, outer):
    ref[(*lead, slice(0, 16), lanes)] = value[0:16]
    ref[(*lead, slice(16, ROWS), lanes)] = value[16:ROWS] * outer


def push(low, high, old, new, lead, outer, factor=None):
    for (lanes, _, minus), (_, plus, _) in zip(
        force_parts(low, (False, True)), force_parts(high, (True, False))
    ):
        for at in range(3):
            value = old(at, lanes) + SCALE * (plus[at] + minus[at])
            if factor is not None:
                value = value * factor
            put(new, (at, lead), lanes, value, outer)


def push_two(loads, old, new, outer):
    for (lanes, _, first), (_, second, third), (_, fourth, _) in zip(
        force_parts(loads[0], (False, True)),
        force_parts(loads[1]),
        force_parts(loads[2], (True, False)),
    ):
        for at in range(3):
            put(new, (at, 0), lanes, old(at, 0, lanes) + SCALE * (second[at] + first[at]), outer)
            put(new, (at, 1), lanes, old(at, 1, lanes) + SCALE * (fourth[at] + third[at]), outer)


def strain(e, bonds, old, new, lead, lanes, outer, factor=None):
    for at, rate in enumerate(stress_rates(e, bonds[:6], bonds[6:])):
        if factor is not None:
            rate = rate * factor
        put(new, (at, lead), lanes, old(at) + rate, outer)


def layer_of(ref, x):
    return lambda at, lanes: ref[at, x, :, lanes]


def plane_of(ref, first=0):
    return lambda at, lanes: ref[first + at, :, lanes]


def span_odd():
    return lax.axis_index("span") % 2 == 1


def rows_scale():
    chord = lax.axis_index("chord")
    return outer_scale(False, chord == 7), outer_scale(chord == 0, False)


def edge_kernel(v_ref, s_ref, v_out, s_out, pair_ref, other_ref, sems):
    copies = [
        pltpu.make_async_copy(s_ref.at[at], s_out.at[at, :, 0:16], sems.at[at]) for at in range(6)
    ]
    copies += [
        pltpu.make_async_copy(v_ref.at[at], v_out.at[at, :, 0:16], sems.at[6 + at])
        for at in range(3)
    ]
    for copy in copies:
        copy.start()
    for copy in copies:
        copy.wait()

    def fill(ref, first):
        rows = slice(first, first + DEEP)
        for at in range(9):
            for x in range(4):
                row = 16 * at + 4 * x
                ref[row : row + 4, :] = s_out[at, x, rows] if at < 6 else v_out[at - 6, x, rows]

    by_chord(fill, pair_ref, other_ref, 0, 16 - DEEP)


def spot(sources_ref, at):
    layer = sources_ref[at, 0].astype(jnp.int32) - 4 * lax.axis_index("span")
    chord = sources_ref[at, 1].astype(jnp.int32) - 16 * lax.axis_index("chord")
    return layer, chord, sources_ref[at, 2].astype(jnp.int32)


def add_at(ref, lead, chord, deep, amount):
    row = jnp.where(chord < 0, chord + ROWS, chord)
    rows = pl.ds(pl.multiple_of((row // 8) * 8, 8), 8)
    lanes = pl.ds(pl.multiple_of((deep // 128) * 128, 128), 128)
    hit = (lax.broadcasted_iota(jnp.int32, (8, 128), 0) == row % 8) & (
        lax.broadcasted_iota(jnp.int32, (8, 128), 1) == deep % 128
    )
    ref[(*lead, rows, lanes)] = ref[(*lead, rows, lanes)] + jnp.where(hit, amount, 0.0)


def push_half(high, old, new, lead, outer, factor=None):
    for lanes, plus, _ in force_parts(high, (True, False)):
        for at in range(3):
            value = old(at, lanes) + SCALE * plus[at]
            if factor is not None:
                value = value * factor
            put(new, (*lead(at),), lanes, value, outer)


def before_span_kernel(v_ref, s_ref, pair_ref, other_ref, v_out, s_out, chip_ref, low_ref, high_ref):
    def take(next_ref, prior_ref):
        for at in range(9):
            out, slot = (s_out, at) if at < 6 else (v_out, at - 6)
            for x in range(4):
                row = 16 * at + 4 * x
                out[slot, x, 16 : 16 + DEEP] = next_ref[row : row + 4, :]
                out[slot, x, 16 + DEEP : ROWS] = prior_ref[row : row + 4, :]

    halo_by_chord(take, pair_ref, other_ref)
    outer = rows_scale()[1]
    push(layer_of(s_out, 0), layer_of(s_out, 1), layer_of(v_out, 0), v_out, 0, outer)
    for lanes, _, minus in force_parts(layer_of(s_out, 3), (False, True)):
        for at in range(3):
            put(v_out, (at, 3), lanes, v_out[at, 3, :, lanes] + SCALE * minus[at], outer)
    for at in range(6):
        low_ref[at] = s_out[at, 0]
    for at in range(3):
        low_ref[6 + at] = v_out[at, 0]
        high_ref[at] = v_out[at, 3]
    odd = span_odd()

    @pl.when(odd)
    def _():
        chip_ref[...] = low_ref[...]

    @pl.when(jnp.logical_not(odd))
    def _():
        chip_ref[0:3] = high_ref[...]
        chip_ref[3:9] = jnp.zeros((6, ROWS, 512), jnp.float32)


def between_kernel(sources_ref, v_ref, s_ref, v_out, e_out, added_ref):
    for at in range(15):
        added_ref[at] = jnp.zeros((ROWS, 512), jnp.float32)
    for at in range(3):
        v_out[at, 0] = v_ref[at, 0]
    outer = rows_scale()[1]
    for x in (1, 2):
        push(layer_of(s_ref, x), layer_of(s_ref, x + 1), layer_of(v_ref, x), v_out, x, outer)
    for at in range(16):
        layer, chord, deep = spot(sources_ref, at)
        inside = (chord >= -DEEP) & (chord < 16 + DEEP)

        @pl.when(inside & ((layer == -1) | (layer == 3) | (layer == 4)))
        def _():
            slot = jnp.where(layer == -1, 0, layer - 2)
            add_at(added_ref, (slot,), chord, deep, sources_ref[at, 3])

        @pl.when(inside & (layer >= 0) & (layer < 3))
        def _():
            add_at(v_out, (2, layer), chord, deep, sources_ref[at, 3])

        @pl.when(inside & (layer >= 0) & (layer < 4))
        def _():
            for step_at in range(1, 4):
                add_at(
                    added_ref, (slot_of(step_at, layer),), chord, deep, sources_ref[at, 3 + step_at]
                )

    for layers in zip(*[strain_parts(layer_of(v_out, x)) for x in range(3)]):
        lanes = layers[0][0]
        for x in range(2):
            for at, value in enumerate(strains(layers[x + 1][1], layers[x][1])):
                e_out[at, x, :, lanes] = value


def after_span_kernel(
    v_ref, s_ref, half_ref, added_ref, chip_ref, low_ref, high_ref, v_out, e_out, s_end_ref, side_ref
):
    odd = span_odd()
    outer = rows_scale()[1]
    inside = jnp.where(lax.axis_index("span") == 0, 0.0, 1.0)

    @pl.when(odd)
    def _():
        for at in range(6):
            s_end_ref[at] = low_ref[at]
        for at in range(3):
            side_ref[at, 0] = chip_ref[at]
            side_ref[at, 1] = low_ref[6 + at]

    @pl.when(jnp.logical_not(odd))
    def _():
        for at in range(6):
            s_end_ref[at] = chip_ref[at]
        for at in range(3):
            side_ref[at, 0] = high_ref[at]
            side_ref[at, 1] = chip_ref[6 + at]

    before = with_source(layer_of(side_ref, 0), added_ref, 0)
    push_half(layer_of(s_ref, 0), before, side_ref, lambda at: (at, 0), outer, inside)
    own = with_source(layer_of(half_ref, 3), added_ref, 1)
    push_half(plane_of(s_end_ref), own, v_out, lambda at: (at,), outer)
    after = with_source(layer_of(side_ref, 1), added_ref, 2)
    streams = [
        strain_parts(load)
        for load in (layer_of(side_ref, 0), layer_of(v_ref, 0), layer_of(v_ref, 2), plane_of(v_out), after)
    ]
    for layers in zip(*streams):
        lanes = layers[0][0]
        for slot, x in enumerate((0, 2, 3)):
            for at, value in enumerate(strains(layers[x + 1][1], layers[x][1])):
                e_out[at, slot, :, lanes] = value


def with_source(load, added_ref, slot):
    def both(at, lanes):
        value = load(at, lanes)
        return value + added_ref[slot, :, lanes] if at == 2 else value

    return both


def slot_of(step_at, layer):
    return 4 * step_at - 1 + layer


def out_by_core(ends_ref, chip_ref, far_ref):
    odd = span_odd()
    for at in range(3):
        chip_ref[at] = jnp.where(odd, ends_ref[at, 0], ends_ref[at, 1])
        far_ref[at] = jnp.where(odd, ends_ref[at, 1], ends_ref[at, 0])


def first_stress(x, slot, rows, lanes, q, e_ref, s_ref, s_end_ref, s_out, b_out):
    bonds = bonds_of(*q)
    for at, value in enumerate(bonds):
        b_out[at, slot, rows, lanes] = value
    ref, index = e_ref
    e = [ref[at, index, rows, lanes] for at in range(6)]
    rates = stress_rates(e, bonds[:6], bonds[6:])
    if x == 4:
        edge = jnp.where(lax.axis_index("span") == 15, 0.0, 1.0)
        rates = [rate * edge for rate in rates]
    return [
        (s_ref[at, x, rows, lanes] if x < 4 else s_end_ref[at, rows, lanes]) + rates[at]
        for at in range(6)
    ]


ENDS = (0, 1, 3, 4)


def strains_of(x, e_ref, e_mid_ref):
    return (e_mid_ref, x - 1) if x in (1, 2) else (e_ref, {0: 0, 3: 1, 4: 2}[x])


def first_own_kernel(e_ref, e_mid_ref, s_ref, s_end_ref, q_ref, s_out, b_out):
    for lanes in LANES:
        for slot, x in enumerate(ENDS):
            for rows in (slice(0, 8), slice(8, 16)):
                q = [q_ref[5 * at + x, rows, lanes] for at in range(3)]
                e = strains_of(x, e_ref, e_mid_ref)
                new = first_stress(x, slot, rows, lanes, q, e, s_ref, s_end_ref, s_out, b_out)
                for at in range(6):
                    s_out[at, slot, rows, lanes] = new[at]


def first_end_kernel(
    s_held, b_held, v_ref, v_last_ref, e_ref, e_mid_ref, s_ref, s_end_ref, pair_ref, other_ref, added_ref,
    s_out, b_out, q_out, chip_ref, far_ref, halo_ref, ends_ref,
):
    halo_ref[...] = jnp.zeros(halo_ref.shape, jnp.float32)

    def take(next_ref, prior_ref):
        for at in range(15):
            halo_ref[at, 0:3] = next_ref[3 * at : 3 * at + 3]
            halo_ref[at, 5:8] = prior_ref[3 * at : 3 * at + 3]

    halo_by_chord(take, pair_ref, other_ref)
    outer_s, outer_v = rows_scale()
    rows = slice(16, ROWS)
    for at in range(3):
        q_out[at] = halo_ref[5 * at + 2]
    for lanes in LANES:
        for slot, x in enumerate(ENDS):
            q = [halo_ref[5 * at + x, :, lanes] for at in range(3)]
            e = strains_of(x, e_ref, e_mid_ref)
            new = first_stress(x, slot, rows, lanes, q, e, s_ref, s_end_ref, s_out, b_out)
            for at in range(6):
                s_out[at, slot, rows, lanes] = new[at] * outer_s
    low = with_source(layer_of(v_ref, 0), added_ref, slot_of(1, 0))
    high = with_source(plane_of(v_last_ref), added_ref, slot_of(1, 3))
    push(layer_of(s_out, 0), layer_of(s_out, 1), low, ends_ref, 0, outer_v)
    push(layer_of(s_out, 2), layer_of(s_out, 3), high, ends_ref, 1, outer_v)
    out_by_core(ends_ref, chip_ref, far_ref)


def middle(v_layers, s_old, bond_of, s_out, outer):
    for layers in zip(*[strain_parts(load) for load in v_layers]):
        lanes = layers[0][0]
        for x in range(3):
            e = strains(layers[x + 1][1], layers[x][1])
            strain(e, bond_of(x, lanes), lambda at: s_old(at, x, lanes), s_out, x, lanes, outer)


def end_layers(chip_ref, far_ref):
    odd = span_odd()
    low = lambda at, lanes: jnp.where(odd, chip_ref[at, :, lanes], far_ref[at, :, lanes])
    high = lambda at, lanes: jnp.where(odd, far_ref[at, :, lanes], chip_ref[at, :, lanes])
    return low, high


def first_middle_kernel(
    v_ref, e_ref, s_ref, ends_ref, b_ref, q_ref, halo_ref, chip_ref, far_ref, added_ref,
    v_out, s_out, b_out, stress_ref, mid_ref,
):
    outer_s, outer_v = rows_scale()
    for lanes in LANES:
        for rows in (slice(0, 8), slice(8, 16), slice(16, ROWS)):
            own = rows.start < 16
            q = [q_ref[5 * at + 2, rows, lanes] if own else halo_ref[at, :, lanes] for at in range(3)]
            new = first_stress(2, 0, rows, lanes, q, (e_ref, 1), s_ref, None, stress_ref, b_out)
            for at in range(6):
                stress_ref[at, 0, rows, lanes] = new[at] if own else new[at] * outer_s

    def push_middle(loads, old, new, step_at):
        def moved(at, x, lanes):
            value = old(at, x, lanes)
            return value + added_ref[slot_of(step_at, 1 + x), :, lanes] if at == 2 else value

        push_two(loads, moved, new, outer_v)

    loads = [layer_of(ends_ref, 1), layer_of(stress_ref, 0), layer_of(ends_ref, 2)]
    push_middle(loads, lambda at, x, lanes: v_ref[at, 1 + x, :, lanes], mid_ref, 1)
    low, high = end_layers(chip_ref, far_ref)

    def s_old(at, x, lanes):
        return stress_ref[at, 0, :, lanes] if x == 1 else ends_ref[at, 1 + x // 2, :, lanes]

    def bond_of(x, lanes):
        return [
            b_out[at, 0, :, lanes] if x == 1 else b_ref[at, 1 + x // 2, :, lanes] for at in range(12)
        ]

    middle([low, layer_of(mid_ref, 0), layer_of(mid_ref, 1), high], s_old, bond_of, s_out, outer_s)
    loads = [layer_of(s_out, x) for x in range(3)]
    push_middle(loads, lambda at, x, lanes: mid_ref[at, x, :, lanes], v_out, 2)


def middle_kernel(v_ref, s_ref, b_ref, b_mid_ref, chip_ref, far_ref, added_ref, v_out, s_out):
    outer_s, outer_v = rows_scale()
    low, high = end_layers(chip_ref, far_ref)

    def bond_of(x, lanes):
        return [
            b_mid_ref[at, 0, :, lanes] if x == 1 else b_ref[at, 1 + x // 2, :, lanes]
            for at in range(12)
        ]

    s_old = lambda at, x, lanes: s_ref[at, x, :, lanes]
    middle([low, layer_of(v_ref, 0), layer_of(v_ref, 1), high], s_old, bond_of, s_out, outer_s)
    loads = [layer_of(s_out, x) for x in range(3)]

    def moved(at, x, lanes):
        value = v_ref[at, x, :, lanes]
        return value + added_ref[slot_of(3, 1 + x), :, lanes] if at == 2 else value

    push_two(loads, moved, v_out, outer_v)


def end_kernel(
    step_at, s_ends_ref, s_mid_ref, b_ref, chip_ref, far_ref, got_chip_ref, got_far_ref, added_ref,
    s_out, first_ref, second_ref, ends_ref,
):
    outer_s, outer_v = rows_scale()
    edge = jnp.where(lax.axis_index("span") == 15, 0.0, 1.0)
    low, high = end_layers(chip_ref, far_ref)
    before, after = end_layers(got_chip_ref, got_far_ref)
    count = s_ends_ref.shape[1]
    for parts in zip(*[strain_parts(load) for load in (before, low, high, after)]):
        lanes = parts[0][0]
        for slot, old, now in ((0, parts[0][1], parts[1][1]), (1, parts[2][1], parts[3][1])):
            bonds = [b_ref[at, 3 * slot, :, lanes] for at in range(12)]
            s_old = lambda at: s_ends_ref[at, slot * (count - 1), :, lanes]
            strain(strains(now, old), bonds, s_old, s_out, slot, lanes, outer_s, edge if slot else None)
    low = with_source(low, added_ref, slot_of(step_at, 0))
    high = with_source(high, added_ref, slot_of(step_at, 3))
    push(layer_of(s_out, 0), layer_of(s_mid_ref, 0), low, ends_ref, 0, outer_v)
    push(layer_of(s_mid_ref, 2), layer_of(s_out, 1), high, ends_ref, 1, outer_v)
    if step_at < 3:
        out_by_core(ends_ref, first_ref, second_ref)
    else:
        for at in range(3):
            first_ref[at] = ends_ref[at, 0]
            second_ref[at] = ends_ref[at, 1]


def last_middle_kernel(v_ref, s_ref, b_ref, b_mid_ref, low_ref, high_ref, v_out, s_out):
    layers = [plane_of(low_ref), layer_of(v_ref, 0), layer_of(v_ref, 1), plane_of(high_ref)]
    for parts in zip(*[strain_parts(load) for load in layers]):
        lanes = parts[0][0]
        for x in range(4):
            for at in range(3):
                v_out[at, x, :, lanes] = layers[x](at, lanes)[0:16]
        for x in range(3):
            e = [value[0:16] for value in strains(parts[x + 1][1], parts[x][1])]
            bonds = [
                b_mid_ref[at, 0, 0:16, lanes] if x == 1 else b_ref[at, 1 + x // 2, 0:16, lanes]
                for at in range(12)
            ]
            for at, rate in enumerate(stress_rates(e, bonds[:6], bonds[6:])):
                s_out[at, 1 + x, :, lanes] = s_ref[at, x, 0:16, lanes] + rate


def last_end_kernel(held_ref, s_ref, b_ref, low_ref, before_ref, out_ref, end_ref, sem):
    for (lanes, old), (_, now) in zip(strain_parts(plane_of(before_ref)), strain_parts(plane_of(low_ref))):
        e = [value[0:16] for value in strains(now, old)]
        bonds = [b_ref[at, 0, 0:16, lanes] for at in range(12)]
        for at, rate in enumerate(stress_rates(e, bonds[:6], bonds[6:])):
            end_ref[at, :, lanes] = s_ref[at, 0, 0:16, lanes] + rate
    copy = pltpu.make_async_copy(end_ref, out_ref.at[:, 0], sem)
    copy.start()
    copy.wait()


def shift(x, axis, by):
    peers = lax.axis_size(axis)
    pairs = [(i, i + by) for i in range(peers) if 0 <= i + by < peers]
    return lax.ppermute(x, axis, pairs)


def swap(x, axis, first):
    peers = lax.axis_size(axis)
    pairs = []
    for i in range(first, peers - 1, 2):
        pairs += [(i, i + 1), (i + 1, i)]
    return lax.ppermute(x, axis, pairs)


def far_shift(x, by):
    peers = lax.axis_size("span")
    first = 2 if by < 0 else 1
    return lax.ppermute(x, "span", [(i, i + by) for i in range(first, peers, 2) if i + by < peers])


def swaps(pair, other, axis):
    second = swap(other, axis, 1)
    return swap(pair, axis, 0), second


def shards(
    velocity, stress, grain_ids, lattice_tilt, grain_orient, orientations, source_cells, source_signal
):
    plane = (ROWS, 512)
    edge, ends = (3, *plane), (3, 2, *plane)
    sources = jnp.concatenate((source_cells.astype(jnp.float32), source_signal), axis=1)
    (sent,) = call(
        rotation_kernel,
        [(16, 64, 128)],
        (
            jnp.transpose(grain_ids, (1, 2, 0)),
            jnp.transpose(lattice_tilt, (0, 2, 3, 1)),
            grain_orient.reshape(32, 128),
            orientations,
        ),
        scratch=[(3, 272, 128)],
        flops=32768 * 200,
    )

    got = lax.all_to_all(sent, "span", 0, 0, tiled=True)

    half, s, pair, other = call(
        edge_kernel,
        [(3, 4, *plane), (6, 4, *plane), (144, 512), (144, 512)],
        (velocity, stress),
        scratch=[pltpu.SemaphoreType.DMA((9,))],
        spaces={0: pltpu.HBM, 1: pltpu.HBM},
    )
    pair, other = swaps(pair, other, "chord")
    half, s, chip, low, high = call(
        before_span_kernel,
        [(3, 4, *plane), (6, 4, *plane), (9, *plane), (9, *plane), edge],
        (half, s, pair, other),
        aliases={0: 0, 1: 1},
    )
    low, high = far_shift(low, -1), far_shift(high, 1)
    chip = swap(chip, "span", 0)
    v, e_mid, added = call(
        between_kernel,
        [(3, 3, *plane), (6, 2, *plane), (15, *plane)],
        (sources, half, s),
        spaces={0: pltpu.SMEM},
    )

    pair, other = call(arrange_edge_kernel, [(48, 512), (48, 512)], (got,))
    pair, other = swaps(pair, other, "chord")
    (q,) = call(arrange_kernel, [(15, 16, 512)], (got,))

    v_last, e, s_end = call(
        after_span_kernel,
        [edge, (6, 3, *plane), (6, *plane)],
        (v, s, half, added, chip, low, high),
        scratch=[ends],
    )
    s_ends, bonds = call(
        first_own_kernel, [(6, 4, *plane), (12, 4, *plane)], (e, e_mid, s, s_end, q), flops=32768 * 100
    )
    s_ends, bonds, halo, chip, far = call(
        first_end_kernel,
        [(6, 4, *plane), (12, 4, *plane), (3, 8, 512), edge, edge],
        (s_ends, bonds, v, v_last, e, e_mid, s, s_end, pair, other, added),
        scratch=[(15, 8, 512), ends],
        aliases={0: 0, 1: 1},
    )
    got_chip, got_far = swaps(chip, far, "span")
    v, s, mid_bonds = call(
        first_middle_kernel,
        [ends, (6, 3, *plane), (12, 1, *plane)],
        (v, e_mid, s, s_ends, bonds, q, halo, chip, far, added),
        scratch=[(6, 1, *plane), ends],
        flops=32768 * 100,
    )
    s_ends, chip, far = call(
        lambda *refs: end_kernel(2, *refs),
        [(6, 2, *plane), edge, edge],
        (s_ends, s, bonds, chip, far, got_chip, got_far, added),
        scratch=[ends],
    )
    got_chip, got_far = swaps(chip, far, "span")
    v, s = call(
        middle_kernel,
        [ends, (6, 3, *plane)],
        (v, s, bonds, mid_bonds, chip, far, added),
        flops=32768 * 100,
    )
    s_ends, low, high = call(
        lambda *refs: end_kernel(3, *refs),
        [(6, 2, *plane), edge, edge],
        (s_ends, s, bonds, chip, far, got_chip, got_far, added),
        scratch=[ends],
    )
    before = shift(high, "span", 1)
    v, s = call(
        last_middle_kernel,
        [velocity.shape, stress.shape],
        (v, s, bonds, mid_bonds, low, high),
        flops=32768 * 100,
    )
    s = pl.pallas_call(
        last_end_kernel,
        out_shape=jax.ShapeDtypeStruct(stress.shape, jnp.float32),
        in_specs=[pl.BlockSpec(memory_space=pl.ANY)] + [WHOLE] * 4,
        out_specs=pl.BlockSpec(memory_space=pl.ANY),
        scratch_shapes=[pltpu.VMEM((6, 16, 512), jnp.float32), pltpu.SemaphoreType.DMA],
        input_output_aliases={0: 0},
        compiler_params=VMEM,
    )(s, s_ends, bonds, low, before)
    return v, s


def solution(mesh):
    return jax.shard_map(
        shards,
        mesh=mesh,
        in_specs=(
            P(None, "span", "chord", None),
            P(None, "span", "chord", None),
            P(None, "chord", "span"),
            P(None, None, "chord", "span"),
            P(),
            P(),
            P(),
            P(),
        ),
        out_specs=(P(None, "span", "chord", None), P(None, "span", "chord", None)),
        check_vma=False,
    )
```

```python
import jax
import jax.numpy as jnp
from jax import lax
from jax.experimental import pallas as pl
from jax.experimental.pallas import tpu as pltpu
from jax.sharding import PartitionSpec as P

normal_modulus = 0.9
cross_modulus = 1.6
shear_modulus = 1.3
time_step = 0.25
anisotropy = normal_modulus - 2.0 * shear_modulus

DEEP = 4
ROWS = 24
TABLE_ROWS = 11
VMEM = pltpu.CompilerParams(vmem_limit_bytes=16 * 2**20)
WHOLE = pl.BlockSpec(memory_space=pltpu.VMEM)
LANES = [slice(128 * at, 128 * at + 128) for at in range(4)]


def call(kernel, outs, operands, scratch=(), spaces=(), aliases=None, flops=0):
    spaces = dict(spaces)
    return pl.pallas_call(
        kernel,
        out_shape=[jax.ShapeDtypeStruct(shape, jnp.float32) for shape in outs],
        in_specs=[pl.BlockSpec(memory_space=spaces.get(at, pltpu.VMEM)) for at in range(len(operands))],
        out_specs=[WHOLE] * len(outs),
        scratch_shapes=[
            pltpu.VMEM(shape, jnp.float32) if isinstance(shape, tuple) else shape for shape in scratch
        ],
        input_output_aliases=aliases or {},
        compiler_params=VMEM,
        cost_estimate=pl.CostEstimate(
            flops=flops,
            bytes_accessed=4 * sum(operand.size for operand in operands),
            transcendentals=0,
        ),
    )(*operands)


def small_sin(x):
    y = x * x
    return x * (
        1.0 + y * (-1.0 / 6 + y * (1.0 / 120 + y * (-1.0 / 5040 + y * (1.0 / 362880))))
    )


def small_cos(x):
    y = x * x
    return 1.0 + y * (
        -0.5
        + y * (1.0 / 24 + y * (-1.0 / 720 + y * (1.0 / 40320 + y * (-1.0 / 3628800))))
    )


def wide_sin_cos(x):
    quarter = 0.25 * x
    s, c = small_sin(quarter), small_cos(quarter)
    s, c = 2.0 * s * c, 1.0 - 2.0 * s * s
    return 2.0 * s * c, 1.0 - 2.0 * s * s


def quaternion(first, middle, last, sin_cos):
    s_mid, c_mid = sin_cos(0.5 * middle)
    s_sum, c_sum = sin_cos(0.5 * (first + last))
    s_dif, c_dif = sin_cos(0.5 * (first - last))
    return c_mid * c_sum, -s_mid * c_dif, -s_mid * s_dif, -c_mid * s_sum


def product(a, b):
    return (
        a[0] * b[0] - a[1] * b[1] - a[2] * b[2] - a[3] * b[3],
        a[0] * b[1] + a[1] * b[0] + a[2] * b[3] - a[3] * b[2],
        a[0] * b[2] - a[1] * b[3] + a[2] * b[0] + a[3] * b[1],
        a[0] * b[3] + a[1] * b[2] - a[2] * b[1] + a[3] * b[0],
    )


def reduced(q):
    w, x, y, z = q
    aw, ax, ay, az = jnp.abs(w), jnp.abs(x), jnp.abs(y), jnp.abs(z)
    low, high = jnp.maximum(aw, ax), jnp.maximum(ay, az)
    upper = high > low
    second = jnp.where(upper, az - ay, ax - aw) > 0.0

    def pick(a, b, c, d):
        return jnp.where(upper, jnp.where(second, d, c), jnp.where(second, b, a))

    lead = pick(w, x, y, z)
    flip = jnp.where(lead < 0.0, -1.0, 1.0)
    return (
        pick(x, -w, z, -y) * flip,
        pick(y, -z, -w, x) * flip,
        pick(z, y, -x, -w) * flip,
    )


def look_up(row, lane):
    return jnp.take_along_axis(
        jnp.broadcast_to(row, lane.shape), lane, axis=1, mode="promise_in_bounds"
    )


LEVEL = 1 << 19
FINE = 0.75 / LEVEL


def coded(q):
    w, x, y, z = q
    aw, ax, ay, az = jnp.abs(w), jnp.abs(x), jnp.abs(y), jnp.abs(z)
    upper = jnp.maximum(ay, az) > jnp.maximum(aw, ax)
    second = jnp.where(upper, az - ay, ax - aw) > 0.0

    def pick(a, b, c, d):
        return jnp.where(upper, jnp.where(second, d, c), jnp.where(second, b, a))

    flip = jnp.where(pick(w, x, y, z) < 0.0, -1.0 / FINE, 1.0 / FINE)
    rest = (pick(x, w, w, w), pick(y, y, x, x), pick(z, z, z, y))
    a, b, c = [jnp.round(part * flip).astype(jnp.int32) + LEVEL for part in rest]
    return (
        a + ((b & 1023) << 20) + jnp.where(second, 1 << 30, 0),
        c + ((b >> 10) << 20) + jnp.where(upper, 1 << 30, 0),
    )


def decoded(one, two):
    mask = (1 << 20) - 1
    a = one & mask
    b = ((one >> 20) & 1023) | (((two >> 20) & 1023) << 10)
    c = two & mask
    a, b, c = [(part - LEVEL).astype(jnp.float32) * FINE for part in (a, b, c)]
    lead = jnp.sqrt(1.0 - a * a - b * b - c * c)
    second, upper = (one >> 30) > 0, (two >> 30) > 0

    def pick(w, x, y, z):
        return jnp.where(upper, jnp.where(second, z, y), jnp.where(second, x, w))

    return pick(lead, a, a, a), pick(a, lead, b, b), pick(b, b, lead, c), pick(c, c, c, lead)


def turned_parts(grain, angles, grain_ref, angle_ref):
    packed = []
    for at in range(TABLE_ROWS):
        row = grain_ref[at : at + 1, :] + grain_ref[at + 11 : at + 12, :] * 512
        if at + 22 < 32:
            row = row + grain_ref[at + 22 : at + 23, :] * (512 * 512)
        packed.append(row)
    table = coded(quaternion(*[angle_ref[at : at + 1, :] for at in range(3)], wide_sin_cos))
    third = jnp.where(grain >= 2816, 2, jnp.where(grain >= 1408, 1, 0))
    grain = grain - 1408 * third
    lane, place = grain & 127, grain >> 7
    entry = look_up(packed[0], lane)
    for at in range(1, TABLE_ROWS):
        entry = jnp.where(place == at, look_up(packed[at], lane), entry)
    entry = (entry >> (9 * third)) & 511
    lane, place = entry & 127, entry >> 7
    found = []
    for code in table:
        part = [code[:, lanes] for lanes in LANES]
        low = jnp.where(place == 1, look_up(part[1], lane), look_up(part[0], lane))
        high = jnp.where(place == 3, look_up(part[3], lane), look_up(part[2], lane))
        found.append(jnp.where(place >= 2, high, low))
    tilt_turn = quaternion(*angles, lambda x: (small_sin(x), small_cos(x)))
    return reduced(product(decoded(*found), tilt_turn))


def side_by_side(ref, *lead):
    *lead, chord = lead
    return jnp.concatenate([ref[(*lead, chord)], ref[(*lead, chord + 1)]], axis=1)


def rotation_kernel(ids_ref, tilt_ref, grain_ref, angle_ref, out_ref, sorted_ref):
    for pair in range(2):
        chords = [4 * group + 2 * pair for group in range(4)]

        def stacked(ref, *lead):
            return jnp.concatenate([side_by_side(ref, *lead, chord) for chord in chords], axis=0)

        values = turned_parts(
            stacked(ids_ref), [stacked(tilt_ref, at) for at in range(3)], grain_ref, angle_ref
        )
        for at in range(3):
            turned = values[at].T
            for half in range(2):
                sorted_ref[at, pl.ds(2 * pair + half, 64, stride=4), :] = turned[
                    64 * half : 64 * half + 64, :
                ]
    for at in range(3):
        sorted_ref[at, 256:272, :] = jnp.zeros((16, 128), jnp.float32)
    for device in range(16):
        for at in range(3):
            row = 16 * device
            out_ref[device, 16 * at : 16 * at + 16, :] = sorted_ref[at, row : row + 16, :]
            out_ref[device, 48 + 4 * at : 52 + 4 * at, :] = sorted_ref[at, row + 16 : row + 20, :]


def depth_parts(got_ref):
    for four, deep in enumerate(LANES):
        pieces = [got_ref[4 * four + at] for at in range(4)]

        def lanes_of(group):
            return jnp.concatenate(
                [piece[:, 32 * group : 32 * group + 32] for piece in pieces], axis=1
            )

        yield deep, lanes_of


def row_of(at, layer):
    return 16 * at + 4 * layer if layer < 4 else 48 + 4 * at


def arrange_edge_kernel(got_ref, pair_ref, other_ref):
    def fill(ref, group, first):
        for deep, lanes_of in depth_parts(got_ref):
            lanes = lanes_of(group)
            for at in range(3):
                for layer in range(5):
                    slot, row = 15 * at + 3 * layer, row_of(at, layer) + first
                    ref[slot : slot + 3, deep] = lanes[row : row + 3, :]
        ref[45:48, :] = jnp.zeros((3, 512), jnp.float32)

    by_chord(lambda ref, low: fill(ref, *low), pair_ref, other_ref, (0, 0), (3, 1))


def arrange_kernel(got_ref, q_ref):
    for deep, lanes_of in depth_parts(got_ref):
        for group in range(4):
            lanes = lanes_of(group)
            for at in range(3):
                for layer in range(5):
                    row = row_of(at, layer)
                    q_ref[5 * at + layer, 4 * group : 4 * group + 4, deep] = lanes[row : row + 4, :]


def by_chord(fill, pair_ref, other_ref, low, high):
    even = lax.axis_index("chord") % 2 == 0

    @pl.when(even)
    def _():
        fill(pair_ref, high)
        fill(other_ref, low)

    @pl.when(jnp.logical_not(even))
    def _():
        fill(pair_ref, low)
        fill(other_ref, high)


def halo_by_chord(take, pair_ref, other_ref):
    even = lax.axis_index("chord") % 2 == 0

    @pl.when(even)
    def _():
        take(pair_ref, other_ref)

    @pl.when(jnp.logical_not(even))
    def _():
        take(other_ref, pair_ref)


SCALE = 0.25 * time_step


def lane_is(at):
    return lax.broadcasted_iota(jnp.int32, (ROWS, 128), 1) == at


def next_row(x):
    return pltpu.roll(x, ROWS - 1, 0)


def row_before(x):
    return pltpu.roll(x, 1, 0)


def strain_parts(load):
    first = lane_is(0)
    held = [0.0] * 3
    for lanes in LANES:
        sums, rows, deeps = [], [], []
        for at in range(3):
            value = load(at, lanes)
            rolled = pltpu.roll(value, 1, 1)
            earlier = jnp.where(first, held[at], rolled)
            held[at] = rolled
            total, change = value + earlier, value - earlier
            behind = row_before(total)
            sums.append(total + behind)
            rows.append(total - behind)
            deeps.append(change + row_before(change))
        yield lanes, (
            sums[0],
            rows[1],
            deeps[2],
            rows[2] + deeps[1],
            deeps[0] + sums[2],
            deeps[0] - sums[2],
            rows[0] + sums[1],
            rows[0] - sums[1],
        )


def strains(now, old):
    return (
        now[0] - old[0],
        now[1] + old[1],
        now[2] + old[2],
        now[3] + old[3],
        now[4] + old[5],
        now[6] + old[7],
    )


def force_parts(load, need=(True, True)):
    last = lane_is(127)
    held = [0.0] * 6
    for lanes in reversed(LANES):
        total, change = [], []
        for at in range(6):
            value = load(at, lanes)
            rolled = pltpu.roll(value, 127, 1)
            later = jnp.where(last, held[at], rolled)
            held[at] = rolled
            total.append(value + later)
            change.append(later - value)
        plus, minus = [], []
        for lead, side, deep in ((0, 5, 4), (5, 1, 3), (4, 3, 2)):
            ahead = total[lead] + next_row(total[lead])
            rest = next_row(total[side] + change[deep]) + (change[deep] - total[side])
            plus.append(rest + ahead if need[0] else None)
            minus.append(rest - ahead if need[1] else None)
        yield lanes, plus, minus


def stress_rates(e, first_bond, second_bond):
    trace = e[0] + e[1] + e[2]
    along = []
    for bond in (first_bond, second_bond):
        part = bond[0] * e[0]
        for at in range(1, 6):
            part = part + bond[at] * e[at]
        along.append(part)
    third = trace - along[0] - along[1]
    first_weight = (SCALE * anisotropy) * (along[0] - third)
    second_weight = (SCALE * anisotropy) * (along[1] - third)
    level = (SCALE * cross_modulus) * trace + (SCALE * anisotropy) * third
    rates = []
    for at in range(6):
        rate = first_bond[at] * first_weight + second_bond[at] * second_weight
        if at < 3:
            rate = rate + ((2.0 * SCALE * shear_modulus) * e[at] + level)
        else:
            rate = rate + (SCALE * shear_modulus) * e[at]
        rates.append(rate)
    return rates


def bonds_of(a, b, c):
    w = jnp.sqrt(jnp.maximum(1.0 - a * a - b * b - c * c, 0.0))
    ab, ac, bc = a * b, a * c, b * c
    wa, wb, wc = w * a, w * b, w * c
    aa, bb, cc = a * a, b * b, c * c
    bonds = []
    for p, q, r in (
        (1.0 - 2.0 * (bb + cc), 2.0 * (ab + wc), 2.0 * (ac - wb)),
        (2.0 * (ab - wc), 1.0 - 2.0 * (aa + cc), 2.0 * (bc + wa)),
    ):
        bonds += [p * p, q * q, r * r, q * r, r * p, p * q]
    return bonds


def outer_scale(outside_low, outside_high):
    row = lax.broadcasted_iota(jnp.int32, (8, 128), 0)
    outside = ((row < DEEP) & outside_high) | ((row >= DEEP) & outside_low)
    return jnp.where(outside, 0.0, 1.0)


def put(ref, lead, lanes, value, outer):
    ref[(*lead, slice(0, 16), lanes)] = value[0:16]
    ref[(*lead, slice(16, ROWS), lanes)] = value[16:ROWS] * outer


def push(low, high, old, new, lead, outer, factor=None):
    for (lanes, _, minus), (_, plus, _) in zip(
        force_parts(low, (False, True)), force_parts(high, (True, False))
    ):
        for at in range(3):
            value = old(at, lanes) + SCALE * (plus[at] + minus[at])
            if factor is not None:
                value = value * factor
            put(new, (at, lead), lanes, value, outer)


def push_two(loads, old, new, outer, low=None, high=None, ends=None):
    for (lanes, below, first), (_, second, third), (_, fourth, above) in zip(
        force_parts(loads[0]),
        force_parts(loads[1]),
        force_parts(loads[2]),
    ):
        for at in range(3):
            put(new, (at, 0), lanes, old(at, 0, lanes) + SCALE * (second[at] + first[at]), outer)
            put(new, (at, 1), lanes, old(at, 1, lanes) + SCALE * (fourth[at] + third[at]), outer)
            if ends is not None:
                ends[at, 0, :, lanes] = low(at, lanes) + SCALE * below[at]
                ends[at, 1, :, lanes] = high(at, lanes) + SCALE * above[at]


NOW = (0, 1, 2, 3, 4, 6)
OLD = (0, 1, 2, 3, 5, 7)


def strain(e, bonds, old, new, lead, lanes, outer, factor=None):
    for at, rate in enumerate(stress_rates(e, bonds[:6], bonds[6:])):
        if factor is not None:
            rate = rate * factor
        put(new, (at, lead), lanes, old(at) + rate, outer)


def layer_of(ref, x):
    return lambda at, lanes: ref[at, x, :, lanes]


def plane_of(ref, first=0):
    return lambda at, lanes: ref[first + at, :, lanes]


def span_odd():
    return lax.axis_index("span") % 2 == 1


def rows_scale():
    chord = lax.axis_index("chord")
    return outer_scale(False, chord == 7), outer_scale(chord == 0, False)


def edge_kernel(field_ref, v_out, s_out, pair_ref, other_ref):
    for at in range(9):
        if at < 6:
            s_out[at, :, 0:16] = field_ref[at]
        else:
            v_out[at - 6, :, 0:16] = field_ref[at]

    def fill(ref, first):
        rows = slice(first, first + DEEP)
        for at in range(9):
            for x in range(4):
                row = 16 * at + 4 * x
                ref[row : row + 4, :] = field_ref[at, x, rows]

    by_chord(fill, pair_ref, other_ref, 0, 16 - DEEP)


def spot(sources_ref, at):
    layer = sources_ref[at, 0].astype(jnp.int32) - 4 * lax.axis_index("span")
    chord = sources_ref[at, 1].astype(jnp.int32) - 16 * lax.axis_index("chord")
    return layer, chord, sources_ref[at, 2].astype(jnp.int32)


def add_at(ref, lead, chord, deep, amount):
    row = jnp.where(chord < 0, chord + ROWS, chord)
    rows = pl.ds(pl.multiple_of((row // 8) * 8, 8), 8)
    lanes = pl.ds(pl.multiple_of((deep // 128) * 128, 128), 128)
    hit = (lax.broadcasted_iota(jnp.int32, (8, 128), 0) == row % 8) & (
        lax.broadcasted_iota(jnp.int32, (8, 128), 1) == deep % 128
    )
    ref[(*lead, rows, lanes)] = ref[(*lead, rows, lanes)] + jnp.where(hit, amount, 0.0)


def push_half(high, old, new, lead, outer, factor=None):
    for lanes, plus, _ in force_parts(high, (True, False)):
        for at in range(3):
            value = old(at, lanes) + SCALE * plus[at]
            if factor is not None:
                value = value * factor
            put(new, (*lead(at),), lanes, value, outer)


def before_span_kernel(v_ref, s_ref, pair_ref, other_ref, v_out, s_out, chip_ref, low_ref, high_ref):
    def take(next_ref, prior_ref):
        for at in range(9):
            out, slot = (s_out, at) if at < 6 else (v_out, at - 6)
            for x in range(4):
                row = 16 * at + 4 * x
                out[slot, x, 16 : 16 + DEEP] = next_ref[row : row + 4, :]
                out[slot, x, 16 + DEEP : ROWS] = prior_ref[row : row + 4, :]

    halo_by_chord(take, pair_ref, other_ref)
    outer = rows_scale()[1]
    push(layer_of(s_out, 0), layer_of(s_out, 1), layer_of(v_out, 0), v_out, 0, outer)
    for lanes, _, minus in force_parts(layer_of(s_out, 3), (False, True)):
        for at in range(3):
            put(v_out, (at, 3), lanes, v_out[at, 3, :, lanes] + SCALE * minus[at], outer)
    for at in range(6):
        low_ref[at] = s_out[at, 0]
    for at in range(3):
        low_ref[6 + at] = v_out[at, 0]
        high_ref[at] = v_out[at, 3]
    odd = span_odd()

    @pl.when(odd)
    def _():
        chip_ref[...] = low_ref[...]

    @pl.when(jnp.logical_not(odd))
    def _():
        chip_ref[0:3] = high_ref[...]
        chip_ref[3:9] = jnp.zeros((6, ROWS, 512), jnp.float32)


def between_kernel(sources_ref, v_ref, s_ref, v_out, e_out, added_ref):
    for at in range(15):
        added_ref[at] = jnp.zeros((ROWS, 512), jnp.float32)
    for at in range(3):
        v_out[at, 0] = v_ref[at, 0]
    outer = rows_scale()[1]
    for x in (1, 2):
        push(layer_of(s_ref, x), layer_of(s_ref, x + 1), layer_of(v_ref, x), v_out, x, outer)
    for at in range(16):
        layer, chord, deep = spot(sources_ref, at)
        inside = (chord >= -DEEP) & (chord < 16 + DEEP)

        @pl.when(inside & ((layer == -1) | (layer == 3) | (layer == 4)))
        def _():
            slot = jnp.where(layer == -1, 0, layer - 2)
            add_at(added_ref, (slot,), chord, deep, sources_ref[at, 3])

        @pl.when(inside & (layer >= 0) & (layer < 3))
        def _():
            add_at(v_out, (2, layer), chord, deep, sources_ref[at, 3])

        @pl.when(inside & (layer >= 0) & (layer < 4))
        def _():
            for step_at in range(1, 4):
                add_at(
                    added_ref, (slot_of(step_at, layer),), chord, deep, sources_ref[at, 3 + step_at]
                )

    for layers in zip(*[strain_parts(layer_of(v_out, x)) for x in range(3)]):
        lanes = layers[0][0]
        for x in range(2):
            for at, value in enumerate(strains(layers[x + 1][1], layers[x][1])):
                e_out[at, x, :, lanes] = value


def after_span_kernel(
    v_ref, s_ref, half_ref, added_ref, chip_ref, low_ref, high_ref, v_out, e_out, s_end_ref, side_ref
):
    odd = span_odd()
    outer = rows_scale()[1]
    inside = jnp.where(lax.axis_index("span") == 0, 0.0, 1.0)

    @pl.when(odd)
    def _():
        for at in range(6):
            s_end_ref[at] = low_ref[at]
        for at in range(3):
            side_ref[at, 0] = chip_ref[at]
            side_ref[at, 1] = low_ref[6 + at]

    @pl.when(jnp.logical_not(odd))
    def _():
        for at in range(6):
            s_end_ref[at] = chip_ref[at]
        for at in range(3):
            side_ref[at, 0] = high_ref[at]
            side_ref[at, 1] = chip_ref[6 + at]

    before = with_source(layer_of(side_ref, 0), added_ref, 0)
    push_half(layer_of(s_ref, 0), before, side_ref, lambda at: (at, 0), outer, inside)
    own = with_source(layer_of(half_ref, 3), added_ref, 1)
    push_half(plane_of(s_end_ref), own, v_out, lambda at: (at,), outer)
    after = with_source(layer_of(side_ref, 1), added_ref, 2)
    streams = [
        strain_parts(load)
        for load in (layer_of(side_ref, 0), layer_of(v_ref, 0), layer_of(v_ref, 2), plane_of(v_out), after)
    ]
    for layers in zip(*streams):
        lanes = layers[0][0]
        for slot, x in enumerate((0, 2, 3)):
            for at, value in enumerate(strains(layers[x + 1][1], layers[x][1])):
                e_out[at, slot, :, lanes] = value


def with_source(load, added_ref, slot):
    def both(at, lanes):
        value = load(at, lanes)
        return value + added_ref[slot, :, lanes] if at == 2 else value

    return both


def slot_of(step_at, layer):
    return 4 * step_at - 1 + layer


def out_by_core(ends_ref, chip_ref, far_ref):
    odd = span_odd()
    for at in range(3):
        chip_ref[at] = jnp.where(odd, ends_ref[at, 0], ends_ref[at, 1])
        far_ref[at] = jnp.where(odd, ends_ref[at, 1], ends_ref[at, 0])


def first_stress(x, slot, rows, lanes, q, e_ref, s_ref, s_end_ref, s_out, b_out):
    bonds = bonds_of(*q)
    for at, value in enumerate(bonds):
        b_out[at, slot, rows, lanes] = value
    ref, index = e_ref
    e = [ref[at, index, rows, lanes] for at in range(6)]
    rates = stress_rates(e, bonds[:6], bonds[6:])
    if x == 4:
        edge = jnp.where(lax.axis_index("span") == 15, 0.0, 1.0)
        rates = [rate * edge for rate in rates]
    return [
        (s_ref[at, x, rows, lanes] if x < 4 else s_end_ref[at, rows, lanes]) + rates[at]
        for at in range(6)
    ]


ENDS = (0, 1, 3, 4)


def strains_of(x, e_ref, e_mid_ref):
    return (e_mid_ref, x - 1) if x in (1, 2) else (e_ref, {0: 0, 3: 1, 4: 2}[x])


def first_own_kernel(e_ref, e_mid_ref, s_ref, s_end_ref, q_ref, s_out, b_out):
    for lanes in LANES:
        for slot, x in enumerate(ENDS):
            for rows in (slice(0, 8), slice(8, 16)):
                q = [q_ref[5 * at + x, rows, lanes] for at in range(3)]
                e = strains_of(x, e_ref, e_mid_ref)
                new = first_stress(x, slot, rows, lanes, q, e, s_ref, s_end_ref, s_out, b_out)
                for at in range(6):
                    s_out[at, slot, rows, lanes] = new[at]


def first_end_kernel(
    s_held, b_held, v_ref, v_last_ref, e_ref, e_mid_ref, s_ref, s_end_ref, pair_ref, other_ref, added_ref,
    s_out, b_out, q_out, chip_ref, far_ref, halo_ref, ends_ref,
):
    halo_ref[...] = jnp.zeros(halo_ref.shape, jnp.float32)

    def take(next_ref, prior_ref):
        for at in range(15):
            halo_ref[at, 0:3] = next_ref[3 * at : 3 * at + 3]
            halo_ref[at, 5:8] = prior_ref[3 * at : 3 * at + 3]

    halo_by_chord(take, pair_ref, other_ref)
    outer_s, outer_v = rows_scale()
    rows = slice(16, ROWS)
    for at in range(3):
        q_out[at] = halo_ref[5 * at + 2]
    for lanes in LANES:
        for slot, x in enumerate(ENDS):
            q = [halo_ref[5 * at + x, :, lanes] for at in range(3)]
            e = strains_of(x, e_ref, e_mid_ref)
            new = first_stress(x, slot, rows, lanes, q, e, s_ref, s_end_ref, s_out, b_out)
            for at in range(6):
                s_out[at, slot, rows, lanes] = new[at] * outer_s
    low = with_source(layer_of(v_ref, 0), added_ref, slot_of(1, 0))
    high = with_source(plane_of(v_last_ref), added_ref, slot_of(1, 3))
    push(layer_of(s_out, 0), layer_of(s_out, 1), low, ends_ref, 0, outer_v)
    push(layer_of(s_out, 2), layer_of(s_out, 3), high, ends_ref, 1, outer_v)
    out_by_core(ends_ref, chip_ref, far_ref)


def middle(v_layers, s_old, bond_of, s_out, outer, parts_out):
    for layers in zip(*[strain_parts(load) for load in v_layers]):
        lanes = layers[0][0]
        for at in range(6):
            parts_out[at, 0, :, lanes] = layers[0][1][NOW[at]]
            parts_out[at, 1, :, lanes] = layers[3][1][OLD[at]]
        for x in range(3):
            e = strains(layers[x + 1][1], layers[x][1])
            strain(e, bond_of(x, lanes), lambda at: s_old(at, x, lanes), s_out, x, lanes, outer)


def end_layers(chip_ref, far_ref):
    odd = span_odd()
    low = lambda at, lanes: jnp.where(odd, chip_ref[at, :, lanes], far_ref[at, :, lanes])
    high = lambda at, lanes: jnp.where(odd, far_ref[at, :, lanes], chip_ref[at, :, lanes])
    return low, high


def first_middle_kernel(
    v_ref, e_ref, s_ref, ends_ref, b_ref, q_ref, halo_ref, chip_ref, far_ref, added_ref,
    v_out, s_out, b_out, half_out, parts_out, stress_ref, mid_ref,
):
    outer_s, outer_v = rows_scale()
    for lanes in LANES:
        for rows in (slice(0, 8), slice(8, 16), slice(16, ROWS)):
            own = rows.start < 16
            q = [q_ref[5 * at + 2, rows, lanes] if own else halo_ref[at, :, lanes] for at in range(3)]
            new = first_stress(2, 0, rows, lanes, q, (e_ref, 1), s_ref, None, stress_ref, b_out)
            for at in range(6):
                stress_ref[at, 0, rows, lanes] = new[at] if own else new[at] * outer_s

    def push_middle(loads, old, new, step_at, *ends):
        def moved(at, x, lanes):
            value = old(at, x, lanes)
            return value + added_ref[slot_of(step_at, 1 + x), :, lanes] if at == 2 else value

        push_two(loads, moved, new, outer_v, *ends)

    loads = [layer_of(ends_ref, 1), layer_of(stress_ref, 0), layer_of(ends_ref, 2)]
    push_middle(loads, lambda at, x, lanes: v_ref[at, 1 + x, :, lanes], mid_ref, 1)
    low, high = end_layers(chip_ref, far_ref)

    def s_old(at, x, lanes):
        return stress_ref[at, 0, :, lanes] if x == 1 else ends_ref[at, 1 + x // 2, :, lanes]

    def bond_of(x, lanes):
        return [
            b_out[at, 0, :, lanes] if x == 1 else b_ref[at, 1 + x // 2, :, lanes] for at in range(12)
        ]

    layers = [low, layer_of(mid_ref, 0), layer_of(mid_ref, 1), high]
    middle(layers, s_old, bond_of, s_out, outer_s, parts_out)
    loads = [layer_of(s_out, x) for x in range(3)]
    low = with_source(low, added_ref, slot_of(2, 0))
    high = with_source(high, added_ref, slot_of(2, 3))
    push_middle(loads, lambda at, x, lanes: mid_ref[at, x, :, lanes], v_out, 2, low, high, half_out)


def middle_kernel(
    v_ref, s_ref, b_ref, b_mid_ref, chip_ref, far_ref, added_ref, v_out, s_out, half_out, parts_out
):
    outer_s, outer_v = rows_scale()
    low, high = end_layers(chip_ref, far_ref)

    def bond_of(x, lanes):
        return [
            b_mid_ref[at, 0, :, lanes] if x == 1 else b_ref[at, 1 + x // 2, :, lanes]
            for at in range(12)
        ]

    s_old = lambda at, x, lanes: s_ref[at, x, :, lanes]
    layers = [low, layer_of(v_ref, 0), layer_of(v_ref, 1), high]
    middle(layers, s_old, bond_of, s_out, outer_s, parts_out)
    loads = [layer_of(s_out, x) for x in range(3)]

    def moved(at, x, lanes):
        value = v_ref[at, x, :, lanes]
        return value + added_ref[slot_of(3, 1 + x), :, lanes] if at == 2 else value

    low = with_source(low, added_ref, slot_of(3, 0))
    high = with_source(high, added_ref, slot_of(3, 3))
    push_two(loads, moved, v_out, outer_v, low, high, half_out)


def end_kernel(
    last, s_ends_ref, half_ref, parts_ref, b_ref, got_chip_ref, got_far_ref,
    s_out, first_ref, second_ref, *rest,
):
    ends_ref = rest[-1]
    outer_s, outer_v = rows_scale()
    edge = jnp.where(lax.axis_index("span") == 15, 0.0, 1.0)
    before, after = end_layers(got_chip_ref, got_far_ref)
    count = s_ends_ref.shape[1]
    for (lanes, old), (_, now) in zip(strain_parts(before), strain_parts(after)):
        low = [parts_ref[at, 0, :, lanes] for at in range(6)]
        high = [parts_ref[at, 1, :, lanes] for at in range(6)]
        low = [low[0] - old[0]] + [low[at] + old[OLD[at]] for at in range(1, 6)]
        high = [now[0] - high[0]] + [now[NOW[at]] + high[at] for at in range(1, 6)]
        for slot, e in ((0, low), (1, high)):
            bonds = [b_ref[at, 3 * slot, :, lanes] for at in range(12)]
            s_old = lambda at: s_ends_ref[at, slot * (count - 1), :, lanes]
            strain(e, bonds, s_old, s_out, slot, lanes, outer_s, edge if slot else None)
    for (lanes, _, minus), (_, plus, _) in zip(
        force_parts(layer_of(s_out, 0), (False, True)), force_parts(layer_of(s_out, 1), (True, False))
    ):
        for at in range(3):
            put(ends_ref, (at, 0), lanes, half_ref[at, 0, :, lanes] + SCALE * minus[at], outer_v)
            put(ends_ref, (at, 1), lanes, half_ref[at, 1, :, lanes] + SCALE * plus[at], outer_v)
    if not last:
        out_by_core(ends_ref, first_ref, second_ref)
        return
    sent_ref = rest[0]
    for at in range(3):
        first_ref[at] = ends_ref[at, 0]
        second_ref[at] = ends_ref[at, 1]
        sent_ref[16 * at : 16 * at + 16, :] = ends_ref[at, 1, 0:16]
        sent_ref[48 + at : 49 + at, :] = ends_ref[at, 1, ROWS - 1 : ROWS]
    sent_ref[51:56, :] = jnp.zeros((5, 512), jnp.float32)


def last_middle_kernel(v_ref, s_ref, b_ref, b_mid_ref, low_ref, high_ref, v_out, s_out, parts_out):
    layers = [plane_of(low_ref), layer_of(v_ref, 0), layer_of(v_ref, 1), plane_of(high_ref)]
    for parts in zip(*[strain_parts(load) for load in layers]):
        lanes = parts[0][0]
        for at in range(6):
            parts_out[at, :, lanes] = parts[0][1][NOW[at]][0:16]
        for x in range(4):
            for at in range(3):
                v_out[at, x, :, lanes] = layers[x](at, lanes)[0:16]
        for x in range(3):
            e = [value[0:16] for value in strains(parts[x + 1][1], parts[x][1])]
            bonds = [
                b_mid_ref[at, 0, 0:16, lanes] if x == 1 else b_ref[at, 1 + x // 2, 0:16, lanes]
                for at in range(12)
            ]
            for at, rate in enumerate(stress_rates(e, bonds[:6], bonds[6:])):
                s_out[at, 1 + x, :, lanes] = s_ref[at, x, 0:16, lanes] + rate


def last_end_kernel(held_ref, s_ref, b_ref, parts_ref, got_ref, out_ref, before_ref, end_ref, sem):
    for at in range(3):
        before_ref[at, 0:16] = got_ref[16 * at : 16 * at + 16, :]
        before_ref[at, 16:ROWS] = jnp.zeros((8, 512), jnp.float32)
        before_ref[at, ROWS - 1 : ROWS] = got_ref[48 + at : 49 + at, :]
    for lanes, old in strain_parts(plane_of(before_ref)):
        now = [parts_ref[at, :, lanes] for at in range(6)]
        old = [value[0:16] for value in old]
        e = [now[0] - old[0]] + [now[at] + old[OLD[at]] for at in range(1, 6)]
        bonds = [b_ref[at, 0, 0:16, lanes] for at in range(12)]
        for at, rate in enumerate(stress_rates(e, bonds[:6], bonds[6:])):
            end_ref[at, :, lanes] = s_ref[at, 0, 0:16, lanes] + rate
    copy = pltpu.make_async_copy(end_ref, out_ref.at[:, 0], sem)
    copy.start()
    copy.wait()


def shift(x, axis, by):
    peers = lax.axis_size(axis)
    pairs = [(i, i + by) for i in range(peers) if 0 <= i + by < peers]
    return lax.ppermute(x, axis, pairs)


def swap(x, axis, first):
    peers = lax.axis_size(axis)
    pairs = []
    for i in range(first, peers - 1, 2):
        pairs += [(i, i + 1), (i + 1, i)]
    return lax.ppermute(x, axis, pairs)


def far_shift(x, by):
    peers = lax.axis_size("span")
    first = 2 if by < 0 else 1
    return lax.ppermute(x, "span", [(i, i + by) for i in range(first, peers, 2) if i + by < peers])


def swaps(pair, other, axis):
    second = swap(other, axis, 1)
    return swap(pair, axis, 0), second


def shards(
    velocity, stress, grain_ids, lattice_tilt, grain_orient, orientations, source_cells, source_signal
):
    plane = (ROWS, 512)
    edge, ends = (3, *plane), (3, 2, *plane)
    sources = jnp.concatenate((source_cells.astype(jnp.float32), source_signal), axis=1)
    (sent,) = call(
        rotation_kernel,
        [(16, 64, 128)],
        (
            jnp.transpose(grain_ids, (1, 2, 0)),
            jnp.transpose(lattice_tilt, (0, 2, 3, 1)),
            grain_orient.reshape(32, 128),
            orientations,
        ),
        scratch=[(3, 272, 128)],
        flops=32768 * 200,
    )

    got = lax.all_to_all(sent, "span", 0, 0, tiled=True)

    half, s, pair, other = call(
        edge_kernel,
        [(3, 4, *plane), (6, 4, *plane), (144, 512), (144, 512)],
        (jnp.concatenate((stress, velocity)),),
    )
    pair, other = swaps(pair, other, "chord")
    half, s, chip, low, high = call(
        before_span_kernel,
        [(3, 4, *plane), (6, 4, *plane), (9, *plane), (9, *plane), edge],
        (half, s, pair, other),
        aliases={0: 0, 1: 1},
    )
    low, high = far_shift(low, -1), far_shift(high, 1)
    chip = swap(chip, "span", 0)
    v, e_mid, added = call(
        between_kernel,
        [(3, 3, *plane), (6, 2, *plane), (15, *plane)],
        (sources, half, s),
        spaces={0: pltpu.SMEM},
    )

    pair, other = call(arrange_edge_kernel, [(48, 512), (48, 512)], (got,))
    pair, other = swaps(pair, other, "chord")
    (q,) = call(arrange_kernel, [(15, 16, 512)], (got,))

    v_last, e, s_end = call(
        after_span_kernel,
        [edge, (6, 3, *plane), (6, *plane)],
        (v, s, half, added, chip, low, high),
        scratch=[ends],
    )
    s_ends, bonds = call(
        first_own_kernel, [(6, 4, *plane), (12, 4, *plane)], (e, e_mid, s, s_end, q), flops=32768 * 100
    )
    s_ends, bonds, halo, chip, far = call(
        first_end_kernel,
        [(6, 4, *plane), (12, 4, *plane), (3, 8, 512), edge, edge],
        (s_ends, bonds, v, v_last, e, e_mid, s, s_end, pair, other, added),
        scratch=[(15, 8, 512), ends],
        aliases={0: 0, 1: 1},
    )
    got_chip, got_far = swaps(chip, far, "span")
    parts = (6, 2, *plane)
    v, s, mid_bonds, half, part = call(
        first_middle_kernel,
        [ends, (6, 3, *plane), (12, 1, *plane), ends, parts],
        (v, e_mid, s, s_ends, bonds, q, halo, chip, far, added),
        scratch=[(6, 1, *plane), ends],
        flops=32768 * 100,
    )
    s_ends, chip, far = call(
        lambda *refs: end_kernel(False, *refs),
        [(6, 2, *plane), edge, edge],
        (s_ends, half, part, bonds, got_chip, got_far),
        scratch=[ends],
    )
    got_chip, got_far = swaps(chip, far, "span")
    v, s, half, part = call(
        middle_kernel,
        [ends, (6, 3, *plane), ends, parts],
        (v, s, bonds, mid_bonds, chip, far, added),
        flops=32768 * 100,
    )
    s_ends, low, high, sent = call(
        lambda *refs: end_kernel(True, *refs),
        [(6, 2, *plane), edge, edge, (56, 512)],
        (s_ends, half, part, bonds, got_chip, got_far),
        scratch=[ends],
    )
    before = shift(sent, "span", 1)
    v, s, part = call(
        last_middle_kernel,
        [velocity.shape, stress.shape, (6, 16, 512)],
        (v, s, bonds, mid_bonds, low, high),
        flops=32768 * 100,
    )
    s = pl.pallas_call(
        last_end_kernel,
        out_shape=jax.ShapeDtypeStruct(stress.shape, jnp.float32),
        in_specs=[pl.BlockSpec(memory_space=pl.ANY)] + [WHOLE] * 4,
        out_specs=pl.BlockSpec(memory_space=pl.ANY),
        scratch_shapes=[
            pltpu.VMEM(edge, jnp.float32),
            pltpu.VMEM((6, 16, 512), jnp.float32),
            pltpu.SemaphoreType.DMA,
        ],
        input_output_aliases={0: 0},
        compiler_params=VMEM,
    )(s, s_ends, bonds, part, before)
    return v, s


def solution(mesh):
    return jax.shard_map(
        shards,
        mesh=mesh,
        in_specs=(
            P(None, "span", "chord", None),
            P(None, "span", "chord", None),
            P(None, "chord", "span"),
            P(None, None, "chord", "span"),
            P(),
            P(),
            P(),
            P(),
        ),
        out_specs=(P(None, "span", "chord", None), P(None, "span", "chord", None)),
        check_vma=False,
    )
```

```python
import jax
import jax.numpy as jnp
from jax import lax
from jax.experimental import pallas as pl
from jax.experimental.pallas import tpu as pltpu
from jax.sharding import PartitionSpec as P

normal_modulus = 0.9
cross_modulus = 1.6
shear_modulus = 1.3
time_step = 0.25
anisotropy = normal_modulus - 2.0 * shear_modulus

DEEP = 4
ROWS = 24
TABLE_ROWS = 11
VMEM = pltpu.CompilerParams(vmem_limit_bytes=16 * 2**20)
WHOLE = pl.BlockSpec(memory_space=pltpu.VMEM)
LANES = [slice(128 * at, 128 * at + 128) for at in range(4)]


def call(kernel, outs, operands, scratch=(), spaces=(), aliases=None, flops=0):
    spaces = dict(spaces)
    return pl.pallas_call(
        kernel,
        out_shape=[jax.ShapeDtypeStruct(shape, jnp.float32) for shape in outs],
        in_specs=[pl.BlockSpec(memory_space=spaces.get(at, pltpu.VMEM)) for at in range(len(operands))],
        out_specs=[WHOLE] * len(outs),
        scratch_shapes=[
            pltpu.VMEM(shape, jnp.float32) if isinstance(shape, tuple) else shape for shape in scratch
        ],
        input_output_aliases=aliases or {},
        compiler_params=VMEM,
        cost_estimate=pl.CostEstimate(
            flops=flops,
            bytes_accessed=4 * sum(operand.size for operand in operands),
            transcendentals=0,
        ),
    )(*operands)


def small_sin(x):
    y = x * x
    return x * (
        1.0 + y * (-1.0 / 6 + y * (1.0 / 120 + y * (-1.0 / 5040 + y * (1.0 / 362880))))
    )


def small_cos(x):
    y = x * x
    return 1.0 + y * (
        -0.5
        + y * (1.0 / 24 + y * (-1.0 / 720 + y * (1.0 / 40320 + y * (-1.0 / 3628800))))
    )


def wide_sin_cos(x):
    quarter = 0.25 * x
    s, c = small_sin(quarter), small_cos(quarter)
    s, c = 2.0 * s * c, 1.0 - 2.0 * s * s
    return 2.0 * s * c, 1.0 - 2.0 * s * s


def quaternion(first, middle, last, sin_cos):
    s_mid, c_mid = sin_cos(0.5 * middle)
    s_sum, c_sum = sin_cos(0.5 * (first + last))
    s_dif, c_dif = sin_cos(0.5 * (first - last))
    return c_mid * c_sum, -s_mid * c_dif, -s_mid * s_dif, -c_mid * s_sum


def product(a, b):
    return (
        a[0] * b[0] - a[1] * b[1] - a[2] * b[2] - a[3] * b[3],
        a[0] * b[1] + a[1] * b[0] + a[2] * b[3] - a[3] * b[2],
        a[0] * b[2] - a[1] * b[3] + a[2] * b[0] + a[3] * b[1],
        a[0] * b[3] + a[1] * b[2] - a[2] * b[1] + a[3] * b[0],
    )


def reduced(q):
    w, x, y, z = q
    aw, ax, ay, az = jnp.abs(w), jnp.abs(x), jnp.abs(y), jnp.abs(z)
    low, high = jnp.maximum(aw, ax), jnp.maximum(ay, az)
    upper = high > low
    second = jnp.where(upper, az - ay, ax - aw) > 0.0

    def pick(a, b, c, d):
        return jnp.where(upper, jnp.where(second, d, c), jnp.where(second, b, a))

    lead = pick(w, x, y, z)
    flip = jnp.where(lead < 0.0, -1.0, 1.0)
    return (
        pick(x, -w, z, -y) * flip,
        pick(y, -z, -w, x) * flip,
        pick(z, y, -x, -w) * flip,
    )


def look_up(row, lane):
    return jnp.take_along_axis(
        jnp.broadcast_to(row, lane.shape), lane, axis=1, mode="promise_in_bounds"
    )


LEVEL = 1 << 19
FINE = 0.75 / LEVEL


def coded(q):
    w, x, y, z = q
    aw, ax, ay, az = jnp.abs(w), jnp.abs(x), jnp.abs(y), jnp.abs(z)
    upper = jnp.maximum(ay, az) > jnp.maximum(aw, ax)
    second = jnp.where(upper, az - ay, ax - aw) > 0.0

    def pick(a, b, c, d):
        return jnp.where(upper, jnp.where(second, d, c), jnp.where(second, b, a))

    flip = jnp.where(pick(w, x, y, z) < 0.0, -1.0 / FINE, 1.0 / FINE)
    rest = (pick(x, w, w, w), pick(y, y, x, x), pick(z, z, z, y))
    a, b, c = [jnp.round(part * flip).astype(jnp.int32) + LEVEL for part in rest]
    return (
        a + ((b & 1023) << 20) + jnp.where(second, 1 << 30, 0),
        c + ((b >> 10) << 20) + jnp.where(upper, 1 << 30, 0),
    )


def decoded(one, two):
    mask = (1 << 20) - 1
    a = one & mask
    b = ((one >> 20) & 1023) | (((two >> 20) & 1023) << 10)
    c = two & mask
    a, b, c = [(part - LEVEL).astype(jnp.float32) * FINE for part in (a, b, c)]
    lead = jnp.sqrt(1.0 - a * a - b * b - c * c)
    second, upper = (one >> 30) > 0, (two >> 30) > 0

    def pick(w, x, y, z):
        return jnp.where(upper, jnp.where(second, z, y), jnp.where(second, x, w))

    return pick(lead, a, a, a), pick(a, lead, b, b), pick(b, b, lead, c), pick(c, c, c, lead)


def turned_parts(grain, angles, grain_ref, angle_ref):
    packed = []
    for at in range(TABLE_ROWS):
        row = grain_ref[at : at + 1, :] + grain_ref[at + 11 : at + 12, :] * 512
        if at + 22 < 32:
            row = row + grain_ref[at + 22 : at + 23, :] * (512 * 512)
        packed.append(row)
    table = coded(quaternion(*[angle_ref[at : at + 1, :] for at in range(3)], wide_sin_cos))
    third = jnp.where(grain >= 2816, 2, jnp.where(grain >= 1408, 1, 0))
    grain = grain - 1408 * third
    lane, place = grain & 127, grain >> 7
    entry = look_up(packed[0], lane)
    for at in range(1, TABLE_ROWS):
        entry = jnp.where(place == at, look_up(packed[at], lane), entry)
    entry = (entry >> (9 * third)) & 511
    lane, place = entry & 127, entry >> 7
    found = []
    for code in table:
        part = [code[:, lanes] for lanes in LANES]
        low = jnp.where(place == 1, look_up(part[1], lane), look_up(part[0], lane))
        high = jnp.where(place == 3, look_up(part[3], lane), look_up(part[2], lane))
        found.append(jnp.where(place >= 2, high, low))
    tilt_turn = quaternion(*angles, lambda x: (small_sin(x), small_cos(x)))
    return reduced(product(decoded(*found), tilt_turn))


def side_by_side(ref, *lead):
    *lead, chord = lead
    return jnp.concatenate([ref[(*lead, chord)], ref[(*lead, chord + 1)]], axis=1)


def rotation_kernel(ids_ref, tilt_ref, grain_ref, angle_ref, out_ref, sorted_ref):
    for pair in range(2):
        chords = [4 * group + 2 * pair for group in range(4)]

        def stacked(ref, *lead):
            return jnp.concatenate([side_by_side(ref, *lead, chord) for chord in chords], axis=0)

        values = turned_parts(
            stacked(ids_ref), [stacked(tilt_ref, at) for at in range(3)], grain_ref, angle_ref
        )
        for at in range(3):
            turned = values[at].T
            for half in range(2):
                sorted_ref[at, pl.ds(2 * pair + half, 64, stride=4), :] = turned[
                    64 * half : 64 * half + 64, :
                ]
    for device in range(16):
        for at in range(3):
            row = 16 * device
            out_ref[device, 16 * at : 16 * at + 16, :] = sorted_ref[at, row : row + 16, :]


def depth_parts(got_ref):
    for four, deep in enumerate(LANES):
        pieces = [got_ref[4 * four + at] for at in range(4)]

        def lanes_of(group):
            return jnp.concatenate(
                [piece[:, 32 * group : 32 * group + 32] for piece in pieces], axis=1
            )

        yield deep, lanes_of


def arrange_edge_kernel(got_ref, pair_ref, other_ref):
    def fill(ref, group, first):
        for deep, lanes_of in depth_parts(got_ref):
            lanes = lanes_of(group)
            for at in range(12):
                ref[3 * at : 3 * at + 3, deep] = lanes[4 * at + first : 4 * at + first + 3, :]
        ref[36:40, :] = jnp.zeros((4, 512), jnp.float32)

    by_chord(lambda ref, low: fill(ref, *low), pair_ref, other_ref, (0, 0), (3, 1))


def arrange_kernel(got_ref, q_ref):
    for deep, lanes_of in depth_parts(got_ref):
        for group in range(4):
            lanes = lanes_of(group)
            for at in range(12):
                q_ref[at, 4 * group : 4 * group + 4, deep] = lanes[4 * at : 4 * at + 4, :]


def by_chord(fill, pair_ref, other_ref, low, high):
    even = lax.axis_index("chord") % 2 == 0

    @pl.when(even)
    def _():
        fill(pair_ref, high)
        fill(other_ref, low)

    @pl.when(jnp.logical_not(even))
    def _():
        fill(pair_ref, low)
        fill(other_ref, high)


def halo_by_chord(take, pair_ref, other_ref):
    even = lax.axis_index("chord") % 2 == 0

    @pl.when(even)
    def _():
        take(pair_ref, other_ref)

    @pl.when(jnp.logical_not(even))
    def _():
        take(other_ref, pair_ref)


SCALE = 0.25 * time_step


def lane_is(at):
    return lax.broadcasted_iota(jnp.int32, (ROWS, 128), 1) == at


def next_row(x):
    return pltpu.roll(x, ROWS - 1, 0)


def row_before(x):
    return pltpu.roll(x, 1, 0)


def strain_parts(load):
    first = lane_is(0)
    held = [0.0] * 3
    for lanes in LANES:
        sums, rows, deeps = [], [], []
        for at in range(3):
            value = load(at, lanes)
            rolled = pltpu.roll(value, 1, 1)
            earlier = jnp.where(first, held[at], rolled)
            held[at] = rolled
            total, change = value + earlier, value - earlier
            behind = row_before(total)
            sums.append(total + behind)
            rows.append(total - behind)
            deeps.append(change + row_before(change))
        yield lanes, (
            sums[0],
            rows[1],
            deeps[2],
            rows[2] + deeps[1],
            deeps[0] + sums[2],
            deeps[0] - sums[2],
            rows[0] + sums[1],
            rows[0] - sums[1],
        )


def strains(now, old):
    return (
        now[0] - old[0],
        now[1] + old[1],
        now[2] + old[2],
        now[3] + old[3],
        now[4] + old[5],
        now[6] + old[7],
    )


def force_parts(load, need=(True, True)):
    last = lane_is(127)
    held = [0.0] * 6
    for lanes in reversed(LANES):
        total, change = [], []
        for at in range(6):
            value = load(at, lanes)
            rolled = pltpu.roll(value, 127, 1)
            later = jnp.where(last, held[at], rolled)
            held[at] = rolled
            total.append(value + later)
            change.append(later - value)
        plus, minus = [], []
        for lead, side, deep in ((0, 5, 4), (5, 1, 3), (4, 3, 2)):
            ahead = total[lead] + next_row(total[lead])
            rest = next_row(total[side] + change[deep]) + (change[deep] - total[side])
            plus.append(rest + ahead if need[0] else None)
            minus.append(rest - ahead if need[1] else None)
        yield lanes, plus, minus


def stress_rates(e, first_bond, second_bond):
    trace = e[0] + e[1] + e[2]
    along = []
    for bond in (first_bond, second_bond):
        part = bond[0] * e[0]
        for at in range(1, 6):
            part = part + bond[at] * e[at]
        along.append(part)
    third = trace - along[0] - along[1]
    first_weight = (SCALE * anisotropy) * (along[0] - third)
    second_weight = (SCALE * anisotropy) * (along[1] - third)
    level = (SCALE * cross_modulus) * trace + (SCALE * anisotropy) * third
    rates = []
    for at in range(6):
        rate = first_bond[at] * first_weight + second_bond[at] * second_weight
        if at < 3:
            rate = rate + ((2.0 * SCALE * shear_modulus) * e[at] + level)
        else:
            rate = rate + (SCALE * shear_modulus) * e[at]
        rates.append(rate)
    return rates


def bonds_of(a, b, c):
    w = jnp.sqrt(jnp.maximum(1.0 - a * a - b * b - c * c, 0.0))
    ab, ac, bc = a * b, a * c, b * c
    wa, wb, wc = w * a, w * b, w * c
    aa, bb, cc = a * a, b * b, c * c
    bonds = []
    for p, q, r in (
        (1.0 - 2.0 * (bb + cc), 2.0 * (ab + wc), 2.0 * (ac - wb)),
        (2.0 * (ab - wc), 1.0 - 2.0 * (aa + cc), 2.0 * (bc + wa)),
    ):
        bonds += [p * p, q * q, r * r, q * r, r * p, p * q]
    return bonds


def outer_scale(outside_low, outside_high):
    row = lax.broadcasted_iota(jnp.int32, (8, 128), 0)
    outside = ((row < DEEP) & outside_high) | ((row >= DEEP) & outside_low)
    return jnp.where(outside, 0.0, 1.0)


def put(ref, lead, lanes, value, outer):
    ref[(*lead, slice(0, 16), lanes)] = value[0:16]
    ref[(*lead, slice(16, ROWS), lanes)] = value[16:ROWS] * outer


NOW = (0, 1, 2, 3, 4, 6)
OLD = (0, 1, 2, 3, 5, 7)


def push_three(loads, old, new, outer):
    for layers in zip(*[force_parts(load, (x > 0, x < 3)) for x, load in enumerate(loads)]):
        lanes = layers[0][0]
        for x in range(3):
            for at in range(3):
                force = layers[x + 1][1][at] + layers[x][2][at]
                put(new, (at, x), lanes, old(at, x, lanes) + SCALE * force, outer)


def send_parts(first, last, high, added, chip_ref, far_ref):
    odd = span_odd()
    for (lanes, plus, _), (_, _, minus) in zip(
        force_parts(first, (True, False)), force_parts(last, (False, True))
    ):
        for at in range(3):
            low = SCALE * plus[at]
            value = high(at, lanes) + SCALE * minus[at]
            if added is not None and at == 2:
                value = value + added(lanes)
            chip_ref[at, :, lanes] = jnp.where(odd, low, value)
            far_ref[at, :, lanes] = jnp.where(odd, value, low)


def take_parts(chip_ref, far_ref, got_chip_ref, got_far_ref, side_ref, added_ref=None):
    odd = span_odd()
    outer = rows_scale()[1]
    inside = jnp.where(lax.axis_index("span") == 0, 0.0, 1.0)
    for lanes in LANES:
        for at in range(3):
            chip = chip_ref[at, :, lanes] + got_chip_ref[at, :, lanes]
            far = far_ref[at, :, lanes] + got_far_ref[at, :, lanes]
            low, high = jnp.where(odd, chip, far), jnp.where(odd, far, chip)
            if added_ref is not None and at == 2:
                low, high = low + added_ref[0, :, lanes], high + added_ref[1, :, lanes]
            put(side_ref, (at, 0), lanes, low * inside, outer)
            put(side_ref, (at, 1), lanes, high, outer)


def strain(e, bonds, old, new, lead, lanes, outer, factor=None):
    for at, rate in enumerate(stress_rates(e, bonds[:6], bonds[6:])):
        if factor is not None:
            rate = rate * factor
        put(new, (at, lead), lanes, old(at) + rate, outer)


def layer_of(ref, x):
    return lambda at, lanes: ref[at, x, :, lanes]


def plane_of(ref, first=0):
    return lambda at, lanes: ref[first + at, :, lanes]


def span_odd():
    return lax.axis_index("span") % 2 == 1


def rows_scale():
    chord = lax.axis_index("chord")
    return outer_scale(False, chord == 7), outer_scale(chord == 0, False)


def edge_kernel(field_ref, v_out, s_out, pair_ref, other_ref):
    for at in range(9):
        if at < 6:
            s_out[at, :, 0:16] = field_ref[at]
        else:
            v_out[at - 6, :, 0:16] = field_ref[at]

    def fill(ref, first):
        rows = slice(first, first + DEEP)
        for at in range(9):
            for x in range(4):
                row = 16 * at + 4 * x
                ref[row : row + 4, :] = field_ref[at, x, rows]

    by_chord(fill, pair_ref, other_ref, 0, 16 - DEEP)


def spot(sources_ref, at):
    layer = sources_ref[at, 0].astype(jnp.int32) - 4 * lax.axis_index("span")
    chord = sources_ref[at, 1].astype(jnp.int32) - 16 * lax.axis_index("chord")
    return layer, chord, sources_ref[at, 2].astype(jnp.int32)


def add_at(ref, lead, chord, deep, amount):
    row = jnp.where(chord < 0, chord + ROWS, chord)
    rows = pl.ds(pl.multiple_of((row // 8) * 8, 8), 8)
    lanes = pl.ds(pl.multiple_of((deep // 128) * 128, 128), 128)
    hit = (lax.broadcasted_iota(jnp.int32, (8, 128), 0) == row % 8) & (
        lax.broadcasted_iota(jnp.int32, (8, 128), 1) == deep % 128
    )
    ref[(*lead, rows, lanes)] = ref[(*lead, rows, lanes)] + jnp.where(hit, amount, 0.0)


def before_span_kernel(v_ref, s_ref, pair_ref, other_ref, v_out, s_out, chip_ref, far_ref):
    def take(next_ref, prior_ref):
        for at in range(9):
            out, slot = (s_out, at) if at < 6 else (v_out, at - 6)
            for x in range(4):
                row = 16 * at + 4 * x
                out[slot, x, 16 : 16 + DEEP] = next_ref[row : row + 4, :]
                out[slot, x, 16 + DEEP : ROWS] = prior_ref[row : row + 4, :]

    halo_by_chord(take, pair_ref, other_ref)
    send_parts(layer_of(s_out, 0), layer_of(s_out, 3), layer_of(v_out, 3), None, chip_ref, far_ref)


def between_kernel(sources_ref, v_ref, s_ref, v_out, e_out, added_ref):
    for at in range(14):
        added_ref[at] = jnp.zeros((ROWS, 512), jnp.float32)
    outer = rows_scale()[1]
    loads = [layer_of(s_ref, x) for x in range(4)]
    push_three(loads, lambda at, x, lanes: v_ref[at, x, :, lanes], v_out, outer)
    for at in range(16):
        layer, chord, deep = spot(sources_ref, at)
        inside = (chord >= -DEEP) & (chord < 16 + DEEP)

        @pl.when(inside & ((layer == -1) | (layer == 3)))
        def _():
            slot = jnp.where(layer == -1, 0, 1)
            add_at(added_ref, (slot,), chord, deep, sources_ref[at, 3])

        @pl.when(inside & (layer >= 0) & (layer < 3))
        def _():
            add_at(v_out, (2, layer), chord, deep, sources_ref[at, 3])

        @pl.when(inside & (layer >= 0) & (layer < 4))
        def _():
            for step_at in range(1, 4):
                add_at(
                    added_ref, (slot_of(step_at, layer),), chord, deep, sources_ref[at, 3 + step_at]
                )

    for layers in zip(*[strain_parts(layer_of(v_out, x)) for x in range(3)]):
        lanes = layers[0][0]
        for x in range(2):
            for at, value in enumerate(strains(layers[x + 1][1], layers[x][1])):
                e_out[at, x, :, lanes] = value


def after_span_kernel(
    v_ref, added_ref, chip_ref, far_ref, got_chip_ref, got_far_ref, v_out, e_out, side_ref
):
    take_parts(chip_ref, far_ref, got_chip_ref, got_far_ref, side_ref, added_ref)
    for at in range(3):
        v_out[at] = side_ref[at, 1]
    loads = (layer_of(side_ref, 0), layer_of(v_ref, 0), layer_of(v_ref, 2), layer_of(side_ref, 1))
    for layers in zip(*[strain_parts(load) for load in loads]):
        lanes = layers[0][0]
        for slot in range(2):
            for at, value in enumerate(strains(layers[2 * slot + 1][1], layers[2 * slot][1])):
                e_out[at, slot, :, lanes] = value


def slot_of(step_at, layer):
    return 4 * step_at - 2 + layer


def first_stress(x, slot, rows, lanes, q, e_ref, index, s_ref, b_out):
    bonds = bonds_of(*q)
    for at, value in enumerate(bonds):
        b_out[at, slot, rows, lanes] = value
    e = [e_ref[at, index, rows, lanes] for at in range(6)]
    rates = stress_rates(e, bonds[:6], bonds[6:])
    return [s_ref[at, x, rows, lanes] + rates[at] for at in range(6)]


ENDS = (0, 3)


def first_own_kernel(e_ref, s_ref, q_ref, s_out, b_out):
    for lanes in LANES:
        for slot, x in enumerate(ENDS):
            for rows in (slice(0, 8), slice(8, 16)):
                q = [q_ref[4 * at + x, rows, lanes] for at in range(3)]
                new = first_stress(x, slot, rows, lanes, q, e_ref, slot, s_ref, b_out)
                for at in range(6):
                    s_out[at, slot, rows, lanes] = new[at]


def first_end_kernel(
    s_held, b_held, v_last_ref, e_ref, s_ref, pair_ref, other_ref, added_ref,
    s_out, b_out, q_out, chip_ref, far_ref, halo_ref,
):
    halo_ref[...] = jnp.zeros(halo_ref.shape, jnp.float32)

    def take(next_ref, prior_ref):
        for at in range(12):
            halo_ref[at, 0:3] = next_ref[3 * at : 3 * at + 3]
            halo_ref[at, 5:8] = prior_ref[3 * at : 3 * at + 3]

    halo_by_chord(take, pair_ref, other_ref)
    outer_s = rows_scale()[0]
    rows = slice(16, ROWS)
    for at in range(3):
        q_out[2 * at] = halo_ref[4 * at + 1]
        q_out[2 * at + 1] = halo_ref[4 * at + 2]
    for lanes in LANES:
        for slot, x in enumerate(ENDS):
            q = [halo_ref[4 * at + x, :, lanes] for at in range(3)]
            new = first_stress(x, slot, rows, lanes, q, e_ref, slot, s_ref, b_out)
            for at in range(6):
                s_out[at, slot, rows, lanes] = new[at] * outer_s
    added = lambda lanes: added_ref[slot_of(1, 3), :, lanes]
    send_parts(layer_of(s_out, 0), layer_of(s_out, 1), plane_of(v_last_ref), added, chip_ref, far_ref)


def middle(v_ref, s_ends_ref, s_mid, added_ref, step_at, bond_of, v_out, s_out, parts_out, rows=ROWS):
    outer_s, outer_v = rows_scale()
    loads = [layer_of(s_ends_ref, 0), s_mid(0), s_mid(1), layer_of(s_ends_ref, 1)]

    def old(at, x, lanes):
        value = v_ref[at, x, :, lanes]
        return value + added_ref[slot_of(step_at, x), :, lanes] if at == 2 else value

    push_three(loads, old, v_out, outer_v)
    for layers in zip(*[strain_parts(layer_of(v_out, x)) for x in range(3)]):
        lanes = layers[0][0]
        for at in range(6):
            parts_out[at, 0, :, lanes] = layers[0][1][NOW[at]][0:rows]
            parts_out[at, 1, :, lanes] = layers[2][1][OLD[at]][0:rows]
        for x in range(2):
            e = strains(layers[x + 1][1], layers[x][1])
            before = lambda at: s_mid(x)(at, lanes)
            if rows == ROWS:
                strain(e, bond_of(x, lanes), before, s_out, x, lanes, outer_s)
            else:
                bonds = [bond[0:rows] for bond in bond_of(x, lanes)]
                e = [value[0:rows] for value in e]
                for at, rate in enumerate(stress_rates(e, bonds[:6], bonds[6:])):
                    s_out[at, 1 + x, :, lanes] = before(at)[0:rows] + rate


def first_middle_kernel(
    v_ref, e_ref, s_ref, s_ends_ref, q_ref, halo_ref, added_ref,
    v_out, s_out, b_out, parts_out, stress_ref,
):
    outer_s, _ = rows_scale()
    for lanes in LANES:
        for x in range(2):
            for rows in (slice(0, 8), slice(8, 16), slice(16, ROWS)):
                own = rows.start < 16
                q = [
                    q_ref[4 * at + 1 + x, rows, lanes] if own else halo_ref[2 * at + x, :, lanes]
                    for at in range(3)
                ]
                new = first_stress(1 + x, x, rows, lanes, q, e_ref, x, s_ref, b_out)
                for at in range(6):
                    stress_ref[at, x, rows, lanes] = new[at] if own else new[at] * outer_s
    bond_of = lambda x, lanes: [b_out[at, x, :, lanes] for at in range(12)]
    s_mid = lambda x: layer_of(stress_ref, x)
    middle(v_ref, s_ends_ref, s_mid, added_ref, 1, bond_of, v_out, s_out, parts_out)


def middle_kernel(v_ref, s_ends_ref, s_ref, b_ref, added_ref, v_out, s_out, parts_out):
    bond_of = lambda x, lanes: [b_ref[at, x, :, lanes] for at in range(12)]
    s_mid = lambda x: layer_of(s_ref, x)
    middle(v_ref, s_ends_ref, s_mid, added_ref, 2, bond_of, v_out, s_out, parts_out)


def last_middle_kernel(
    v_ref, s_ends_ref, s_ref, b_ref, added_ref, v_out, s_out, parts_out, moved_ref
):
    bond_of = lambda x, lanes: [b_ref[at, x, :, lanes] for at in range(12)]
    s_mid = lambda x: layer_of(s_ref, x)
    middle(v_ref, s_ends_ref, s_mid, added_ref, 3, bond_of, moved_ref, s_out, parts_out, 16)
    for at in range(3):
        v_out[at, 0:3] = moved_ref[at, :, 0:16]


def end_strains(parts, slot, lanes, other):
    if slot == 0:
        return [parts[0] - other[0]] + [parts[at] + other[OLD[at]] for at in range(1, 6)]
    return [other[0] - parts[0]] + [other[NOW[at]] + parts[at] for at in range(1, 6)]


def end_kernel(
    last, s_ends_ref, parts_ref, b_ref, chip_ref, far_ref, got_chip_ref, got_far_ref, added_ref,
    s_out, next_chip_ref, next_far_ref, side_ref, *rest,
):
    take_parts(chip_ref, far_ref, got_chip_ref, got_far_ref, side_ref)
    outer_s = rows_scale()[0]
    for layers in zip(*[strain_parts(layer_of(side_ref, slot)) for slot in range(2)]):
        lanes = layers[0][0]
        for slot in range(2):
            parts = [parts_ref[at, slot, :, lanes] for at in range(6)]
            e = end_strains(parts, slot, lanes, layers[slot][1])
            bonds = [b_ref[at, slot, :, lanes] for at in range(12)]
            old = lambda at: s_ends_ref[at, slot, :, lanes]
            strain(e, bonds, old, s_out, slot, lanes, outer_s)
    chip, far = rest if last else (next_chip_ref, next_far_ref)
    added = lambda lanes: added_ref[slot_of(3 if last else 2, 3), :, lanes]
    send_parts(layer_of(s_out, 0), layer_of(s_out, 1), layer_of(side_ref, 1), added, chip, far)
    if last:
        for ref, full in ((next_chip_ref, chip), (next_far_ref, far)):
            for at in range(3):
                ref[16 * at : 16 * at + 16, :] = full[at, 0:16]
                ref[48 + at : 49 + at, :] = full[at, ROWS - 1 : ROWS]
            ref[51:56, :] = jnp.zeros((5, 512), jnp.float32)


def last_end_kernel(
    v_held, s_held, s_ref, b_ref, parts_ref, chip_ref, far_ref, got_chip_ref, got_far_ref,
    v_out, s_out, side_ref, end_ref, sems,
):
    odd = span_odd()
    inside = jnp.where(lax.axis_index("span") == 0, 0.0, 1.0)
    low_row = jnp.where(lax.axis_index("chord") == 0, 0.0, 1.0)
    for at in range(3):
        for slot in range(2):
            side_ref[at, slot, 16:ROWS] = jnp.zeros((8, 512), jnp.float32)
        for rows, place, factor in (
            (slice(16 * at, 16 * at + 16), slice(0, 16), 1.0),
            (slice(48 + at, 49 + at), slice(ROWS - 1, ROWS), low_row),
        ):
            chip = chip_ref[rows, :] + got_chip_ref[rows, :]
            far = far_ref[rows, :] + got_far_ref[rows, :]
            side_ref[at, 0, place] = jnp.where(odd, chip, far) * inside * factor
            side_ref[at, 1, place] = jnp.where(odd, far, chip) * factor
    copies = [pltpu.make_async_copy(side_ref.at[:, 1, 0:16], v_out.at[:, 3], sems.at[0])]
    copies[0].start()
    for slot, x in enumerate(ENDS):
        for lanes, other in strain_parts(layer_of(side_ref, slot)):
            parts = [parts_ref[at, slot, :, lanes] for at in range(6)]
            e = end_strains(parts, slot, lanes, [value[0:16] for value in other])
            bonds = [b_ref[at, slot, 0:16, lanes] for at in range(12)]
            for at, rate in enumerate(stress_rates(e, bonds[:6], bonds[6:])):
                end_ref[at, slot, :, lanes] = s_ref[at, slot, 0:16, lanes] + rate
        copies.append(
            pltpu.make_async_copy(end_ref.at[:, slot], s_out.at[:, x], sems.at[1 + slot])
        )
        copies[-1].start()
    for copy in copies:
        copy.wait()


def swap(x, axis, first):
    peers = lax.axis_size(axis)
    pairs = []
    for i in range(first, peers - 1, 2):
        pairs += [(i, i + 1), (i + 1, i)]
    return lax.ppermute(x, axis, pairs)


def swaps(pair, other, axis):
    second = swap(other, axis, 1)
    return swap(pair, axis, 0), second


def shards(
    velocity, stress, grain_ids, lattice_tilt, grain_orient, orientations, source_cells, source_signal
):
    plane = (ROWS, 512)
    edge, ends, pair_of = (3, *plane), (3, 2, *plane), (6, 2, *plane)
    sources = jnp.concatenate((source_cells.astype(jnp.float32), source_signal), axis=1)
    (sent,) = call(
        rotation_kernel,
        [(16, 48, 128)],
        (
            jnp.transpose(grain_ids, (1, 2, 0)),
            jnp.transpose(lattice_tilt, (0, 2, 3, 1)),
            grain_orient.reshape(32, 128),
            orientations,
        ),
        scratch=[(3, 256, 128)],
        flops=32768 * 200,
    )

    got = lax.all_to_all(sent, "span", 0, 0, tiled=True)

    half, s, pair, other = call(
        edge_kernel,
        [(3, 4, *plane), (6, 4, *plane), (144, 512), (144, 512)],
        (jnp.concatenate((stress, velocity)),),
    )
    pair, other = swaps(pair, other, "chord")
    v, s, chip, far = call(
        before_span_kernel,
        [(3, 4, *plane), (6, 4, *plane), edge, edge],
        (half, s, pair, other),
        aliases={0: 0, 1: 1},
        flops=32768 * 40000,
    )
    got_chip, got_far = swaps(chip, far, "span")
    v, e_mid, added = call(
        between_kernel,
        [(3, 3, *plane), pair_of, (14, *plane)],
        (sources, v, s),
        spaces={0: pltpu.SMEM},
    )

    pair, other = call(arrange_edge_kernel, [(40, 512), (40, 512)], (got,))
    pair, other = swaps(pair, other, "chord")
    (q,) = call(arrange_kernel, [(12, 16, 512)], (got,))

    v_last, e = call(
        after_span_kernel,
        [edge, pair_of],
        (v, added, chip, far, got_chip, got_far),
        scratch=[ends],
    )
    s_ends, bonds = call(
        first_own_kernel, [pair_of, (12, 2, *plane)], (e, s, q), flops=32768 * 100
    )
    s_ends, bonds, halo, chip, far = call(
        first_end_kernel,
        [pair_of, (12, 2, *plane), (6, 8, 512), edge, edge],
        (s_ends, bonds, v_last, e, s, pair, other, added),
        scratch=[(12, 8, 512)],
        aliases={0: 0, 1: 1},
    )
    got_chip, got_far = swaps(chip, far, "span")
    v, s, mid_bonds, part = call(
        first_middle_kernel,
        [(3, 3, *plane), pair_of, (12, 2, *plane), pair_of],
        (v, e_mid, s, s_ends, q, halo, added),
        scratch=[pair_of],
        flops=32768 * 100,
    )
    s_ends, chip, far = call(
        lambda *refs: end_kernel(False, *refs),
        [pair_of, edge, edge],
        (s_ends, part, bonds, chip, far, got_chip, got_far, added),
        scratch=[ends],
    )
    got_chip, got_far = swaps(chip, far, "span")
    v, s, part = call(
        middle_kernel,
        [(3, 3, *plane), pair_of, pair_of],
        (v, s_ends, s, mid_bonds, added),
        flops=32768 * 100,
    )
    s_ends, chip, far = call(
        lambda *refs: end_kernel(True, *refs),
        [pair_of, (56, 512), (56, 512)],
        (s_ends, part, bonds, chip, far, got_chip, got_far, added),
        scratch=[ends, edge, edge],
    )
    got_chip, got_far = swaps(chip, far, "span")
    v, s, part = call(
        last_middle_kernel,
        [velocity.shape, stress.shape, (6, 2, 16, 512)],
        (v, s_ends, s, mid_bonds, added),
        scratch=[(3, 3, *plane)],
        flops=32768 * 100,
    )
    v, s = pl.pallas_call(
        last_end_kernel,
        out_shape=[
            jax.ShapeDtypeStruct(velocity.shape, jnp.float32),
            jax.ShapeDtypeStruct(stress.shape, jnp.float32),
        ],
        in_specs=[pl.BlockSpec(memory_space=pl.ANY)] * 2 + [WHOLE] * 7,
        out_specs=[pl.BlockSpec(memory_space=pl.ANY)] * 2,
        scratch_shapes=[
            pltpu.VMEM(ends, jnp.float32),
            pltpu.VMEM((6, 2, 16, 512), jnp.float32),
            pltpu.SemaphoreType.DMA((3,)),
        ],
        input_output_aliases={0: 0, 1: 1},
        compiler_params=VMEM,
    )(v, s, s_ends, bonds, part, chip, far, got_chip, got_far)
    return v, s


def solution(mesh):
    return jax.shard_map(
        shards,
        mesh=mesh,
        in_specs=(
            P(None, "span", "chord", None),
            P(None, "span", "chord", None),
            P(None, "chord", "span"),
            P(None, None, "chord", "span"),
            P(),
            P(),
            P(),
            P(),
        ),
        out_specs=(P(None, "span", "chord", None), P(None, "span", "chord", None)),
        check_vma=False,
    )
```

```python
import jax
import jax.numpy as jnp
from jax import lax
from jax.experimental import pallas as pl
from jax.experimental.pallas import tpu as pltpu
from jax.sharding import PartitionSpec as P

normal_modulus = 0.9
cross_modulus = 1.6
shear_modulus = 1.3
time_step = 0.25
anisotropy = normal_modulus - 2.0 * shear_modulus

DEEP = 4
ROWS = 24
TABLE_ROWS = 11
VMEM = pltpu.CompilerParams(vmem_limit_bytes=16 * 2**20)
WHOLE = pl.BlockSpec(memory_space=pltpu.VMEM)
LANES = [slice(128 * at, 128 * at + 128) for at in range(4)]


def call(kernel, outs, operands, scratch=(), spaces=(), aliases=None, flops=0):
    spaces = dict(spaces)
    return pl.pallas_call(
        kernel,
        out_shape=[jax.ShapeDtypeStruct(shape, jnp.float32) for shape in outs],
        in_specs=[pl.BlockSpec(memory_space=spaces.get(at, pltpu.VMEM)) for at in range(len(operands))],
        out_specs=[WHOLE] * len(outs),
        scratch_shapes=[
            pltpu.VMEM(shape, jnp.float32) if isinstance(shape, tuple) else shape for shape in scratch
        ],
        input_output_aliases=aliases or {},
        compiler_params=VMEM,
        cost_estimate=pl.CostEstimate(
            flops=flops,
            bytes_accessed=4 * sum(operand.size for operand in operands),
            transcendentals=0,
        ),
    )(*operands)


def small_sin(x):
    y = x * x
    return x * (
        1.0 + y * (-1.0 / 6 + y * (1.0 / 120 + y * (-1.0 / 5040 + y * (1.0 / 362880))))
    )


def small_cos(x):
    y = x * x
    return 1.0 + y * (
        -0.5
        + y * (1.0 / 24 + y * (-1.0 / 720 + y * (1.0 / 40320 + y * (-1.0 / 3628800))))
    )


def wide_sin_cos(x):
    quarter = 0.25 * x
    s, c = small_sin(quarter), small_cos(quarter)
    s, c = 2.0 * s * c, 1.0 - 2.0 * s * s
    return 2.0 * s * c, 1.0 - 2.0 * s * s


def quaternion(first, middle, last, sin_cos):
    s_mid, c_mid = sin_cos(0.5 * middle)
    s_sum, c_sum = sin_cos(0.5 * (first + last))
    s_dif, c_dif = sin_cos(0.5 * (first - last))
    return c_mid * c_sum, -s_mid * c_dif, -s_mid * s_dif, -c_mid * s_sum


def product(a, b):
    return (
        a[0] * b[0] - a[1] * b[1] - a[2] * b[2] - a[3] * b[3],
        a[0] * b[1] + a[1] * b[0] + a[2] * b[3] - a[3] * b[2],
        a[0] * b[2] - a[1] * b[3] + a[2] * b[0] + a[3] * b[1],
        a[0] * b[3] + a[1] * b[2] - a[2] * b[1] + a[3] * b[0],
    )


def reduced(q):
    w, x, y, z = q
    aw, ax, ay, az = jnp.abs(w), jnp.abs(x), jnp.abs(y), jnp.abs(z)
    low, high = jnp.maximum(aw, ax), jnp.maximum(ay, az)
    upper = high > low
    second = jnp.where(upper, az - ay, ax - aw) > 0.0

    def pick(a, b, c, d):
        return jnp.where(upper, jnp.where(second, d, c), jnp.where(second, b, a))

    lead = pick(w, x, y, z)
    flip = jnp.where(lead < 0.0, -1.0, 1.0)
    return (
        pick(x, -w, z, -y) * flip,
        pick(y, -z, -w, x) * flip,
        pick(z, y, -x, -w) * flip,
    )


def look_up(row, lane):
    return jnp.take_along_axis(
        jnp.broadcast_to(row, lane.shape), lane, axis=1, mode="promise_in_bounds"
    )


LEVEL = 1 << 19
FINE = 0.75 / LEVEL


def coded(q):
    w, x, y, z = q
    aw, ax, ay, az = jnp.abs(w), jnp.abs(x), jnp.abs(y), jnp.abs(z)
    upper = jnp.maximum(ay, az) > jnp.maximum(aw, ax)
    second = jnp.where(upper, az - ay, ax - aw) > 0.0

    def pick(a, b, c, d):
        return jnp.where(upper, jnp.where(second, d, c), jnp.where(second, b, a))

    flip = jnp.where(pick(w, x, y, z) < 0.0, -1.0 / FINE, 1.0 / FINE)
    rest = (pick(x, w, w, w), pick(y, y, x, x), pick(z, z, z, y))
    a, b, c = [jnp.round(part * flip).astype(jnp.int32) + LEVEL for part in rest]
    return (
        a + ((b & 1023) << 20) + jnp.where(second, 1 << 30, 0),
        c + ((b >> 10) << 20) + jnp.where(upper, 1 << 30, 0),
    )


def decoded(one, two):
    mask = (1 << 20) - 1
    a = one & mask
    b = ((one >> 20) & 1023) | (((two >> 20) & 1023) << 10)
    c = two & mask
    a, b, c = [(part - LEVEL).astype(jnp.float32) * FINE for part in (a, b, c)]
    lead = jnp.sqrt(1.0 - a * a - b * b - c * c)
    second, upper = (one >> 30) > 0, (two >> 30) > 0

    def pick(w, x, y, z):
        return jnp.where(upper, jnp.where(second, z, y), jnp.where(second, x, w))

    return pick(lead, a, a, a), pick(a, lead, b, b), pick(b, b, lead, c), pick(c, c, c, lead)


def turned_parts(grain, angles, grain_ref, angle_ref):
    packed = []
    for at in range(TABLE_ROWS):
        row = grain_ref[at : at + 1, :] + grain_ref[at + 11 : at + 12, :] * 512
        if at + 22 < 32:
            row = row + grain_ref[at + 22 : at + 23, :] * (512 * 512)
        packed.append(row)
    table = coded(quaternion(*[angle_ref[at : at + 1, :] for at in range(3)], wide_sin_cos))
    third = jnp.where(grain >= 2816, 2, jnp.where(grain >= 1408, 1, 0))
    grain = grain - 1408 * third
    lane, place = grain & 127, grain >> 7
    entry = look_up(packed[0], lane)
    for at in range(1, TABLE_ROWS):
        entry = jnp.where(place == at, look_up(packed[at], lane), entry)
    entry = (entry >> (9 * third)) & 511
    lane, place = entry & 127, entry >> 7
    found = []
    for code in table:
        part = [code[:, lanes] for lanes in LANES]
        low = jnp.where(place == 1, look_up(part[1], lane), look_up(part[0], lane))
        high = jnp.where(place == 3, look_up(part[3], lane), look_up(part[2], lane))
        found.append(jnp.where(place >= 2, high, low))
    tilt_turn = quaternion(*angles, lambda x: (small_sin(x), small_cos(x)))
    return reduced(product(decoded(*found), tilt_turn))


def side_by_side(ref, *lead):
    *lead, chord = lead
    return jnp.concatenate([ref[(*lead, chord)], ref[(*lead, chord + 1)]], axis=1)


def rotation_kernel(ids_ref, tilt_ref, grain_ref, angle_ref, out_ref, sorted_ref):
    for pair in range(2):
        chords = [4 * group + 2 * pair for group in range(4)]

        def stacked(ref, *lead):
            return jnp.concatenate([side_by_side(ref, *lead, chord) for chord in chords], axis=0)

        values = turned_parts(
            stacked(ids_ref), [stacked(tilt_ref, at) for at in range(3)], grain_ref, angle_ref
        )
        for at in range(3):
            turned = values[at].T
            for half in range(2):
                sorted_ref[at, pl.ds(2 * pair + half, 64, stride=4), :] = turned[
                    64 * half : 64 * half + 64, :
                ]
    for device in range(16):
        for at in range(3):
            row = 16 * device
            out_ref[device, 16 * at : 16 * at + 16, :] = sorted_ref[at, row : row + 16, :]


def depth_parts(got_ref):
    for four, deep in enumerate(LANES):
        pieces = [got_ref[4 * four + at] for at in range(4)]

        def lanes_of(group):
            return jnp.concatenate(
                [piece[:, 32 * group : 32 * group + 32] for piece in pieces], axis=1
            )

        yield deep, lanes_of


def arrange_edge_kernel(got_ref, pair_ref, other_ref):
    def fill(ref, group, first):
        for deep, lanes_of in depth_parts(got_ref):
            lanes = lanes_of(group)
            for at in range(12):
                ref[3 * at : 3 * at + 3, deep] = lanes[4 * at + first : 4 * at + first + 3, :]
        blank(ref, 36)

    by_chord(lambda ref, low: fill(ref, *low), pair_ref, other_ref, (0, 0), (3, 1))


def arrange_kernel(got_ref, q_ref):
    for deep, lanes_of in depth_parts(got_ref):
        for group in range(4):
            lanes = lanes_of(group)
            for at in range(12):
                q_ref[at, 4 * group : 4 * group + 4, deep] = lanes[4 * at : 4 * at + 4, :]


def blank(ref, used):
    if ref.shape[0] > used:
        ref[used:, :] = jnp.zeros((ref.shape[0] - used, 512), jnp.float32)


def by_chord(fill, pair_ref, other_ref, low, high):
    even = lax.axis_index("chord") % 2 == 0

    @pl.when(even)
    def _():
        fill(pair_ref, high)
        fill(other_ref, low)

    @pl.when(jnp.logical_not(even))
    def _():
        fill(pair_ref, low)
        fill(other_ref, high)


def halo_by_chord(take, pair_ref, other_ref):
    even = lax.axis_index("chord") % 2 == 0

    @pl.when(even)
    def _():
        take(pair_ref, other_ref)

    @pl.when(jnp.logical_not(even))
    def _():
        take(other_ref, pair_ref)


SCALE = 0.25 * time_step


def lane_is(at):
    return lax.broadcasted_iota(jnp.int32, (ROWS, 128), 1) == at


def next_row(x):
    return pltpu.roll(x, ROWS - 1, 0)


def row_before(x):
    return pltpu.roll(x, 1, 0)


def strain_parts(load):
    first = lane_is(0)
    held = [0.0] * 3
    for lanes in LANES:
        sums, rows, deeps = [], [], []
        for at in range(3):
            value = load(at, lanes)
            rolled = pltpu.roll(value, 1, 1)
            earlier = jnp.where(first, held[at], rolled)
            held[at] = rolled
            total, change = value + earlier, value - earlier
            behind = row_before(total)
            sums.append(total + behind)
            rows.append(total - behind)
            deeps.append(change + row_before(change))
        yield lanes, (
            sums[0],
            rows[1],
            deeps[2],
            rows[2] + deeps[1],
            deeps[0] + sums[2],
            deeps[0] - sums[2],
            rows[0] + sums[1],
            rows[0] - sums[1],
        )


def strains(now, old):
    return (
        now[0] - old[0],
        now[1] + old[1],
        now[2] + old[2],
        now[3] + old[3],
        now[4] + old[5],
        now[6] + old[7],
    )


def force_parts(load, need=(True, True)):
    last = lane_is(127)
    held = [0.0] * 6
    for lanes in reversed(LANES):
        total, change = [], []
        for at in range(6):
            value = load(at, lanes)
            rolled = pltpu.roll(value, 127, 1)
            later = jnp.where(last, held[at], rolled)
            held[at] = rolled
            total.append(value + later)
            change.append(later - value)
        plus, minus = [], []
        for lead, side, deep in ((0, 5, 4), (5, 1, 3), (4, 3, 2)):
            ahead = total[lead] + next_row(total[lead])
            rest = next_row(total[side] + change[deep]) + (change[deep] - total[side])
            plus.append(rest + ahead if need[0] else None)
            minus.append(rest - ahead if need[1] else None)
        yield lanes, plus, minus


def stress_rates(e, first_bond, second_bond):
    trace = e[0] + e[1] + e[2]
    along = []
    for bond in (first_bond, second_bond):
        part = bond[0] * e[0]
        for at in range(1, 6):
            part = part + bond[at] * e[at]
        along.append(part)
    third = trace - along[0] - along[1]
    first_weight = (SCALE * anisotropy) * (along[0] - third)
    second_weight = (SCALE * anisotropy) * (along[1] - third)
    level = (SCALE * cross_modulus) * trace + (SCALE * anisotropy) * third
    rates = []
    for at in range(6):
        rate = first_bond[at] * first_weight + second_bond[at] * second_weight
        if at < 3:
            rate = rate + ((2.0 * SCALE * shear_modulus) * e[at] + level)
        else:
            rate = rate + (SCALE * shear_modulus) * e[at]
        rates.append(rate)
    return rates


def bonds_of(a, b, c):
    w = jnp.sqrt(jnp.maximum(1.0 - a * a - b * b - c * c, 0.0))
    ab, ac, bc = a * b, a * c, b * c
    wa, wb, wc = w * a, w * b, w * c
    aa, bb, cc = a * a, b * b, c * c
    bonds = []
    for p, q, r in (
        (1.0 - 2.0 * (bb + cc), 2.0 * (ab + wc), 2.0 * (ac - wb)),
        (2.0 * (ab - wc), 1.0 - 2.0 * (aa + cc), 2.0 * (bc + wa)),
    ):
        bonds += [p * p, q * q, r * r, q * r, r * p, p * q]
    return bonds


def outer_scale(outside_low, outside_high):
    row = lax.broadcasted_iota(jnp.int32, (8, 128), 0)
    outside = ((row < DEEP) & outside_high) | ((row >= DEEP) & outside_low)
    return jnp.where(outside, 0.0, 1.0)


def put(ref, lead, lanes, value, outer):
    ref[(*lead, slice(0, 16), lanes)] = value[0:16]
    ref[(*lead, slice(16, ROWS), lanes)] = value[16:ROWS] * outer


NOW = (0, 1, 2, 3, 4, 6)
OLD = (0, 1, 2, 3, 5, 7)


def push_three(loads, old, new, outer):
    for layers in zip(*[force_parts(load, (x > 0, x < 3)) for x, load in enumerate(loads)]):
        lanes = layers[0][0]
        for x in range(3):
            for at in range(3):
                force = layers[x + 1][1][at] + layers[x][2][at]
                put(new, (at, x), lanes, old(at, x, lanes) + SCALE * force, outer)


def whole_rows(ref, at, lanes, value):
    ref[at, :, lanes] = value


def some_rows(runs):
    count = sum(stop - start for start, stop in runs)

    def store(ref, at, lanes, value):
        ref[16 * at : 16 * at + 16, lanes] = value[0:16]
        row = 48 + count * at
        for start, stop in runs:
            ref[row : row + stop - start, lanes] = value[start:stop]
            row += stop - start

    return store


MOST = ((16, 18), (21, 24))
LAST = ((23, 24),)


def send_parts(first, last, high, added, chip_ref, far_ref, store=whole_rows):
    odd = span_odd()
    for (lanes, plus, _), (_, _, minus) in zip(
        force_parts(first, (True, False)), force_parts(last, (False, True))
    ):
        for at in range(3):
            low = SCALE * plus[at]
            value = high(at, lanes) + SCALE * minus[at]
            if added is not None and at == 2:
                value = value + added(lanes)
            store(chip_ref, at, lanes, jnp.where(odd, low, value))
            store(far_ref, at, lanes, jnp.where(odd, value, low))


def take_rows(chip_ref, far_ref, got_chip_ref, got_far_ref, side_ref, runs):
    odd = span_odd()
    inside = jnp.where(lax.axis_index("span") == 0, 0.0, 1.0)
    low_row = jnp.where(lax.axis_index("chord") == 0, 0.0, 1.0)
    count = sum(stop - start for start, stop in runs)
    for at in range(3):
        side_ref[at, :, 16:ROWS] = jnp.zeros((2, 8, 512), jnp.float32)
        row, places = 48 + count * at, [(16 * at, 0, 16)]
        for start, stop in runs:
            places.append((row, start, stop))
            row += stop - start
        for row, start, stop in places:
            rows, factor = slice(row, row + stop - start), low_row if start > 20 else 1.0
            chip = chip_ref[rows, :] + got_chip_ref[rows, :]
            far = far_ref[rows, :] + got_far_ref[rows, :]
            side_ref[at, 0, start:stop] = jnp.where(odd, chip, far) * (inside * factor)
            side_ref[at, 1, start:stop] = jnp.where(odd, far, chip) * factor


def take_parts(chip_ref, far_ref, got_chip_ref, got_far_ref, side_ref, added_ref=None):
    odd = span_odd()
    outer = rows_scale()[1]
    inside = jnp.where(lax.axis_index("span") == 0, 0.0, 1.0)
    for lanes in LANES:
        for at in range(3):
            chip = chip_ref[at, :, lanes] + got_chip_ref[at, :, lanes]
            far = far_ref[at, :, lanes] + got_far_ref[at, :, lanes]
            low, high = jnp.where(odd, chip, far), jnp.where(odd, far, chip)
            if added_ref is not None and at == 2:
                low, high = low + added_ref[0, :, lanes], high + added_ref[1, :, lanes]
            put(side_ref, (at, 0), lanes, low * inside, outer)
            put(side_ref, (at, 1), lanes, high, outer)


def strain(e, bonds, old, new, lead, lanes, outer, factor=None):
    for at, rate in enumerate(stress_rates(e, bonds[:6], bonds[6:])):
        if factor is not None:
            rate = rate * factor
        put(new, (at, lead), lanes, old(at) + rate, outer)


def layer_of(ref, x):
    return lambda at, lanes: ref[at, x, :, lanes]


def plane_of(ref, first=0):
    return lambda at, lanes: ref[first + at, :, lanes]


def span_odd():
    return lax.axis_index("span") % 2 == 1


def rows_scale():
    chord = lax.axis_index("chord")
    return outer_scale(False, chord == 7), outer_scale(chord == 0, False)


def edge_kernel(field_ref, v_out, s_out, pair_ref, other_ref):
    for at in range(9):
        if at < 6:
            s_out[at, :, 0:16] = field_ref[at]
        else:
            v_out[at - 6, :, 0:16] = field_ref[at]

    def fill(ref, first):
        rows = slice(first, first + DEEP)
        for at in range(9):
            for x in range(4):
                row = 16 * at + 4 * x
                ref[row : row + 4, :] = field_ref[at, x, rows]
        blank(ref, 144)

    by_chord(fill, pair_ref, other_ref, 0, 16 - DEEP)


def spot(sources_ref, at):
    layer = sources_ref[at, 0].astype(jnp.int32) - 4 * lax.axis_index("span")
    chord = sources_ref[at, 1].astype(jnp.int32) - 16 * lax.axis_index("chord")
    return layer, chord, sources_ref[at, 2].astype(jnp.int32)


def add_at(ref, lead, chord, deep, amount):
    row = jnp.where(chord < 0, chord + ROWS, chord)
    rows = pl.ds(pl.multiple_of((row // 8) * 8, 8), 8)
    lanes = pl.ds(pl.multiple_of((deep // 128) * 128, 128), 128)
    hit = (lax.broadcasted_iota(jnp.int32, (8, 128), 0) == row % 8) & (
        lax.broadcasted_iota(jnp.int32, (8, 128), 1) == deep % 128
    )
    ref[(*lead, rows, lanes)] = ref[(*lead, rows, lanes)] + jnp.where(hit, amount, 0.0)


def before_span_kernel(v_ref, s_ref, pair_ref, other_ref, v_out, s_out, chip_ref, far_ref):
    def take(next_ref, prior_ref):
        for at in range(9):
            out, slot = (s_out, at) if at < 6 else (v_out, at - 6)
            for x in range(4):
                row = 16 * at + 4 * x
                out[slot, x, 16 : 16 + DEEP] = next_ref[row : row + 4, :]
                out[slot, x, 16 + DEEP : ROWS] = prior_ref[row : row + 4, :]

    halo_by_chord(take, pair_ref, other_ref)
    send_parts(layer_of(s_out, 0), layer_of(s_out, 3), layer_of(v_out, 3), None, chip_ref, far_ref)


def between_kernel(sources_ref, v_ref, s_ref, v_out, e_out, added_ref):
    for at in range(14):
        added_ref[at] = jnp.zeros((ROWS, 512), jnp.float32)
    outer = rows_scale()[1]
    loads = [layer_of(s_ref, x) for x in range(4)]
    push_three(loads, lambda at, x, lanes: v_ref[at, x, :, lanes], v_out, outer)
    for at in range(16):
        layer, chord, deep = spot(sources_ref, at)
        inside = (chord >= -DEEP) & (chord < 16 + DEEP)

        @pl.when(inside & ((layer == -1) | (layer == 3)))
        def _():
            slot = jnp.where(layer == -1, 0, 1)
            add_at(added_ref, (slot,), chord, deep, sources_ref[at, 3])

        @pl.when(inside & (layer >= 0) & (layer < 3))
        def _():
            add_at(v_out, (2, layer), chord, deep, sources_ref[at, 3])

        @pl.when(inside & (layer >= 0) & (layer < 4))
        def _():
            for step_at in range(1, 4):
                add_at(
                    added_ref, (slot_of(step_at, layer),), chord, deep, sources_ref[at, 3 + step_at]
                )

    for layers in zip(*[strain_parts(layer_of(v_out, x)) for x in range(3)]):
        lanes = layers[0][0]
        for x in range(2):
            for at, value in enumerate(strains(layers[x + 1][1], layers[x][1])):
                e_out[at, x, :, lanes] = value


def after_span_kernel(
    v_ref, added_ref, chip_ref, far_ref, got_chip_ref, got_far_ref, v_out, e_out, side_ref
):
    take_parts(chip_ref, far_ref, got_chip_ref, got_far_ref, side_ref, added_ref)
    for at in range(3):
        v_out[at] = side_ref[at, 1]
    loads = (layer_of(side_ref, 0), layer_of(v_ref, 0), layer_of(v_ref, 2), layer_of(side_ref, 1))
    for layers in zip(*[strain_parts(load) for load in loads]):
        lanes = layers[0][0]
        for slot in range(2):
            for at, value in enumerate(strains(layers[2 * slot + 1][1], layers[2 * slot][1])):
                e_out[at, slot, :, lanes] = value


def slot_of(step_at, layer):
    return 4 * step_at - 2 + layer


def first_stress(x, slot, rows, lanes, q, e_ref, index, s_ref, b_out):
    bonds = bonds_of(*q)
    for at, value in enumerate(bonds):
        b_out[at, slot, rows, lanes] = value
    e = [e_ref[at, index, rows, lanes] for at in range(6)]
    rates = stress_rates(e, bonds[:6], bonds[6:])
    return [s_ref[at, x, rows, lanes] + rates[at] for at in range(6)]


ENDS = (0, 3)


def first_own_kernel(e_ref, s_ref, q_ref, s_out, b_out):
    for lanes in LANES:
        for slot, x in enumerate(ENDS):
            for rows in (slice(0, 8), slice(8, 16)):
                q = [q_ref[4 * at + x, rows, lanes] for at in range(3)]
                new = first_stress(x, slot, rows, lanes, q, e_ref, slot, s_ref, b_out)
                for at in range(6):
                    s_out[at, slot, rows, lanes] = new[at]


def first_end_kernel(
    s_held, b_held, v_last_ref, e_ref, s_ref, pair_ref, other_ref, added_ref,
    s_out, b_out, q_out, chip_ref, far_ref, halo_ref,
):
    halo_ref[...] = jnp.zeros(halo_ref.shape, jnp.float32)

    def take(next_ref, prior_ref):
        for at in range(12):
            halo_ref[at, 0:3] = next_ref[3 * at : 3 * at + 3]
            halo_ref[at, 5:8] = prior_ref[3 * at : 3 * at + 3]

    halo_by_chord(take, pair_ref, other_ref)
    outer_s = rows_scale()[0]
    rows = slice(16, ROWS)
    for at in range(3):
        q_out[2 * at] = halo_ref[4 * at + 1]
        q_out[2 * at + 1] = halo_ref[4 * at + 2]
    for lanes in LANES:
        for slot, x in enumerate(ENDS):
            q = [halo_ref[4 * at + x, :, lanes] for at in range(3)]
            new = first_stress(x, slot, rows, lanes, q, e_ref, slot, s_ref, b_out)
            for at in range(6):
                s_out[at, slot, rows, lanes] = new[at] * outer_s
    added = lambda lanes: added_ref[slot_of(1, 3), :, lanes]
    store = some_rows(MOST)
    blank(far_ref, 63)
    send_parts(
        layer_of(s_out, 0), layer_of(s_out, 1), plane_of(v_last_ref), added, chip_ref, far_ref, store
    )


def middle(v_ref, s_ends_ref, s_mid, added_ref, step_at, bond_of, v_out, s_out, parts_out, rows=ROWS):
    outer_s, outer_v = rows_scale()
    loads = [layer_of(s_ends_ref, 0), s_mid(0), s_mid(1), layer_of(s_ends_ref, 1)]

    def old(at, x, lanes):
        value = v_ref[at, x, :, lanes]
        return value + added_ref[slot_of(step_at, x), :, lanes] if at == 2 else value

    push_three(loads, old, v_out, outer_v)
    for layers in zip(*[strain_parts(layer_of(v_out, x)) for x in range(3)]):
        lanes = layers[0][0]
        for at in range(6):
            parts_out[at, 0, :, lanes] = layers[0][1][NOW[at]][0:rows]
            parts_out[at, 1, :, lanes] = layers[2][1][OLD[at]][0:rows]
        for x in range(2):
            e = strains(layers[x + 1][1], layers[x][1])
            before = lambda at: s_mid(x)(at, lanes)
            if rows == ROWS:
                strain(e, bond_of(x, lanes), before, s_out, x, lanes, outer_s)
            else:
                bonds = [bond[0:rows] for bond in bond_of(x, lanes)]
                e = [value[0:rows] for value in e]
                for at, rate in enumerate(stress_rates(e, bonds[:6], bonds[6:])):
                    s_out[at, 1 + x, :, lanes] = before(at)[0:rows] + rate


def first_middle_kernel(
    v_ref, e_ref, s_ref, s_ends_ref, q_ref, halo_ref, added_ref,
    v_out, s_out, b_out, parts_out, stress_ref,
):
    outer_s, _ = rows_scale()
    for lanes in LANES:
        for x in range(2):
            for rows in (slice(0, 8), slice(8, 16), slice(16, ROWS)):
                own = rows.start < 16
                q = [
                    q_ref[4 * at + 1 + x, rows, lanes] if own else halo_ref[2 * at + x, :, lanes]
                    for at in range(3)
                ]
                new = first_stress(1 + x, x, rows, lanes, q, e_ref, x, s_ref, b_out)
                for at in range(6):
                    stress_ref[at, x, rows, lanes] = new[at] if own else new[at] * outer_s
    bond_of = lambda x, lanes: [b_out[at, x, :, lanes] for at in range(12)]
    s_mid = lambda x: layer_of(stress_ref, x)
    middle(v_ref, s_ends_ref, s_mid, added_ref, 1, bond_of, v_out, s_out, parts_out)


def middle_kernel(v_ref, s_ends_ref, s_ref, b_ref, added_ref, v_out, s_out, parts_out):
    bond_of = lambda x, lanes: [b_ref[at, x, :, lanes] for at in range(12)]
    s_mid = lambda x: layer_of(s_ref, x)
    middle(v_ref, s_ends_ref, s_mid, added_ref, 2, bond_of, v_out, s_out, parts_out)


def last_middle_kernel(
    v_ref, s_ends_ref, s_ref, b_ref, added_ref, v_out, s_out, parts_out, moved_ref
):
    bond_of = lambda x, lanes: [b_ref[at, x, :, lanes] for at in range(12)]
    s_mid = lambda x: layer_of(s_ref, x)
    middle(v_ref, s_ends_ref, s_mid, added_ref, 3, bond_of, moved_ref, s_out, parts_out, 16)
    for at in range(3):
        v_out[at, 0:3] = moved_ref[at, :, 0:16]


def end_strains(parts, slot, lanes, other):
    if slot == 0:
        return [parts[0] - other[0]] + [parts[at] + other[OLD[at]] for at in range(1, 6)]
    return [other[0] - parts[0]] + [other[NOW[at]] + parts[at] for at in range(1, 6)]


def end_kernel(
    last, s_ends_ref, parts_ref, b_ref, chip_ref, far_ref, got_chip_ref, got_far_ref, added_ref,
    s_out, next_chip_ref, next_far_ref, side_ref,
):
    take_rows(chip_ref, far_ref, got_chip_ref, got_far_ref, side_ref, MOST)
    outer_s = rows_scale()[0]
    for layers in zip(*[strain_parts(layer_of(side_ref, slot)) for slot in range(2)]):
        lanes = layers[0][0]
        for slot in range(2):
            parts = [parts_ref[at, slot, :, lanes] for at in range(6)]
            e = end_strains(parts, slot, lanes, layers[slot][1])
            bonds = [b_ref[at, slot, :, lanes] for at in range(12)]
            old = lambda at: s_ends_ref[at, slot, :, lanes]
            strain(e, bonds, old, s_out, slot, lanes, outer_s)
    added = lambda lanes: added_ref[slot_of(3 if last else 2, 3), :, lanes]
    first, second, high = layer_of(s_out, 0), layer_of(s_out, 1), layer_of(side_ref, 1)
    store = some_rows(LAST if last else MOST)
    blank(next_far_ref, 51 if last else 63)
    send_parts(first, second, high, added, next_chip_ref, next_far_ref, store)


def last_end_kernel(
    v_held, s_held, s_ref, b_ref, parts_ref, chip_ref, far_ref, got_chip_ref, got_far_ref,
    v_out, s_out, side_ref, end_ref, sems,
):
    take_rows(chip_ref, far_ref, got_chip_ref, got_far_ref, side_ref, LAST)
    copies = [pltpu.make_async_copy(side_ref.at[:, 1, 0:16], v_out.at[:, 3], sems.at[0])]
    copies[0].start()
    for slot, x in enumerate(ENDS):
        for lanes, other in strain_parts(layer_of(side_ref, slot)):
            parts = [parts_ref[at, slot, :, lanes] for at in range(6)]
            e = end_strains(parts, slot, lanes, [value[0:16] for value in other])
            bonds = [b_ref[at, slot, 0:16, lanes] for at in range(12)]
            for at, rate in enumerate(stress_rates(e, bonds[:6], bonds[6:])):
                end_ref[at, slot, :, lanes] = s_ref[at, slot, 0:16, lanes] + rate
        copies.append(
            pltpu.make_async_copy(end_ref.at[:, slot], s_out.at[:, x], sems.at[1 + slot])
        )
        copies[-1].start()
    for copy in copies:
        copy.wait()


def swap(x, axis, first):
    peers = lax.axis_size(axis)
    pairs = []
    for i in range(first, peers - 1, 2):
        pairs += [(i, i + 1), (i + 1, i)]
    return lax.ppermute(x, axis, pairs)


def swaps(pair, other, axis):
    second = swap(other, axis, 1)
    return swap(pair, axis, 0), second


def shards(
    velocity, stress, grain_ids, lattice_tilt, grain_orient, orientations, source_cells, source_signal
):
    plane = (ROWS, 512)
    edge, ends, pair_of = (3, *plane), (3, 2, *plane), (6, 2, *plane)
    sources = jnp.concatenate((source_cells.astype(jnp.float32), source_signal), axis=1)
    (sent,) = call(
        rotation_kernel,
        [(16, 48, 128)],
        (
            jnp.transpose(grain_ids, (1, 2, 0)),
            jnp.transpose(lattice_tilt, (0, 2, 3, 1)),
            grain_orient.reshape(32, 128),
            orientations,
        ),
        scratch=[(3, 256, 128)],
        flops=32768 * 200,
    )

    got = lax.all_to_all(sent, "span", 0, 0, tiled=True)

    half, s, pair, other = call(
        edge_kernel,
        [(3, 4, *plane), (6, 4, *plane), (144, 512), (152, 512)],
        (jnp.concatenate((stress, velocity)),),
    )
    pair, other = swaps(pair, other, "chord")
    v, s, chip, far = call(
        before_span_kernel,
        [(3, 4, *plane), (6, 4, *plane), edge, edge],
        (half, s, pair, other),
        aliases={0: 0, 1: 1},
        flops=32768 * 40000,
    )
    got_chip, got_far = swaps(chip, far, "span")
    v, e_mid, added = call(
        between_kernel,
        [(3, 3, *plane), pair_of, (14, *plane)],
        (sources, v, s),
        spaces={0: pltpu.SMEM},
    )

    pair, other = call(arrange_edge_kernel, [(36, 512), (56, 512)], (got,))
    pair, other = swaps(pair, other, "chord")
    (q,) = call(arrange_kernel, [(12, 16, 512)], (got,))

    v_last, e = call(
        after_span_kernel,
        [edge, pair_of],
        (v, added, chip, far, got_chip, got_far),
        scratch=[ends],
    )
    s_ends, bonds = call(
        first_own_kernel, [pair_of, (12, 2, *plane)], (e, s, q), flops=32768 * 100
    )
    s_ends, bonds, halo, chip, far = call(
        first_end_kernel,
        [pair_of, (12, 2, *plane), (6, 8, 512), (63, 512), (64, 512)],
        (s_ends, bonds, v_last, e, s, pair, other, added),
        scratch=[(12, 8, 512)],
        aliases={0: 0, 1: 1},
    )
    got_chip, got_far = swaps(chip, far, "span")
    v, s, mid_bonds, part = call(
        first_middle_kernel,
        [(3, 3, *plane), pair_of, (12, 2, *plane), pair_of],
        (v, e_mid, s, s_ends, q, halo, added),
        scratch=[pair_of],
        flops=32768 * 100,
    )
    s_ends, chip, far = call(
        lambda *refs: end_kernel(False, *refs),
        [pair_of, (63, 512), (64, 512)],
        (s_ends, part, bonds, chip, far, got_chip, got_far, added),
        scratch=[ends],
    )
    got_chip, got_far = swaps(chip, far, "span")
    v, s, part = call(
        middle_kernel,
        [(3, 3, *plane), pair_of, pair_of],
        (v, s_ends, s, mid_bonds, added),
        flops=32768 * 100,
    )
    s_ends, chip, far = call(
        lambda *refs: end_kernel(True, *refs),
        [pair_of, (51, 512), (56, 512)],
        (s_ends, part, bonds, chip, far, got_chip, got_far, added),
        scratch=[ends],
    )
    got_chip, got_far = swaps(chip, far, "span")
    v, s, part = call(
        last_middle_kernel,
        [velocity.shape, stress.shape, (6, 2, 16, 512)],
        (v, s_ends, s, mid_bonds, added),
        scratch=[(3, 3, *plane)],
        flops=32768 * 100,
    )
    v, s = pl.pallas_call(
        last_end_kernel,
        out_shape=[
            jax.ShapeDtypeStruct(velocity.shape, jnp.float32),
            jax.ShapeDtypeStruct(stress.shape, jnp.float32),
        ],
        in_specs=[pl.BlockSpec(memory_space=pl.ANY)] * 2 + [WHOLE] * 7,
        out_specs=[pl.BlockSpec(memory_space=pl.ANY)] * 2,
        scratch_shapes=[
            pltpu.VMEM(ends, jnp.float32),
            pltpu.VMEM((6, 2, 16, 512), jnp.float32),
            pltpu.SemaphoreType.DMA((3,)),
        ],
        input_output_aliases={0: 0, 1: 1},
        compiler_params=VMEM,
    )(v, s, s_ends, bonds, part, chip, far, got_chip, got_far)
    return v, s


def solution(mesh):
    return jax.shard_map(
        shards,
        mesh=mesh,
        in_specs=(
            P(None, "span", "chord", None),
            P(None, "span", "chord", None),
            P(None, "chord", "span"),
            P(None, None, "chord", "span"),
            P(),
            P(),
            P(),
            P(),
        ),
        out_specs=(P(None, "span", "chord", None), P(None, "span", "chord", None)),
        check_vma=False,
    )
```

```python
import jax
import jax.numpy as jnp
from jax import lax
from jax.experimental import pallas as pl
from jax.experimental.pallas import tpu as pltpu
from jax.sharding import PartitionSpec as P

normal_modulus = 0.9
cross_modulus = 1.6
shear_modulus = 1.3
time_step = 0.25
anisotropy = normal_modulus - 2.0 * shear_modulus

DEEP = 4
ROWS = 24
TABLE_ROWS = 11
VMEM = pltpu.CompilerParams(vmem_limit_bytes=16 * 2**20)
WHOLE = pl.BlockSpec(memory_space=pltpu.VMEM)
LANES = [slice(128 * at, 128 * at + 128) for at in range(4)]


def call(kernel, outs, operands, scratch=(), spaces=(), aliases=None, flops=0):
    spaces = dict(spaces)
    return pl.pallas_call(
        kernel,
        out_shape=[jax.ShapeDtypeStruct(shape, jnp.float32) for shape in outs],
        in_specs=[pl.BlockSpec(memory_space=spaces.get(at, pltpu.VMEM)) for at in range(len(operands))],
        out_specs=[WHOLE] * len(outs),
        scratch_shapes=[
            pltpu.VMEM(shape, jnp.float32) if isinstance(shape, tuple) else shape for shape in scratch
        ],
        input_output_aliases=aliases or {},
        compiler_params=VMEM,
        cost_estimate=pl.CostEstimate(
            flops=flops,
            bytes_accessed=4 * sum(operand.size for operand in operands),
            transcendentals=0,
        ),
    )(*operands)


def small_sin(x):
    y = x * x
    return x * (
        1.0 + y * (-1.0 / 6 + y * (1.0 / 120 + y * (-1.0 / 5040 + y * (1.0 / 362880))))
    )


def small_cos(x):
    y = x * x
    return 1.0 + y * (
        -0.5
        + y * (1.0 / 24 + y * (-1.0 / 720 + y * (1.0 / 40320 + y * (-1.0 / 3628800))))
    )


def wide_sin_cos(x):
    quarter = 0.25 * x
    s, c = small_sin(quarter), small_cos(quarter)
    s, c = 2.0 * s * c, 1.0 - 2.0 * s * s
    return 2.0 * s * c, 1.0 - 2.0 * s * s


def quaternion(first, middle, last, sin_cos):
    s_mid, c_mid = sin_cos(0.5 * middle)
    s_sum, c_sum = sin_cos(0.5 * (first + last))
    s_dif, c_dif = sin_cos(0.5 * (first - last))
    return c_mid * c_sum, -s_mid * c_dif, -s_mid * s_dif, -c_mid * s_sum


def product(a, b):
    return (
        a[0] * b[0] - a[1] * b[1] - a[2] * b[2] - a[3] * b[3],
        a[0] * b[1] + a[1] * b[0] + a[2] * b[3] - a[3] * b[2],
        a[0] * b[2] - a[1] * b[3] + a[2] * b[0] + a[3] * b[1],
        a[0] * b[3] + a[1] * b[2] - a[2] * b[1] + a[3] * b[0],
    )


def reduced(q):
    w, x, y, z = q
    aw, ax, ay, az = jnp.abs(w), jnp.abs(x), jnp.abs(y), jnp.abs(z)
    low, high = jnp.maximum(aw, ax), jnp.maximum(ay, az)
    upper = high > low
    second = jnp.where(upper, az - ay, ax - aw) > 0.0

    def pick(a, b, c, d):
        return jnp.where(upper, jnp.where(second, d, c), jnp.where(second, b, a))

    lead = pick(w, x, y, z)
    flip = jnp.where(lead < 0.0, -1.0, 1.0)
    return (
        pick(x, -w, z, -y) * flip,
        pick(y, -z, -w, x) * flip,
        pick(z, y, -x, -w) * flip,
    )


def look_up(row, lane):
    return jnp.take_along_axis(
        jnp.broadcast_to(row, lane.shape), lane, axis=1, mode="promise_in_bounds"
    )


LEVEL = 1 << 19
FINE = 0.75 / LEVEL


def coded(q):
    w, x, y, z = q
    aw, ax, ay, az = jnp.abs(w), jnp.abs(x), jnp.abs(y), jnp.abs(z)
    upper = jnp.maximum(ay, az) > jnp.maximum(aw, ax)
    second = jnp.where(upper, az - ay, ax - aw) > 0.0

    def pick(a, b, c, d):
        return jnp.where(upper, jnp.where(second, d, c), jnp.where(second, b, a))

    flip = jnp.where(pick(w, x, y, z) < 0.0, -1.0 / FINE, 1.0 / FINE)
    rest = (pick(x, w, w, w), pick(y, y, x, x), pick(z, z, z, y))
    a, b, c = [jnp.round(part * flip).astype(jnp.int32) + LEVEL for part in rest]
    return (
        a + ((b & 1023) << 20) + jnp.where(second, 1 << 30, 0),
        c + ((b >> 10) << 20) + jnp.where(upper, 1 << 30, 0),
    )


def decoded(one, two):
    mask = (1 << 20) - 1
    a = one & mask
    b = ((one >> 20) & 1023) | (((two >> 20) & 1023) << 10)
    c = two & mask
    a, b, c = [(part - LEVEL).astype(jnp.float32) * FINE for part in (a, b, c)]
    lead = jnp.sqrt(1.0 - a * a - b * b - c * c)
    second, upper = (one >> 30) > 0, (two >> 30) > 0

    def pick(w, x, y, z):
        return jnp.where(upper, jnp.where(second, z, y), jnp.where(second, x, w))

    return pick(lead, a, a, a), pick(a, lead, b, b), pick(b, b, lead, c), pick(c, c, c, lead)


def turned_parts(grain, angles, grain_ref, angle_ref):
    packed = []
    for at in range(TABLE_ROWS):
        row = grain_ref[at : at + 1, :] + grain_ref[at + 11 : at + 12, :] * 512
        if at + 22 < 32:
            row = row + grain_ref[at + 22 : at + 23, :] * (512 * 512)
        packed.append(row)
    table = coded(quaternion(*[angle_ref[at : at + 1, :] for at in range(3)], wide_sin_cos))
    third = jnp.where(grain >= 2816, 2, jnp.where(grain >= 1408, 1, 0))
    grain = grain - 1408 * third
    lane, place = grain & 127, grain >> 7
    entry = look_up(packed[0], lane)
    for at in range(1, TABLE_ROWS):
        entry = jnp.where(place == at, look_up(packed[at], lane), entry)
    entry = (entry >> (9 * third)) & 511
    lane, place = entry & 127, entry >> 7
    found = []
    for code in table:
        part = [code[:, lanes] for lanes in LANES]
        low = jnp.where(place == 1, look_up(part[1], lane), look_up(part[0], lane))
        high = jnp.where(place == 3, look_up(part[3], lane), look_up(part[2], lane))
        found.append(jnp.where(place >= 2, high, low))
    tilt_turn = quaternion(*angles, lambda x: (small_sin(x), small_cos(x)))
    return reduced(product(decoded(*found), tilt_turn))


def side_by_side(ref, *lead):
    *lead, chord = lead
    return jnp.concatenate([ref[(*lead, chord)], ref[(*lead, chord + 1)]], axis=1)


def rotation_kernel(ids_ref, tilt_ref, grain_ref, angle_ref, out_ref, sorted_ref):
    for pair in range(2):
        chords = [4 * group + 2 * pair for group in range(4)]

        def stacked(ref, *lead):
            return jnp.concatenate([side_by_side(ref, *lead, chord) for chord in chords], axis=0)

        values = turned_parts(
            stacked(ids_ref), [stacked(tilt_ref, at) for at in range(3)], grain_ref, angle_ref
        )
        for at in range(3):
            turned = values[at].T
            for half in range(2):
                sorted_ref[at, pl.ds(2 * pair + half, 64, stride=4), :] = turned[
                    64 * half : 64 * half + 64, :
                ]
    for device in range(16):
        for at in range(3):
            row = 16 * device
            out_ref[device, 16 * at : 16 * at + 16, :] = sorted_ref[at, row : row + 16, :]


def depth_parts(got_ref):
    for four, deep in enumerate(LANES):
        pieces = [got_ref[4 * four + at] for at in range(4)]

        def lanes_of(group):
            return jnp.concatenate(
                [piece[:, 32 * group : 32 * group + 32] for piece in pieces], axis=1
            )

        yield deep, lanes_of


def arrange_edge_kernel(got_ref, pair_ref, other_ref):
    def fill(ref, group, first):
        for deep, lanes_of in depth_parts(got_ref):
            lanes = lanes_of(group)
            for at in range(12):
                ref[3 * at : 3 * at + 3, deep] = lanes[4 * at + first : 4 * at + first + 3, :]
        blank(ref, 36)

    by_chord(lambda ref, low: fill(ref, *low), pair_ref, other_ref, (0, 0), (3, 1))


def arrange_kernel(got_ref, q_ref):
    for deep, lanes_of in depth_parts(got_ref):
        for group in range(4):
            lanes = lanes_of(group)
            for at in range(12):
                q_ref[at, 4 * group : 4 * group + 4, deep] = lanes[4 * at : 4 * at + 4, :]


def blank(ref, used):
    if ref.shape[0] > used:
        ref[used:, :] = jnp.zeros((ref.shape[0] - used, 512), jnp.float32)


def by_chord(fill, pair_ref, other_ref, low, high):
    even = lax.axis_index("chord") % 2 == 0

    @pl.when(even)
    def _():
        fill(pair_ref, high)
        fill(other_ref, low)

    @pl.when(jnp.logical_not(even))
    def _():
        fill(pair_ref, low)
        fill(other_ref, high)


def halo_by_chord(take, pair_ref, other_ref):
    even = lax.axis_index("chord") % 2 == 0

    @pl.when(even)
    def _():
        take(pair_ref, other_ref)

    @pl.when(jnp.logical_not(even))
    def _():
        take(other_ref, pair_ref)


SCALE = 0.25 * time_step


def lane_is(at):
    return lax.broadcasted_iota(jnp.int32, (ROWS, 128), 1) == at


def next_row(x):
    return pltpu.roll(x, ROWS - 1, 0)


def row_before(x):
    return pltpu.roll(x, 1, 0)


def strain_parts(load):
    first = lane_is(0)
    held = [0.0] * 3
    for lanes in LANES:
        sums, rows, deeps = [], [], []
        for at in range(3):
            value = load(at, lanes)
            rolled = pltpu.roll(value, 1, 1)
            earlier = jnp.where(first, held[at], rolled)
            held[at] = rolled
            total, change = value + earlier, value - earlier
            behind = row_before(total)
            sums.append(total + behind)
            rows.append(total - behind)
            deeps.append(change + row_before(change))
        yield lanes, (
            sums[0],
            rows[1],
            deeps[2],
            rows[2] + deeps[1],
            deeps[0] + sums[2],
            deeps[0] - sums[2],
            rows[0] + sums[1],
            rows[0] - sums[1],
        )


def strains(now, old):
    return (
        now[0] - old[0],
        now[1] + old[1],
        now[2] + old[2],
        now[3] + old[3],
        now[4] + old[5],
        now[6] + old[7],
    )


def force_parts(load, need=(True, True)):
    last = lane_is(127)
    held = [0.0] * 6
    for lanes in reversed(LANES):
        total, change = [], []
        for at in range(6):
            value = load(at, lanes)
            rolled = pltpu.roll(value, 127, 1)
            later = jnp.where(last, held[at], rolled)
            held[at] = rolled
            total.append(value + later)
            change.append(later - value)
        plus, minus = [], []
        for lead, side, deep in ((0, 5, 4), (5, 1, 3), (4, 3, 2)):
            ahead = total[lead] + next_row(total[lead])
            rest = next_row(total[side] + change[deep]) + (change[deep] - total[side])
            plus.append(rest + ahead if need[0] else None)
            minus.append(rest - ahead if need[1] else None)
        yield lanes, plus, minus


def stress_rates(e, first_bond, second_bond):
    trace = e[0] + e[1] + e[2]
    along = []
    for bond in (first_bond, second_bond):
        part = bond[0] * e[0]
        for at in range(1, 6):
            part = part + bond[at] * e[at]
        along.append(part)
    third = trace - along[0] - along[1]
    first_weight = (SCALE * anisotropy) * (along[0] - third)
    second_weight = (SCALE * anisotropy) * (along[1] - third)
    level = (SCALE * cross_modulus) * trace + (SCALE * anisotropy) * third
    rates = []
    for at in range(6):
        rate = first_bond[at] * first_weight + second_bond[at] * second_weight
        if at < 3:
            rate = rate + ((2.0 * SCALE * shear_modulus) * e[at] + level)
        else:
            rate = rate + (SCALE * shear_modulus) * e[at]
        rates.append(rate)
    return rates


def bonds_of(a, b, c):
    w = jnp.sqrt(jnp.maximum(1.0 - a * a - b * b - c * c, 0.0))
    ab, ac, bc = a * b, a * c, b * c
    wa, wb, wc = w * a, w * b, w * c
    aa, bb, cc = a * a, b * b, c * c
    bonds = []
    for p, q, r in (
        (1.0 - 2.0 * (bb + cc), 2.0 * (ab + wc), 2.0 * (ac - wb)),
        (2.0 * (ab - wc), 1.0 - 2.0 * (aa + cc), 2.0 * (bc + wa)),
    ):
        bonds += [p * p, q * q, r * r, q * r, r * p, p * q]
    return bonds


def outer_scale(outside_low, outside_high):
    row = lax.broadcasted_iota(jnp.int32, (8, 128), 0)
    outside = ((row < DEEP) & outside_high) | ((row >= DEEP) & outside_low)
    return jnp.where(outside, 0.0, 1.0)


def put(ref, lead, lanes, value, outer):
    ref[(*lead, slice(0, 16), lanes)] = value[0:16]
    ref[(*lead, slice(16, ROWS), lanes)] = value[16:ROWS] * outer


NOW = (0, 1, 2, 3, 4, 6)
OLD = (0, 1, 2, 3, 5, 7)


def push_three(loads, old, new, outer):
    for layers in zip(*[force_parts(load, (x > 0, x < 3)) for x, load in enumerate(loads)]):
        lanes = layers[0][0]
        for x in range(3):
            for at in range(3):
                force = layers[x + 1][1][at] + layers[x][2][at]
                put(new, (at, x), lanes, old(at, x, lanes) + SCALE * force, outer)


def whole_rows(ref, at, lanes, value):
    ref[at, :, lanes] = value


def some_rows(runs):
    count = sum(stop - start for start, stop in runs)

    def store(ref, at, lanes, value):
        ref[16 * at : 16 * at + 16, lanes] = value[0:16]
        row = 48 + count * at
        for start, stop in runs:
            ref[row : row + stop - start, lanes] = value[start:stop]
            row += stop - start

    return store


MOST = ((16, 18), (21, 24))
LAST = ((23, 24),)


def send_parts(first, last, high, added, chip_ref, far_ref, store=whole_rows):
    odd = span_odd()
    for (lanes, plus, _), (_, _, minus) in zip(
        force_parts(first, (True, False)), force_parts(last, (False, True))
    ):
        for at in range(3):
            low = SCALE * plus[at]
            value = high(at, lanes) + SCALE * minus[at]
            if added is not None and at == 2:
                value = value + added(lanes)
            store(chip_ref, at, lanes, jnp.where(odd, low, value))
            store(far_ref, at, lanes, jnp.where(odd, value, low))


def take_rows(chip_ref, far_ref, got_chip_ref, got_far_ref, side_ref, runs):
    odd = span_odd()
    inside = jnp.where(lax.axis_index("span") == 0, 0.0, 1.0)
    low_row = jnp.where(lax.axis_index("chord") == 0, 0.0, 1.0)
    count = sum(stop - start for start, stop in runs)
    for at in range(3):
        side_ref[at, :, 16:ROWS] = jnp.zeros((2, 8, 512), jnp.float32)
        row, places = 48 + count * at, [(16 * at, 0, 16)]
        for start, stop in runs:
            places.append((row, start, stop))
            row += stop - start
        for row, start, stop in places:
            rows, factor = slice(row, row + stop - start), low_row if start > 20 else 1.0
            chip = chip_ref[rows, :] + got_chip_ref[rows, :]
            far = far_ref[rows, :] + got_far_ref[rows, :]
            side_ref[at, 0, start:stop] = jnp.where(odd, chip, far) * (inside * factor)
            side_ref[at, 1, start:stop] = jnp.where(odd, far, chip) * factor


def take_parts(chip_ref, far_ref, got_chip_ref, got_far_ref, side_ref, added_ref=None):
    odd = span_odd()
    outer = rows_scale()[1]
    inside = jnp.where(lax.axis_index("span") == 0, 0.0, 1.0)
    for lanes in LANES:
        for at in range(3):
            chip = chip_ref[at, :, lanes] + got_chip_ref[at, :, lanes]
            far = far_ref[at, :, lanes] + got_far_ref[at, :, lanes]
            low, high = jnp.where(odd, chip, far), jnp.where(odd, far, chip)
            if added_ref is not None and at == 2:
                low, high = low + added_ref[0, :, lanes], high + added_ref[1, :, lanes]
            put(side_ref, (at, 0), lanes, low * inside, outer)
            put(side_ref, (at, 1), lanes, high, outer)


def strain(e, bonds, old, new, lead, lanes, outer, factor=None):
    for at, rate in enumerate(stress_rates(e, bonds[:6], bonds[6:])):
        if factor is not None:
            rate = rate * factor
        put(new, (at, lead), lanes, old(at) + rate, outer)


def layer_of(ref, x):
    return lambda at, lanes: ref[at, x, :, lanes]


def plane_of(ref, first=0):
    return lambda at, lanes: ref[first + at, :, lanes]


def span_odd():
    return lax.axis_index("span") % 2 == 1


def rows_scale():
    chord = lax.axis_index("chord")
    return outer_scale(False, chord == 7), outer_scale(chord == 0, False)


def edge_kernel(field_ref, v_out, s_out, pair_ref, other_ref):
    for at in range(9):
        if at < 6:
            s_out[at, :, 0:16] = field_ref[at]
        else:
            v_out[at - 6, :, 0:16] = field_ref[at]

    def fill(ref, first):
        rows = slice(first, first + DEEP)
        for at in range(9):
            for x in range(4):
                row = 16 * at + 4 * x
                ref[row : row + 4, :] = field_ref[at, x, rows]
        blank(ref, 144)

    by_chord(fill, pair_ref, other_ref, 0, 16 - DEEP)


def spot(sources_ref, at):
    layer = sources_ref[at, 0].astype(jnp.int32) - 4 * lax.axis_index("span")
    chord = sources_ref[at, 1].astype(jnp.int32) - 16 * lax.axis_index("chord")
    return layer, chord, sources_ref[at, 2].astype(jnp.int32)


def add_at(ref, lead, chord, deep, amount):
    row = jnp.where(chord < 0, chord + ROWS, chord)
    rows = pl.ds(pl.multiple_of((row // 8) * 8, 8), 8)
    lanes = pl.ds(pl.multiple_of((deep // 128) * 128, 128), 128)
    hit = (lax.broadcasted_iota(jnp.int32, (8, 128), 0) == row % 8) & (
        lax.broadcasted_iota(jnp.int32, (8, 128), 1) == deep % 128
    )
    ref[(*lead, rows, lanes)] = ref[(*lead, rows, lanes)] + jnp.where(hit, amount, 0.0)


def before_span_kernel(v_ref, s_ref, pair_ref, other_ref, v_out, s_out, chip_ref, far_ref):
    def take(next_ref, prior_ref):
        for at in range(9):
            out, slot = (s_out, at) if at < 6 else (v_out, at - 6)
            for x in range(4):
                row = 16 * at + 4 * x
                out[slot, x, 16 : 16 + DEEP] = next_ref[row : row + 4, :]
                out[slot, x, 16 + DEEP : ROWS] = prior_ref[row : row + 4, :]

    halo_by_chord(take, pair_ref, other_ref)
    send_parts(layer_of(s_out, 0), layer_of(s_out, 3), layer_of(v_out, 3), None, chip_ref, far_ref)


def between_kernel(sources_ref, v_ref, s_ref, v_out, e_out, added_ref):
    for at in range(14):
        added_ref[at] = jnp.zeros((ROWS, 512), jnp.float32)
    outer = rows_scale()[1]
    loads = [layer_of(s_ref, x) for x in range(4)]
    push_three(loads, lambda at, x, lanes: v_ref[at, x, :, lanes], v_out, outer)
    for at in range(16):
        layer, chord, deep = spot(sources_ref, at)
        inside = (chord >= -DEEP) & (chord < 16 + DEEP)

        @pl.when(inside & ((layer == -1) | (layer == 3)))
        def _():
            slot = jnp.where(layer == -1, 0, 1)
            add_at(added_ref, (slot,), chord, deep, sources_ref[at, 3])

        @pl.when(inside & (layer >= 0) & (layer < 3))
        def _():
            add_at(v_out, (2, layer), chord, deep, sources_ref[at, 3])

        @pl.when(inside & (layer >= 0) & (layer < 4))
        def _():
            for step_at in range(1, 4):
                add_at(
                    added_ref, (slot_of(step_at, layer),), chord, deep, sources_ref[at, 3 + step_at]
                )

    for layers in zip(*[strain_parts(layer_of(v_out, x)) for x in range(3)]):
        lanes = layers[0][0]
        for x in range(2):
            for at, value in enumerate(strains(layers[x + 1][1], layers[x][1])):
                e_out[at, x, :, lanes] = value


def after_span_kernel(
    v_ref, added_ref, chip_ref, far_ref, got_chip_ref, got_far_ref, v_out, e_out, side_ref
):
    take_parts(chip_ref, far_ref, got_chip_ref, got_far_ref, side_ref, added_ref)
    for at in range(3):
        v_out[at] = side_ref[at, 1]
    loads = (layer_of(side_ref, 0), layer_of(v_ref, 0), layer_of(v_ref, 2), layer_of(side_ref, 1))
    for layers in zip(*[strain_parts(load) for load in loads]):
        lanes = layers[0][0]
        for slot in range(2):
            for at, value in enumerate(strains(layers[2 * slot + 1][1], layers[2 * slot][1])):
                e_out[at, slot, :, lanes] = value


def slot_of(step_at, layer):
    return 4 * step_at - 2 + layer


def first_stress(x, slot, rows, lanes, q, e_ref, index, s_ref, b_out):
    bonds = bonds_of(*q)
    for at, value in enumerate(bonds):
        b_out[at, slot, rows, lanes] = value
    e = [e_ref[at, index, rows, lanes] for at in range(6)]
    rates = stress_rates(e, bonds[:6], bonds[6:])
    return [s_ref[at, x, rows, lanes] + rates[at] for at in range(6)]


ENDS = (0, 3)


def first_own_kernel(e_ref, s_ref, q_ref, s_out, b_out):
    for lanes in LANES:
        for slot, x in enumerate(ENDS):
            for rows in (slice(0, 8), slice(8, 16)):
                q = [q_ref[4 * at + x, rows, lanes] for at in range(3)]
                new = first_stress(x, slot, rows, lanes, q, e_ref, slot, s_ref, b_out)
                for at in range(6):
                    s_out[at, slot, rows, lanes] = new[at]


def first_end_kernel(
    s_held, b_held, v_last_ref, e_ref, s_ref, pair_ref, other_ref, added_ref,
    s_out, b_out, q_out, chip_ref, far_ref, halo_ref,
):
    halo_ref[...] = jnp.zeros(halo_ref.shape, jnp.float32)

    def take(next_ref, prior_ref):
        for at in range(12):
            halo_ref[at, 0:3] = next_ref[3 * at : 3 * at + 3]
            halo_ref[at, 5:8] = prior_ref[3 * at : 3 * at + 3]

    halo_by_chord(take, pair_ref, other_ref)
    outer_s = rows_scale()[0]
    rows = slice(16, ROWS)
    for at in range(3):
        q_out[2 * at] = halo_ref[4 * at + 1]
        q_out[2 * at + 1] = halo_ref[4 * at + 2]
    for lanes in LANES:
        for slot, x in enumerate(ENDS):
            q = [halo_ref[4 * at + x, :, lanes] for at in range(3)]
            new = first_stress(x, slot, rows, lanes, q, e_ref, slot, s_ref, b_out)
            for at in range(6):
                s_out[at, slot, rows, lanes] = new[at] * outer_s
    added = lambda lanes: added_ref[slot_of(1, 3), :, lanes]
    store = some_rows(MOST)
    blank(far_ref, 63)
    send_parts(
        layer_of(s_out, 0), layer_of(s_out, 1), plane_of(v_last_ref), added, chip_ref, far_ref, store
    )


def middle(v_ref, ends, s_mid, added_ref, step_at, bond_of, v_out, s_out, parts_out, rows=ROWS):
    outer_s, outer_v = rows_scale()
    loads = [ends[0], s_mid(0), s_mid(1), ends[1]]

    def old(at, x, lanes):
        value = v_ref[at, x, :, lanes]
        return value + added_ref[slot_of(step_at, x), :, lanes] if at == 2 else value

    push_three(loads, old, v_out, outer_v)
    for layers in zip(*[strain_parts(layer_of(v_out, x)) for x in range(3)]):
        lanes = layers[0][0]
        for at in range(6):
            parts_out[at, 0, :, lanes] = layers[0][1][NOW[at]][0:rows]
            parts_out[at, 1, :, lanes] = layers[2][1][OLD[at]][0:rows]
        for x in range(2):
            e = strains(layers[x + 1][1], layers[x][1])
            before = lambda at: s_mid(x)(at, lanes)
            if rows == ROWS:
                strain(e, bond_of(x, lanes), before, s_out, x, lanes, outer_s)
            else:
                bonds = [bond[0:rows] for bond in bond_of(x, lanes)]
                e = [value[0:rows] for value in e]
                for at, rate in enumerate(stress_rates(e, bonds[:6], bonds[6:])):
                    s_out[at, 1 + x, :, lanes] = before(at)[0:rows] + rate


def first_middle_kernel(
    v_ref, e_ref, s_ref, s_ends_ref, q_ref, halo_ref, added_ref,
    v_out, s_out, b_out, parts_out, stress_ref,
):
    outer_s, _ = rows_scale()
    for lanes in LANES:
        for x in range(2):
            for rows in (slice(0, 8), slice(8, 16), slice(16, ROWS)):
                own = rows.start < 16
                q = [
                    q_ref[4 * at + 1 + x, rows, lanes] if own else halo_ref[2 * at + x, :, lanes]
                    for at in range(3)
                ]
                new = first_stress(1 + x, x, rows, lanes, q, e_ref, x, s_ref, b_out)
                for at in range(6):
                    stress_ref[at, x, rows, lanes] = new[at] if own else new[at] * outer_s
    bond_of = lambda x, lanes: [b_out[at, x, :, lanes] for at in range(12)]
    s_mid = lambda x: layer_of(stress_ref, x)
    ends = layer_of(s_ends_ref, 0), layer_of(s_ends_ref, 1)
    middle(v_ref, ends, s_mid, added_ref, 1, bond_of, v_out, s_out, parts_out)


def middle_kernel(v_ref, s_chip_ref, s_far_ref, s_ref, b_ref, added_ref, v_out, s_out, parts_out):
    bond_of = lambda x, lanes: [b_ref[at, x, :, lanes] for at in range(12)]
    s_mid = lambda x: layer_of(s_ref, x)
    ends = end_layers(s_chip_ref, s_far_ref)
    middle(v_ref, ends, s_mid, added_ref, 2, bond_of, v_out, s_out, parts_out)


def last_middle_kernel(
    v_ref, s_chip_ref, s_far_ref, s_ref, b_ref, added_ref, v_out, s_out, parts_out, moved_ref
):
    bond_of = lambda x, lanes: [b_ref[at, x, :, lanes] for at in range(12)]
    s_mid = lambda x: layer_of(s_ref, x)
    ends = end_layers(s_chip_ref, s_far_ref)
    middle(v_ref, ends, s_mid, added_ref, 3, bond_of, moved_ref, s_out, parts_out, 16)
    for at in range(3):
        v_out[at, 0:3] = moved_ref[at, :, 0:16]


def end_strains(parts, slot, lanes, other):
    if slot == 0:
        return [parts[0] - other[0]] + [parts[at] + other[OLD[at]] for at in range(1, 6)]
    return [other[0] - parts[0]] + [other[NOW[at]] + parts[at] for at in range(1, 6)]


def end_layers(chip_ref, far_ref):
    odd = span_odd()
    low = lambda at, lanes: jnp.where(odd, chip_ref[at, :, lanes], far_ref[at, :, lanes])
    high = lambda at, lanes: jnp.where(odd, far_ref[at, :, lanes], chip_ref[at, :, lanes])
    return low, high


def end_kernel(
    chip_side, first, last, s_ref, parts_ref, b_ref, sent_ref, got_ref, added_ref,
    s_out, next_ref, side_ref,
):
    outer_s = rows_scale()[0]
    low_row = jnp.where(lax.axis_index("chord") == 0, 0.0, 1.0)
    inside = jnp.where(lax.axis_index("span") == 0, 0.0, 1.0)
    store = some_rows(LAST if last else MOST)
    blank(next_ref, 51 if last else 63)

    def work(slot):
        for at in range(3):
            side_ref[at, 16:ROWS] = jnp.zeros((8, 512), jnp.float32)
            row, places = 48 + 5 * at, [(16 * at, 0, 16)]
            for start, stop in MOST:
                places.append((row, start, stop))
                row += stop - start
            for row, start, stop in places:
                rows, factor = slice(row, row + stop - start), low_row if start > 20 else 1.0
                factor = factor * inside if slot == 0 else factor
                side_ref[at, start:stop] = (sent_ref[rows, :] + got_ref[rows, :]) * factor
        for lanes, other in strain_parts(plane_of(side_ref)):
            e = end_strains([parts_ref[at, slot, :, lanes] for at in range(6)], slot, lanes, other)
            bonds = [b_ref[at, slot, :, lanes] for at in range(12)]
            for at, rate in enumerate(stress_rates(e, bonds[:6], bonds[6:])):
                value = (s_ref[at, slot, :, lanes] if first else s_ref[at, :, lanes]) + rate
                put(s_out, (at,), lanes, value, outer_s)
        for lanes, plus, minus in force_parts(plane_of(s_out), (slot == 0, slot == 1)):
            for at in range(3):
                if slot == 0:
                    value = SCALE * plus[at]
                else:
                    value = side_ref[at, :, lanes] + SCALE * minus[at]
                    if at == 2:
                        value = value + added_ref[slot_of(3 if last else 2, 3), :, lanes]
                store(next_ref, at, lanes, value)

    low = span_odd() if chip_side else jnp.logical_not(span_odd())

    @pl.when(low)
    def _():
        work(0)

    @pl.when(jnp.logical_not(low))
    def _():
        work(1)


def last_end_kernel(
    v_held, s_held, s_chip_ref, s_far_ref, b_ref, parts_ref, chip_ref, far_ref, got_chip_ref, got_far_ref,
    v_out, s_out, side_ref, end_ref, sems,
):
    take_rows(chip_ref, far_ref, got_chip_ref, got_far_ref, side_ref, LAST)
    ends = end_layers(s_chip_ref, s_far_ref)
    copies = [pltpu.make_async_copy(side_ref.at[:, 1, 0:16], v_out.at[:, 3], sems.at[0])]
    copies[0].start()
    for slot, x in enumerate(ENDS):
        for lanes, other in strain_parts(layer_of(side_ref, slot)):
            parts = [parts_ref[at, slot, :, lanes] for at in range(6)]
            e = end_strains(parts, slot, lanes, [value[0:16] for value in other])
            bonds = [b_ref[at, slot, 0:16, lanes] for at in range(12)]
            for at, rate in enumerate(stress_rates(e, bonds[:6], bonds[6:])):
                end_ref[at, slot, :, lanes] = ends[slot](at, lanes)[0:16] + rate
        copies.append(
            pltpu.make_async_copy(end_ref.at[:, slot], s_out.at[:, x], sems.at[1 + slot])
        )
        copies[-1].start()
    for copy in copies:
        copy.wait()


def swap(x, axis, first):
    peers = lax.axis_size(axis)
    pairs = []
    for i in range(first, peers - 1, 2):
        pairs += [(i, i + 1), (i + 1, i)]
    return lax.ppermute(x, axis, pairs)


def swaps(pair, other, axis):
    second = swap(other, axis, 1)
    return swap(pair, axis, 0), second


def shards(
    velocity, stress, grain_ids, lattice_tilt, grain_orient, orientations, source_cells, source_signal
):
    plane = (ROWS, 512)
    edge, ends, pair_of = (3, *plane), (3, 2, *plane), (6, 2, *plane)
    sources = jnp.concatenate((source_cells.astype(jnp.float32), source_signal), axis=1)
    (sent,) = call(
        rotation_kernel,
        [(16, 48, 128)],
        (
            jnp.transpose(grain_ids, (1, 2, 0)),
            jnp.transpose(lattice_tilt, (0, 2, 3, 1)),
            grain_orient.reshape(32, 128),
            orientations,
        ),
        scratch=[(3, 256, 128)],
        flops=32768 * 200,
    )

    got = lax.all_to_all(sent, "span", 0, 0, tiled=True)

    half, s, pair, other = call(
        edge_kernel,
        [(3, 4, *plane), (6, 4, *plane), (144, 512), (152, 512)],
        (jnp.concatenate((stress, velocity)),),
    )
    pair, other = swaps(pair, other, "chord")
    v, s, chip, far = call(
        before_span_kernel,
        [(3, 4, *plane), (6, 4, *plane), edge, edge],
        (half, s, pair, other),
        aliases={0: 0, 1: 1},
        flops=32768 * 40000,
    )
    got_chip, got_far = swaps(chip, far, "span")
    v, e_mid, added = call(
        between_kernel,
        [(3, 3, *plane), pair_of, (14, *plane)],
        (sources, v, s),
        spaces={0: pltpu.SMEM},
    )

    pair, other = call(arrange_edge_kernel, [(36, 512), (56, 512)], (got,))
    pair, other = swaps(pair, other, "chord")
    (q,) = call(arrange_kernel, [(12, 16, 512)], (got,))

    v_last, e = call(
        after_span_kernel,
        [edge, pair_of],
        (v, added, chip, far, got_chip, got_far),
        scratch=[ends],
    )
    s_ends, bonds = call(
        first_own_kernel, [pair_of, (12, 2, *plane)], (e, s, q), flops=32768 * 100
    )
    s_ends, bonds, halo, chip, far = call(
        first_end_kernel,
        [pair_of, (12, 2, *plane), (6, 8, 512), (63, 512), (64, 512)],
        (s_ends, bonds, v_last, e, s, pair, other, added),
        scratch=[(12, 8, 512)],
        aliases={0: 0, 1: 1},
    )
    got_chip, got_far = swaps(chip, far, "span")
    v, s, mid_bonds, part = call(
        first_middle_kernel,
        [(3, 3, *plane), pair_of, (12, 2, *plane), pair_of],
        (v, e_mid, s, s_ends, q, halo, added),
        scratch=[pair_of],
        flops=32768 * 100,
    )
    s_chip, chip = call(
        lambda *refs: end_kernel(True, True, False, *refs),
        [(6, *plane), (63, 512)],
        (s_ends, part, bonds, chip, got_chip, added),
        scratch=[edge],
    )
    s_far, far = call(
        lambda *refs: end_kernel(False, True, False, *refs),
        [(6, *plane), (64, 512)],
        (s_ends, part, bonds, far, got_far, added),
        scratch=[edge],
    )
    got_chip, got_far = swaps(chip, far, "span")
    v, s, part = call(
        middle_kernel,
        [(3, 3, *plane), pair_of, pair_of],
        (v, s_chip, s_far, s, mid_bonds, added),
        flops=32768 * 100,
    )
    s_chip, chip = call(
        lambda *refs: end_kernel(True, False, True, *refs),
        [(6, *plane), (51, 512)],
        (s_chip, part, bonds, chip, got_chip, added),
        scratch=[edge],
    )
    s_far, far = call(
        lambda *refs: end_kernel(False, False, True, *refs),
        [(6, *plane), (56, 512)],
        (s_far, part, bonds, far, got_far, added),
        scratch=[edge],
    )
    got_chip, got_far = swaps(chip, far, "span")
    v, s, part = call(
        last_middle_kernel,
        [velocity.shape, stress.shape, (6, 2, 16, 512)],
        (v, s_chip, s_far, s, mid_bonds, added),
        scratch=[(3, 3, *plane)],
        flops=32768 * 100,
    )
    v, s = pl.pallas_call(
        last_end_kernel,
        out_shape=[
            jax.ShapeDtypeStruct(velocity.shape, jnp.float32),
            jax.ShapeDtypeStruct(stress.shape, jnp.float32),
        ],
        in_specs=[pl.BlockSpec(memory_space=pl.ANY)] * 2 + [WHOLE] * 8,
        out_specs=[pl.BlockSpec(memory_space=pl.ANY)] * 2,
        scratch_shapes=[
            pltpu.VMEM(ends, jnp.float32),
            pltpu.VMEM((6, 2, 16, 512), jnp.float32),
            pltpu.SemaphoreType.DMA((3,)),
        ],
        input_output_aliases={0: 0, 1: 1},
        compiler_params=VMEM,
    )(v, s, s_chip, s_far, bonds, part, chip, far, got_chip, got_far)
    return v, s


def solution(mesh):
    return jax.shard_map(
        shards,
        mesh=mesh,
        in_specs=(
            P(None, "span", "chord", None),
            P(None, "span", "chord", None),
            P(None, "chord", "span"),
            P(None, None, "chord", "span"),
            P(),
            P(),
            P(),
            P(),
        ),
        out_specs=(P(None, "span", "chord", None), P(None, "span", "chord", None)),
        check_vma=False,
    )
```

```python
import jax
import jax.numpy as jnp
from jax import lax
from jax.experimental import pallas as pl
from jax.experimental.pallas import tpu as pltpu
from jax.sharding import PartitionSpec as P

normal_modulus = 0.9
cross_modulus = 1.6
shear_modulus = 1.3
time_step = 0.25
anisotropy = normal_modulus - 2.0 * shear_modulus

DEEP = 4
ROWS = 24
TABLE_ROWS = 11
VMEM = pltpu.CompilerParams(vmem_limit_bytes=16 * 2**20)
WHOLE = pl.BlockSpec(memory_space=pltpu.VMEM)
LANES = [slice(128 * at, 128 * at + 128) for at in range(4)]


def call(kernel, outs, operands, scratch=(), spaces=(), aliases=None, flops=0):
    spaces = dict(spaces)
    return pl.pallas_call(
        kernel,
        out_shape=[jax.ShapeDtypeStruct(shape, jnp.float32) for shape in outs],
        in_specs=[pl.BlockSpec(memory_space=spaces.get(at, pltpu.VMEM)) for at in range(len(operands))],
        out_specs=[WHOLE] * len(outs),
        scratch_shapes=[
            pltpu.VMEM(shape, jnp.float32) if isinstance(shape, tuple) else shape for shape in scratch
        ],
        input_output_aliases=aliases or {},
        compiler_params=VMEM,
        cost_estimate=pl.CostEstimate(
            flops=flops,
            bytes_accessed=4 * sum(operand.size for operand in operands),
            transcendentals=0,
        ),
    )(*operands)


def small_sin(x):
    y = x * x
    return x * (
        1.0 + y * (-1.0 / 6 + y * (1.0 / 120 + y * (-1.0 / 5040 + y * (1.0 / 362880))))
    )


def small_cos(x):
    y = x * x
    return 1.0 + y * (
        -0.5
        + y * (1.0 / 24 + y * (-1.0 / 720 + y * (1.0 / 40320 + y * (-1.0 / 3628800))))
    )


def wide_sin_cos(x):
    quarter = 0.25 * x
    s, c = small_sin(quarter), small_cos(quarter)
    s, c = 2.0 * s * c, 1.0 - 2.0 * s * s
    return 2.0 * s * c, 1.0 - 2.0 * s * s


def quaternion(first, middle, last, sin_cos):
    s_mid, c_mid = sin_cos(0.5 * middle)
    s_sum, c_sum = sin_cos(0.5 * (first + last))
    s_dif, c_dif = sin_cos(0.5 * (first - last))
    return c_mid * c_sum, -s_mid * c_dif, -s_mid * s_dif, -c_mid * s_sum


def product(a, b):
    return (
        a[0] * b[0] - a[1] * b[1] - a[2] * b[2] - a[3] * b[3],
        a[0] * b[1] + a[1] * b[0] + a[2] * b[3] - a[3] * b[2],
        a[0] * b[2] - a[1] * b[3] + a[2] * b[0] + a[3] * b[1],
        a[0] * b[3] + a[1] * b[2] - a[2] * b[1] + a[3] * b[0],
    )


def reduced(q):
    w, x, y, z = q
    aw, ax, ay, az = jnp.abs(w), jnp.abs(x), jnp.abs(y), jnp.abs(z)
    low, high = jnp.maximum(aw, ax), jnp.maximum(ay, az)
    upper = high > low
    second = jnp.where(upper, az - ay, ax - aw) > 0.0

    def pick(a, b, c, d):
        return jnp.where(upper, jnp.where(second, d, c), jnp.where(second, b, a))

    lead = pick(w, x, y, z)
    flip = jnp.where(lead < 0.0, -1.0, 1.0)
    return (
        pick(x, -w, z, -y) * flip,
        pick(y, -z, -w, x) * flip,
        pick(z, y, -x, -w) * flip,
    )


def look_up(row, lane):
    return jnp.take_along_axis(
        jnp.broadcast_to(row, lane.shape), lane, axis=1, mode="promise_in_bounds"
    )


LEVEL = 1 << 19
FINE = 0.75 / LEVEL


def coded(q):
    w, x, y, z = q
    aw, ax, ay, az = jnp.abs(w), jnp.abs(x), jnp.abs(y), jnp.abs(z)
    upper = jnp.maximum(ay, az) > jnp.maximum(aw, ax)
    second = jnp.where(upper, az - ay, ax - aw) > 0.0

    def pick(a, b, c, d):
        return jnp.where(upper, jnp.where(second, d, c), jnp.where(second, b, a))

    flip = jnp.where(pick(w, x, y, z) < 0.0, -1.0 / FINE, 1.0 / FINE)
    rest = (pick(x, w, w, w), pick(y, y, x, x), pick(z, z, z, y))
    a, b, c = [jnp.round(part * flip).astype(jnp.int32) + LEVEL for part in rest]
    return (
        a + ((b & 1023) << 20) + jnp.where(second, 1 << 30, 0),
        c + ((b >> 10) << 20) + jnp.where(upper, 1 << 30, 0),
    )


def decoded(one, two):
    mask = (1 << 20) - 1
    a = one & mask
    b = ((one >> 20) & 1023) | (((two >> 20) & 1023) << 10)
    c = two & mask
    a, b, c = [(part - LEVEL).astype(jnp.float32) * FINE for part in (a, b, c)]
    lead = jnp.sqrt(1.0 - a * a - b * b - c * c)
    second, upper = (one >> 30) > 0, (two >> 30) > 0

    def pick(w, x, y, z):
        return jnp.where(upper, jnp.where(second, z, y), jnp.where(second, x, w))

    return pick(lead, a, a, a), pick(a, lead, b, b), pick(b, b, lead, c), pick(c, c, c, lead)


def turned_parts(grain, angles, grain_ref, angle_ref):
    packed = []
    for at in range(TABLE_ROWS):
        row = grain_ref[at : at + 1, :] + grain_ref[at + 11 : at + 12, :] * 512
        if at + 22 < 32:
            row = row + grain_ref[at + 22 : at + 23, :] * (512 * 512)
        packed.append(row)
    table = coded(quaternion(*[angle_ref[at : at + 1, :] for at in range(3)], wide_sin_cos))
    third = jnp.where(grain >= 2816, 2, jnp.where(grain >= 1408, 1, 0))
    grain = grain - 1408 * third
    lane, place = grain & 127, grain >> 7
    entry = look_up(packed[0], lane)
    for at in range(1, TABLE_ROWS):
        entry = jnp.where(place == at, look_up(packed[at], lane), entry)
    entry = (entry >> (9 * third)) & 511
    lane, place = entry & 127, entry >> 7
    found = []
    for code in table:
        part = [code[:, lanes] for lanes in LANES]
        low = jnp.where(place == 1, look_up(part[1], lane), look_up(part[0], lane))
        high = jnp.where(place == 3, look_up(part[3], lane), look_up(part[2], lane))
        found.append(jnp.where(place >= 2, high, low))
    tilt_turn = quaternion(*angles, lambda x: (small_sin(x), small_cos(x)))
    return reduced(product(decoded(*found), tilt_turn))


def side_by_side(ref, *lead):
    *lead, chord = lead
    return jnp.concatenate([ref[(*lead, chord)], ref[(*lead, chord + 1)]], axis=1)


def rotation_kernel(ids_ref, tilt_ref, grain_ref, angle_ref, out_ref, sorted_ref):
    for pair in range(2):
        chords = [4 * group + 2 * pair for group in range(4)]

        def stacked(ref, *lead):
            return jnp.concatenate([side_by_side(ref, *lead, chord) for chord in chords], axis=0)

        values = turned_parts(
            stacked(ids_ref), [stacked(tilt_ref, at) for at in range(3)], grain_ref, angle_ref
        )
        for at in range(3):
            turned = values[at].T
            for half in range(2):
                sorted_ref[at, pl.ds(2 * pair + half, 64, stride=4), :] = turned[
                    64 * half : 64 * half + 64, :
                ]
    for device in range(16):
        for at in range(3):
            row = 16 * device
            out_ref[device, 16 * at : 16 * at + 16, :] = sorted_ref[at, row : row + 16, :]


def depth_parts(got_ref):
    for four, deep in enumerate(LANES):
        pieces = [got_ref[4 * four + at] for at in range(4)]

        def lanes_of(group):
            return jnp.concatenate(
                [piece[:, 32 * group : 32 * group + 32] for piece in pieces], axis=1
            )

        yield deep, lanes_of


def arrange_edge_kernel(got_ref, pair_ref, other_ref):
    def fill(ref, group, first):
        for deep, lanes_of in depth_parts(got_ref):
            lanes = lanes_of(group)
            for at in range(12):
                ref[3 * at : 3 * at + 3, deep] = lanes[4 * at + first : 4 * at + first + 3, :]
        blank(ref, 36)

    by_chord(lambda ref, low: fill(ref, *low), pair_ref, other_ref, (0, 0), (3, 1))


def arrange_kernel(got_ref, q_ref):
    for deep, lanes_of in depth_parts(got_ref):
        for group in range(4):
            lanes = lanes_of(group)
            for at in range(12):
                q_ref[at, 4 * group : 4 * group + 4, deep] = lanes[4 * at : 4 * at + 4, :]


def blank(ref, used):
    if ref.shape[0] > used:
        ref[used:, :] = jnp.zeros((ref.shape[0] - used, 512), jnp.float32)


def by_chord(fill, pair_ref, other_ref, low, high):
    even = lax.axis_index("chord") % 2 == 0

    @pl.when(even)
    def _():
        fill(pair_ref, high)
        fill(other_ref, low)

    @pl.when(jnp.logical_not(even))
    def _():
        fill(pair_ref, low)
        fill(other_ref, high)


def halo_by_chord(take, pair_ref, other_ref):
    even = lax.axis_index("chord") % 2 == 0

    @pl.when(even)
    def _():
        take(pair_ref, other_ref)

    @pl.when(jnp.logical_not(even))
    def _():
        take(other_ref, pair_ref)


SCALE = 0.25 * time_step


def lane_is(at):
    return lax.broadcasted_iota(jnp.int32, (ROWS, 128), 1) == at


def next_row(x):
    return pltpu.roll(x, ROWS - 1, 0)


def row_before(x):
    return pltpu.roll(x, 1, 0)


def strain_parts(load):
    first = lane_is(0)
    held = [0.0] * 3
    for lanes in LANES:
        sums, rows, deeps = [], [], []
        for at in range(3):
            value = load(at, lanes)
            rolled = pltpu.roll(value, 1, 1)
            earlier = jnp.where(first, held[at], rolled)
            held[at] = rolled
            total, change = value + earlier, value - earlier
            behind = row_before(total)
            sums.append(total + behind)
            rows.append(total - behind)
            deeps.append(change + row_before(change))
        yield lanes, (
            sums[0],
            rows[1],
            deeps[2],
            rows[2] + deeps[1],
            deeps[0] + sums[2],
            deeps[0] - sums[2],
            rows[0] + sums[1],
            rows[0] - sums[1],
        )


def strains(now, old):
    return (
        now[0] - old[0],
        now[1] + old[1],
        now[2] + old[2],
        now[3] + old[3],
        now[4] + old[5],
        now[6] + old[7],
    )


def force_parts(load, need=(True, True)):
    last = lane_is(127)
    held = [0.0] * 6
    for lanes in reversed(LANES):
        total, change = [], []
        for at in range(6):
            value = load(at, lanes)
            rolled = pltpu.roll(value, 127, 1)
            later = jnp.where(last, held[at], rolled)
            held[at] = rolled
            total.append(value + later)
            change.append(later - value)
        plus, minus = [], []
        for lead, side, deep in ((0, 5, 4), (5, 1, 3), (4, 3, 2)):
            ahead = total[lead] + next_row(total[lead])
            rest = next_row(total[side] + change[deep]) + (change[deep] - total[side])
            plus.append(rest + ahead if need[0] else None)
            minus.append(rest - ahead if need[1] else None)
        yield lanes, plus, minus


def stress_rates(e, first_bond, second_bond):
    trace = e[0] + e[1] + e[2]
    along = []
    for bond in (first_bond, second_bond):
        part = bond[0] * e[0]
        for at in range(1, 6):
            part = part + bond[at] * e[at]
        along.append(part)
    third = trace - along[0] - along[1]
    first_weight = (SCALE * anisotropy) * (along[0] - third)
    second_weight = (SCALE * anisotropy) * (along[1] - third)
    level = (SCALE * cross_modulus) * trace + (SCALE * anisotropy) * third
    rates = []
    for at in range(6):
        rate = first_bond[at] * first_weight + second_bond[at] * second_weight
        if at < 3:
            rate = rate + ((2.0 * SCALE * shear_modulus) * e[at] + level)
        else:
            rate = rate + (SCALE * shear_modulus) * e[at]
        rates.append(rate)
    return rates


def bonds_of(a, b, c):
    w = jnp.sqrt(jnp.maximum(1.0 - a * a - b * b - c * c, 0.0))
    ab, ac, bc = a * b, a * c, b * c
    wa, wb, wc = w * a, w * b, w * c
    aa, bb, cc = a * a, b * b, c * c
    bonds = []
    for p, q, r in (
        (1.0 - 2.0 * (bb + cc), 2.0 * (ab + wc), 2.0 * (ac - wb)),
        (2.0 * (ab - wc), 1.0 - 2.0 * (aa + cc), 2.0 * (bc + wa)),
    ):
        bonds += [p * p, q * q, r * r, q * r, r * p, p * q]
    return bonds


def outer_scale(outside_low, outside_high):
    row = lax.broadcasted_iota(jnp.int32, (8, 128), 0)
    outside = ((row < DEEP) & outside_high) | ((row >= DEEP) & outside_low)
    return jnp.where(outside, 0.0, 1.0)


def put(ref, lead, lanes, value, outer):
    ref[(*lead, slice(0, 16), lanes)] = value[0:16]
    ref[(*lead, slice(16, ROWS), lanes)] = value[16:ROWS] * outer


NOW = (0, 1, 2, 3, 4, 6)
OLD = (0, 1, 2, 3, 5, 7)


def push_three(loads, old, new, outer):
    for layers in zip(*[force_parts(load, (x > 0, x < 3)) for x, load in enumerate(loads)]):
        lanes = layers[0][0]
        for x in range(3):
            for at in range(3):
                force = layers[x + 1][1][at] + layers[x][2][at]
                put(new, (at, x), lanes, old(at, x, lanes) + SCALE * force, outer)


def whole_rows(ref, at, lanes, value):
    ref[at, :, lanes] = value


def some_rows(runs):
    count = sum(stop - start for start, stop in runs)

    def store(ref, at, lanes, value):
        ref[16 * at : 16 * at + 16, lanes] = value[0:16]
        row = 48 + count * at
        for start, stop in runs:
            ref[row : row + stop - start, lanes] = value[start:stop]
            row += stop - start

    return store


MOST = ((16, 18), (21, 24))
LAST = ((23, 24),)


def send_parts(first, last, high, added, chip_ref, far_ref, store=whole_rows):
    odd = span_odd()
    for (lanes, plus, _), (_, _, minus) in zip(
        force_parts(first, (True, False)), force_parts(last, (False, True))
    ):
        for at in range(3):
            low = SCALE * plus[at]
            value = high(at, lanes) + SCALE * minus[at]
            if added is not None and at == 2:
                value = value + added(lanes)
            store(chip_ref, at, lanes, jnp.where(odd, low, value))
            store(far_ref, at, lanes, jnp.where(odd, value, low))


def take_rows(chip_ref, far_ref, got_chip_ref, got_far_ref, side_ref, runs):
    odd = span_odd()
    inside = jnp.where(lax.axis_index("span") == 0, 0.0, 1.0)
    low_row = jnp.where(lax.axis_index("chord") == 0, 0.0, 1.0)
    count = sum(stop - start for start, stop in runs)
    for at in range(3):
        side_ref[at, :, 16:ROWS] = jnp.zeros((2, 8, 512), jnp.float32)
        row, places = 48 + count * at, [(16 * at, 0, 16)]
        for start, stop in runs:
            places.append((row, start, stop))
            row += stop - start
        for row, start, stop in places:
            rows, factor = slice(row, row + stop - start), low_row if start > 20 else 1.0
            chip = chip_ref[rows, :] + got_chip_ref[rows, :]
            far = far_ref[rows, :] + got_far_ref[rows, :]
            side_ref[at, 0, start:stop] = jnp.where(odd, chip, far) * (inside * factor)
            side_ref[at, 1, start:stop] = jnp.where(odd, far, chip) * factor


def take_parts(chip_ref, far_ref, got_chip_ref, got_far_ref, side_ref, added_ref=None):
    odd = span_odd()
    outer = rows_scale()[1]
    inside = jnp.where(lax.axis_index("span") == 0, 0.0, 1.0)
    for lanes in LANES:
        for at in range(3):
            chip = chip_ref[at, :, lanes] + got_chip_ref[at, :, lanes]
            far = far_ref[at, :, lanes] + got_far_ref[at, :, lanes]
            low, high = jnp.where(odd, chip, far), jnp.where(odd, far, chip)
            if added_ref is not None and at == 2:
                low, high = low + added_ref[0, :, lanes], high + added_ref[1, :, lanes]
            put(side_ref, (at, 0), lanes, low * inside, outer)
            put(side_ref, (at, 1), lanes, high, outer)


def strain(e, bonds, old, new, lead, lanes, outer, factor=None):
    for at, rate in enumerate(stress_rates(e, bonds[:6], bonds[6:])):
        if factor is not None:
            rate = rate * factor
        put(new, (at, lead), lanes, old(at) + rate, outer)


def layer_of(ref, x):
    return lambda at, lanes: ref[at, x, :, lanes]


def plane_of(ref, first=0):
    return lambda at, lanes: ref[first + at, :, lanes]


def span_odd():
    return lax.axis_index("span") % 2 == 1


def rows_scale():
    chord = lax.axis_index("chord")
    return outer_scale(False, chord == 7), outer_scale(chord == 0, False)


def edge_kernel(field_ref, v_out, s_out, pair_ref, other_ref):
    for at in range(9):
        if at < 6:
            s_out[at, :, 0:16] = field_ref[at]
        else:
            v_out[at - 6, :, 0:16] = field_ref[at]

    def fill(ref, first):
        rows = slice(first, first + DEEP)
        for at in range(9):
            for x in range(4):
                row = 16 * at + 4 * x
                ref[row : row + 4, :] = field_ref[at, x, rows]
        blank(ref, 144)

    by_chord(fill, pair_ref, other_ref, 0, 16 - DEEP)


def spot(sources_ref, at):
    layer = sources_ref[at, 0].astype(jnp.int32) - 4 * lax.axis_index("span")
    chord = sources_ref[at, 1].astype(jnp.int32) - 16 * lax.axis_index("chord")
    return layer, chord, sources_ref[at, 2].astype(jnp.int32)


def add_at(ref, lead, chord, deep, amount):
    row = jnp.where(chord < 0, chord + ROWS, chord)
    rows = pl.ds(pl.multiple_of((row // 8) * 8, 8), 8)
    lanes = pl.ds(pl.multiple_of((deep // 128) * 128, 128), 128)
    hit = (lax.broadcasted_iota(jnp.int32, (8, 128), 0) == row % 8) & (
        lax.broadcasted_iota(jnp.int32, (8, 128), 1) == deep % 128
    )
    ref[(*lead, rows, lanes)] = ref[(*lead, rows, lanes)] + jnp.where(hit, amount, 0.0)


def before_span_kernel(v_ref, s_ref, pair_ref, other_ref, v_out, s_out, chip_ref, far_ref):
    def take(next_ref, prior_ref):
        for at in range(9):
            out, slot = (s_out, at) if at < 6 else (v_out, at - 6)
            for x in range(4):
                row = 16 * at + 4 * x
                out[slot, x, 16 : 16 + DEEP] = next_ref[row : row + 4, :]
                out[slot, x, 16 + DEEP : ROWS] = prior_ref[row : row + 4, :]

    halo_by_chord(take, pair_ref, other_ref)
    send_parts(layer_of(s_out, 0), layer_of(s_out, 3), layer_of(v_out, 3), None, chip_ref, far_ref)


def between_kernel(sources_ref, v_ref, s_ref, v_out, e_out, added_ref):
    for at in range(14):
        added_ref[at] = jnp.zeros((ROWS, 512), jnp.float32)
    outer = rows_scale()[1]
    loads = [layer_of(s_ref, x) for x in range(4)]
    push_three(loads, lambda at, x, lanes: v_ref[at, x, :, lanes], v_out, outer)
    for at in range(16):
        layer, chord, deep = spot(sources_ref, at)
        inside = (chord >= -DEEP) & (chord < 16 + DEEP)

        @pl.when(inside & ((layer == -1) | (layer == 3)))
        def _():
            slot = jnp.where(layer == -1, 0, 1)
            add_at(added_ref, (slot,), chord, deep, sources_ref[at, 3])

        @pl.when(inside & (layer >= 0) & (layer < 3))
        def _():
            add_at(v_out, (2, layer), chord, deep, sources_ref[at, 3])

        @pl.when(inside & (layer >= 0) & (layer < 4))
        def _():
            for step_at in range(1, 4):
                add_at(
                    added_ref, (slot_of(step_at, layer),), chord, deep, sources_ref[at, 3 + step_at]
                )

    for layers in zip(*[strain_parts(layer_of(v_out, x)) for x in range(3)]):
        lanes = layers[0][0]
        for x in range(2):
            for at, value in enumerate(strains(layers[x + 1][1], layers[x][1])):
                e_out[at, x, :, lanes] = value


def after_span_kernel(
    v_ref, added_ref, chip_ref, far_ref, got_chip_ref, got_far_ref, v_out, e_out, side_ref
):
    take_parts(chip_ref, far_ref, got_chip_ref, got_far_ref, side_ref, added_ref)
    for at in range(3):
        v_out[at] = side_ref[at, 1]
    loads = (layer_of(side_ref, 0), layer_of(v_ref, 0), layer_of(v_ref, 2), layer_of(side_ref, 1))
    for layers in zip(*[strain_parts(load) for load in loads]):
        lanes = layers[0][0]
        for slot in range(2):
            for at, value in enumerate(strains(layers[2 * slot + 1][1], layers[2 * slot][1])):
                e_out[at, slot, :, lanes] = value


def slot_of(step_at, layer):
    return 4 * step_at - 2 + layer


def first_stress(x, slot, rows, lanes, q, e_ref, index, s_ref, b_out):
    bonds = bonds_of(*q)
    for at, value in enumerate(bonds):
        b_out[at, slot, rows, lanes] = value
    e = [e_ref[at, index, rows, lanes] for at in range(6)]
    rates = stress_rates(e, bonds[:6], bonds[6:])
    return [s_ref[at, x, rows, lanes] + rates[at] for at in range(6)]


ENDS = (0, 3)


def first_own_kernel(e_ref, s_ref, q_ref, s_out, b_out):
    for lanes in LANES:
        for slot, x in enumerate(ENDS):
            for rows in (slice(0, 8), slice(8, 16)):
                q = [q_ref[4 * at + x, rows, lanes] for at in range(3)]
                new = first_stress(x, slot, rows, lanes, q, e_ref, slot, s_ref, b_out)
                for at in range(6):
                    s_out[at, slot, rows, lanes] = new[at]


def first_end_kernel(
    s_held, b_held, v_last_ref, e_ref, s_ref, pair_ref, other_ref, added_ref,
    s_out, b_out, q_out, chip_ref, far_ref, halo_ref,
):
    halo_ref[...] = jnp.zeros(halo_ref.shape, jnp.float32)

    def take(next_ref, prior_ref):
        for at in range(12):
            halo_ref[at, 0:3] = next_ref[3 * at : 3 * at + 3]
            halo_ref[at, 5:8] = prior_ref[3 * at : 3 * at + 3]

    halo_by_chord(take, pair_ref, other_ref)
    outer_s = rows_scale()[0]
    rows = slice(16, ROWS)
    for at in range(3):
        q_out[2 * at] = halo_ref[4 * at + 1]
        q_out[2 * at + 1] = halo_ref[4 * at + 2]
    for lanes in LANES:
        for slot, x in enumerate(ENDS):
            q = [halo_ref[4 * at + x, :, lanes] for at in range(3)]
            new = first_stress(x, slot, rows, lanes, q, e_ref, slot, s_ref, b_out)
            for at in range(6):
                s_out[at, slot, rows, lanes] = new[at] * outer_s
    added = lambda lanes: added_ref[slot_of(1, 3), :, lanes]
    store = some_rows(MOST)
    blank(far_ref, 63)
    send_parts(
        layer_of(s_out, 0), layer_of(s_out, 1), plane_of(v_last_ref), added, chip_ref, far_ref, store
    )


def middle(v_ref, ends, s_mid, added_ref, step_at, bond_of, v_out, s_out, parts_out, rows=ROWS):
    outer_s, outer_v = rows_scale()
    loads = [ends[0], s_mid(0), s_mid(1), ends[1]]

    def old(at, x, lanes):
        value = v_ref[at, x, :, lanes]
        return value + added_ref[slot_of(step_at, x), :, lanes] if at == 2 else value

    push_three(loads, old, v_out, outer_v)
    for layers in zip(*[strain_parts(layer_of(v_out, x)) for x in range(3)]):
        lanes = layers[0][0]
        for at in range(6):
            parts_out[at, 0, :, lanes] = layers[0][1][NOW[at]][0:rows]
            parts_out[at, 1, :, lanes] = layers[2][1][OLD[at]][0:rows]
        for x in range(2):
            e = strains(layers[x + 1][1], layers[x][1])
            before = lambda at: s_mid(x)(at, lanes)
            if rows == ROWS:
                strain(e, bond_of(x, lanes), before, s_out, x, lanes, outer_s)
            else:
                bonds = [bond[0:rows] for bond in bond_of(x, lanes)]
                e = [value[0:rows] for value in e]
                for at, rate in enumerate(stress_rates(e, bonds[:6], bonds[6:])):
                    s_out[at, 1 + x, :, lanes] = before(at)[0:rows] + rate


def first_middle_kernel(
    v_ref, e_ref, s_ref, s_ends_ref, q_ref, halo_ref, added_ref,
    v_out, s_out, b_out, parts_out, stress_ref,
):
    outer_s, _ = rows_scale()
    for lanes in LANES:
        for x in range(2):
            for rows in (slice(0, 8), slice(8, 16), slice(16, ROWS)):
                own = rows.start < 16
                q = [
                    q_ref[4 * at + 1 + x, rows, lanes] if own else halo_ref[2 * at + x, :, lanes]
                    for at in range(3)
                ]
                new = first_stress(1 + x, x, rows, lanes, q, e_ref, x, s_ref, b_out)
                for at in range(6):
                    stress_ref[at, x, rows, lanes] = new[at] if own else new[at] * outer_s
    bond_of = lambda x, lanes: [b_out[at, x, :, lanes] for at in range(12)]
    s_mid = lambda x: layer_of(stress_ref, x)
    ends = layer_of(s_ends_ref, 0), layer_of(s_ends_ref, 1)
    middle(v_ref, ends, s_mid, added_ref, 1, bond_of, v_out, s_out, parts_out)


def middle_kernel(v_ref, s_chip_ref, s_far_ref, s_ref, b_ref, added_ref, v_out, s_out, parts_out):
    bond_of = lambda x, lanes: [b_ref[at, x, :, lanes] for at in range(12)]
    s_mid = lambda x: layer_of(s_ref, x)
    ends = end_layers(s_chip_ref, s_far_ref)
    middle(v_ref, ends, s_mid, added_ref, 2, bond_of, v_out, s_out, parts_out)


def last_middle_kernel(
    v_ref, s_chip_ref, s_far_ref, s_ref, b_ref, added_ref, v_out, s_out, parts_out, moved_ref
):
    bond_of = lambda x, lanes: [b_ref[at, x, :, lanes] for at in range(12)]
    s_mid = lambda x: layer_of(s_ref, x)
    ends = end_layers(s_chip_ref, s_far_ref)
    middle(v_ref, ends, s_mid, added_ref, 3, bond_of, moved_ref, s_out, parts_out, 16)
    for at in range(3):
        v_out[at, 0:3] = moved_ref[at, :, 0:16]


def end_strains(parts, slot, lanes, other):
    if slot == 0:
        return [parts[0] - other[0]] + [parts[at] + other[OLD[at]] for at in range(1, 6)]
    return [other[0] - parts[0]] + [other[NOW[at]] + parts[at] for at in range(1, 6)]


def end_layers(chip_ref, far_ref):
    odd = span_odd()
    low = lambda at, lanes: jnp.where(odd, chip_ref[at, :, lanes], far_ref[at, :, lanes])
    high = lambda at, lanes: jnp.where(odd, far_ref[at, :, lanes], chip_ref[at, :, lanes])
    return low, high


def end_kernel(
    chip_side, first, last, s_ref, parts_ref, b_ref, sent_ref, got_ref, added_ref,
    s_out, next_ref, side_ref,
):
    outer_s = rows_scale()[0]
    low_row = jnp.where(lax.axis_index("chord") == 0, 0.0, 1.0)
    inside = jnp.where(lax.axis_index("span") == 0, 0.0, 1.0)
    store = some_rows(LAST if last else MOST)
    blank(next_ref, 51 if last else 63)

    def work(slot):
        for at in range(3):
            side_ref[at, 16:ROWS] = jnp.zeros((8, 512), jnp.float32)
            row, places = 48 + 5 * at, [(16 * at, 0, 16)]
            for start, stop in MOST:
                places.append((row, start, stop))
                row += stop - start
            for row, start, stop in places:
                rows, factor = slice(row, row + stop - start), low_row if start > 20 else 1.0
                factor = factor * inside if slot == 0 else factor
                side_ref[at, start:stop] = (sent_ref[rows, :] + got_ref[rows, :]) * factor
        for lanes, other in strain_parts(plane_of(side_ref)):
            e = end_strains([parts_ref[at, slot, :, lanes] for at in range(6)], slot, lanes, other)
            bonds = [b_ref[at, slot, :, lanes] for at in range(12)]
            for at, rate in enumerate(stress_rates(e, bonds[:6], bonds[6:])):
                value = (s_ref[at, slot, :, lanes] if first else s_ref[at, :, lanes]) + rate
                put(s_out, (at,), lanes, value, outer_s)
        for lanes, plus, minus in force_parts(plane_of(s_out), (slot == 0, slot == 1)):
            for at in range(3):
                if slot == 0:
                    value = SCALE * plus[at]
                else:
                    value = side_ref[at, :, lanes] + SCALE * minus[at]
                    if at == 2:
                        value = value + added_ref[slot_of(3 if last else 2, 3), :, lanes]
                store(next_ref, at, lanes, value)

    low = span_odd() if chip_side else jnp.logical_not(span_odd())

    @pl.when(low)
    def _():
        work(0)

    @pl.when(jnp.logical_not(low))
    def _():
        work(1)


def last_end_kernel(
    chip_side, v_held, s_held, s_ref, b_ref, parts_ref, sent_ref, got_ref,
    v_out, s_out, side_ref, end_ref, sems,
):
    inside = jnp.where(lax.axis_index("span") == 0, 0.0, 1.0)
    low_row = jnp.where(lax.axis_index("chord") == 0, 0.0, 1.0)

    def work(slot):
        side = inside if slot == 0 else 1.0
        for at in range(3):
            own, halo = slice(16 * at, 16 * at + 16), slice(48 + at, 49 + at)
            side_ref[at, 16:ROWS] = jnp.zeros((8, 512), jnp.float32)
            side_ref[at, 0:16] = (sent_ref[own, :] + got_ref[own, :]) * side
            side_ref[at, ROWS - 1 : ROWS] = (sent_ref[halo, :] + got_ref[halo, :]) * (side * low_row)
        copies = []
        if slot == 1:
            copies.append(pltpu.make_async_copy(side_ref.at[:, 0:16], v_out.at[:, 3], sems.at[0]))
            copies[0].start()
        for lanes, other in strain_parts(plane_of(side_ref)):
            parts = [parts_ref[at, slot, :, lanes] for at in range(6)]
            e = end_strains(parts, slot, lanes, [value[0:16] for value in other])
            bonds = [b_ref[at, slot, 0:16, lanes] for at in range(12)]
            for at, rate in enumerate(stress_rates(e, bonds[:6], bonds[6:])):
                end_ref[at, :, lanes] = s_ref[at, 0:16, lanes] + rate
        copies.append(pltpu.make_async_copy(end_ref, s_out.at[:, ENDS[slot]], sems.at[1]))
        copies[-1].start()
        for copy in copies:
            copy.wait()

    low = span_odd() if chip_side else jnp.logical_not(span_odd())

    @pl.when(low)
    def _():
        work(0)

    @pl.when(jnp.logical_not(low))
    def _():
        work(1)


def swap(x, axis, first):
    peers = lax.axis_size(axis)
    pairs = []
    for i in range(first, peers - 1, 2):
        pairs += [(i, i + 1), (i + 1, i)]
    return lax.ppermute(x, axis, pairs)


def swaps(pair, other, axis):
    second = swap(other, axis, 1)
    return swap(pair, axis, 0), second


def shards(
    velocity, stress, grain_ids, lattice_tilt, grain_orient, orientations, source_cells, source_signal
):
    plane = (ROWS, 512)
    edge, ends, pair_of = (3, *plane), (3, 2, *plane), (6, 2, *plane)
    sources = jnp.concatenate((source_cells.astype(jnp.float32), source_signal), axis=1)
    (sent,) = call(
        rotation_kernel,
        [(16, 48, 128)],
        (
            jnp.transpose(grain_ids, (1, 2, 0)),
            jnp.transpose(lattice_tilt, (0, 2, 3, 1)),
            grain_orient.reshape(32, 128),
            orientations,
        ),
        scratch=[(3, 256, 128)],
        flops=32768 * 200,
    )

    got = lax.all_to_all(sent, "span", 0, 0, tiled=True)

    half, s, pair, other = call(
        edge_kernel,
        [(3, 4, *plane), (6, 4, *plane), (144, 512), (152, 512)],
        (jnp.concatenate((stress, velocity)),),
    )
    pair, other = swaps(pair, other, "chord")
    v, s, chip, far = call(
        before_span_kernel,
        [(3, 4, *plane), (6, 4, *plane), edge, edge],
        (half, s, pair, other),
        aliases={0: 0, 1: 1},
        flops=32768 * 40000,
    )
    got_chip, got_far = swaps(chip, far, "span")
    v, e_mid, added = call(
        between_kernel,
        [(3, 3, *plane), pair_of, (14, *plane)],
        (sources, v, s),
        spaces={0: pltpu.SMEM},
    )

    pair, other = call(arrange_edge_kernel, [(36, 512), (56, 512)], (got,))
    pair, other = swaps(pair, other, "chord")
    (q,) = call(arrange_kernel, [(12, 16, 512)], (got,))

    v_last, e = call(
        after_span_kernel,
        [edge, pair_of],
        (v, added, chip, far, got_chip, got_far),
        scratch=[ends],
    )
    s_ends, bonds = call(
        first_own_kernel, [pair_of, (12, 2, *plane)], (e, s, q), flops=32768 * 100
    )
    s_ends, bonds, halo, chip, far = call(
        first_end_kernel,
        [pair_of, (12, 2, *plane), (6, 8, 512), (63, 512), (64, 512)],
        (s_ends, bonds, v_last, e, s, pair, other, added),
        scratch=[(12, 8, 512)],
        aliases={0: 0, 1: 1},
    )
    got_chip, got_far = swaps(chip, far, "span")
    v, s, mid_bonds, part = call(
        first_middle_kernel,
        [(3, 3, *plane), pair_of, (12, 2, *plane), pair_of],
        (v, e_mid, s, s_ends, q, halo, added),
        scratch=[pair_of],
        flops=32768 * 100,
    )
    s_chip, chip = call(
        lambda *refs: end_kernel(True, True, False, *refs),
        [(6, *plane), (63, 512)],
        (s_ends, part, bonds, chip, got_chip, added),
        scratch=[edge],
    )
    s_far, far = call(
        lambda *refs: end_kernel(False, True, False, *refs),
        [(6, *plane), (64, 512)],
        (s_ends, part, bonds, far, got_far, added),
        scratch=[edge],
    )
    got_chip, got_far = swaps(chip, far, "span")
    v, s, part = call(
        middle_kernel,
        [(3, 3, *plane), pair_of, pair_of],
        (v, s_chip, s_far, s, mid_bonds, added),
        flops=32768 * 100,
    )
    s_chip, chip = call(
        lambda *refs: end_kernel(True, False, True, *refs),
        [(6, *plane), (51, 512)],
        (s_chip, part, bonds, chip, got_chip, added),
        scratch=[edge],
    )
    s_far, far = call(
        lambda *refs: end_kernel(False, False, True, *refs),
        [(6, *plane), (56, 512)],
        (s_far, part, bonds, far, got_far, added),
        scratch=[edge],
    )
    got_chip, got_far = swaps(chip, far, "span")
    v, s, part = call(
        last_middle_kernel,
        [velocity.shape, stress.shape, (6, 2, 16, 512)],
        (v, s_chip, s_far, s, mid_bonds, added),
        scratch=[(3, 3, *plane)],
        flops=32768 * 100,
    )
    for chip_side, s_side, sent, got in ((True, s_chip, chip, got_chip), (False, s_far, far, got_far)):
        v, s = pl.pallas_call(
            lambda *refs, chip_side=chip_side: last_end_kernel(chip_side, *refs),
            out_shape=[
                jax.ShapeDtypeStruct(velocity.shape, jnp.float32),
                jax.ShapeDtypeStruct(stress.shape, jnp.float32),
            ],
            in_specs=[pl.BlockSpec(memory_space=pl.ANY)] * 2 + [WHOLE] * 5,
            out_specs=[pl.BlockSpec(memory_space=pl.ANY)] * 2,
            scratch_shapes=[
                pltpu.VMEM(edge, jnp.float32),
                pltpu.VMEM((6, 16, 512), jnp.float32),
                pltpu.SemaphoreType.DMA((2,)),
            ],
            input_output_aliases={0: 0, 1: 1},
            compiler_params=VMEM,
        )(v, s, s_side, bonds, part, sent, got)
    return v, s


def solution(mesh):
    return jax.shard_map(
        shards,
        mesh=mesh,
        in_specs=(
            P(None, "span", "chord", None),
            P(None, "span", "chord", None),
            P(None, "chord", "span"),
            P(None, None, "chord", "span"),
            P(),
            P(),
            P(),
            P(),
        ),
        out_specs=(P(None, "span", "chord", None), P(None, "span", "chord", None)),
        check_vma=False,
    )
```
